32 devices in a mesh: row: 4 (over y, core), seq: 8 (over z, x).
Axes of the slice: x: 2, y: 2, z: 4, core: 2. Of those that a mesh axis runs over, the one named last changes fastest.
Arguments:
- activations: bfloat16 [3, 4, 1024, 1024], P(None, 'row', 'seq'), may hold values from -6 to 6
- cotangent: bfloat16 [3, 4, 1024, 1024], P(None, 'row', 'seq'), may hold values from -6 to 6
- segment_ids: int32 [3, 4, 1024], P(None, 'row', 'seq'), may hold values from 0 to 3, never falling along the last dimension, each value on 1 to 512 neighbouring positions
- prefix_embed: float32 [10, 1024], replicated, may hold values from -6 to 6
- adapt_in: float32 [1024, 512], replicated, may hold values from -0.1875 to 0.1875
- adapt_in_bias: float32 [512], replicated, may hold values from -1.8 to 1.8
- adapt_out: float32 [512, 2048], replicated, may hold values from -0.375 to 0.375
- adapt_out_bias: float32 [2048], replicated, may hold values from -1.8 to 1.8
- ln1_gain: bfloat16 [1024], replicated, may hold values from 0.5 to 1.5
- ln1_bias: bfloat16 [1024], replicated, may hold values from -1.796875 to 1.796875
- qkv_weight: bfloat16 [1024, 3072], P('row', 'seq'), may hold values from -0.1875 to 0.1875
- qkv_bias: bfloat16 [3072], replicated, may hold values from -1.796875 to 1.796875
- out_weight: bfloat16 [1024, 1024], P('row', 'seq'), may hold values from -0.75 to 0.75
- out_bias: bfloat16 [1024], replicated, may hold values from -1.796875 to 1.796875
- ln2_gain: bfloat16 [1024], replicated, may hold values from 0.5 to 1.5
- ln2_bias: bfloat16 [1024], replicated, may hold values from -1.796875 to 1.796875
- fc_weight: bfloat16 [1024, 4096], P('row', 'seq'), may hold values from -0.1875 to 0.1875
- fc_bias: bfloat16 [4096], replicated, may hold values from -1.796875 to 1.796875
- proj_weight: bfloat16 [4096, 1024], P('row', 'seq'), may hold values from -0.09375 to 0.09375
- proj_bias: bfloat16 [1024], replicated, may hold values from -1.796875 to 1.796875
Outputs:
- output: bfloat16 [3, 4, 1024, 1024], P(None, 'row', 'seq')
- in_grad: bfloat16 [3, 4, 1024, 1024], P(None, 'row', 'seq')
- prefix_grad: float32 [10, 1024], replicated
- adapt_in_grad: float32 [1024, 512], replicated
- adapt_in_bias_grad: float32 [512], replicated
- adapt_out_grad: float32 [512, 2048], replicated
- adapt_out_bias_grad: float32 [2048], replicated
The draws below stay inside these ranges and needn't reach their ends.
Inputs may be any that keep to these rules, and one draw needn't show every extreme that they name: `segment_ids`: along every packed row the ids never fall; each document has 1 to 512 tokens and some document has exactly 512.
All inputs are finite; a program needn't handle non-finite values.
Results may differ from the reference program's by a relative error of at most 0.014.
Values may be sent and summed in bfloat16 or wider, within the bound.
No kernel may reach another device: no remote copies, remote signals or barrier semaphores. Data moves between devices by JAX's collectives and lax.ppermute only.
A program may use at most 192 MiB of HBM per device.

```python
import math
import jax
import jax.numpy as jnp
import numpy as np
from jax import lax

D = 1024
HEADS = 16
HEAD_DIM = 64
FF = 4096
PREFIX = 10
ADAPT = 512
MB = 3
SEG_MOST = 512
LEN = 1024
SEGS = 4
ROWS = 4


def levels(key, shape, shards, low, largest):
    def one(dim, blocks):
        heights = jax.random.uniform(jax.random.fold_in(jax.random.fold_in(key, 6), dim), (blocks,), jnp.float32, low / len(shards), largest / len(shards))
        return jnp.repeat(jnp.exp(heights), shape[dim] // blocks).reshape((-1,) + (1,) * (len(shape) - dim - 1))

    factor_of = one(*shards[0])
    for cut in shards[1:]:
        factor_of = factor_of * one(*cut)
    return factor_of


def split_up(amount, total, bound, lean):
    weights = [(1 << 20) // math.isqrt(rank ** lean) + 1 for rank in range(2, amount + 1)]
    spare, given = total - bound - (amount - 1), [1] * (amount - 1)
    while spare > 0:
        free = [i for i in range(amount - 1) if given[i] < bound]
        whole, left = sum([weights[i] for i in free]), spare
        for i in free:
            extra = min(bound - given[i], max(1, left * weights[i] // whole), spare)
            given[i] = given[i] + extra
            spare = spare - extra
    return np.array([bound] + given)


def uneven(own_key, count, total, bound, skew):
    if count == 2:
        one = jax.random.randint(own_key, (), max(1, total - bound), min(bound, total - 1) + 1)
        return jnp.stack([one, total - one])
    tallies = jnp.asarray(split_up(count, total, bound, skew), jnp.int32)
    couples = (count - 1) // 2
    source_of, taker = tallies[1:1 + 2 * couples:2], tallies[2:2 + 2 * couples:2]
    margin = jnp.minimum(source_of - 1, bound - taker)
    passed = jax.random.randint(jax.random.fold_in(own_key, 1), (couples,), 0, 1 << 20) % (margin + 1)
    tallies = tallies.at[1:1 + 2 * couples:2].set(source_of - passed).at[2:2 + 2 * couples:2].set(taker + passed)
    return tallies[jax.random.permutation(jax.random.fold_in(own_key, 2), count)]


def scatter_about(stream_key, shape, scale, reach, cuts=(), held_as=jnp.bfloat16):
    values = jax.random.normal(stream_key, shape, jnp.float32) * scale
    if len(cuts) > 0:
        values = levels(stream_key, shape, cuts, -0.22, 0.18) * values
    return jnp.clip(values, min=-reach, max=reach).astype(held_as)


def setup_inputs(seed: int = 0) -> dict:
    key_list = jax.random.split(jax.random.key(seed), 21)
    activations = scatter_about(key_list[0], (MB, ROWS, LEN, D), 1.0, 6.0, ((1, 4), (2, 8)))
    cotangent = scatter_about(key_list[1], (MB, ROWS, LEN, D), 1.0, 6.0, ((1, 4), (2, 8)))
    segment_ids = jax.vmap(lambda own: jnp.searchsorted(jnp.cumsum(uneven(own, SEGS, LEN, SEG_MOST, 2)), jnp.arange(LEN), side="right"))(jax.random.split(key_list[2], MB * ROWS)).reshape((MB, ROWS, LEN)).astype(jnp.int32)
    prefix_embed = scatter_about(key_list[3], (PREFIX, D), 1.0, 6.0, (), jnp.float32)
    adapt_in = scatter_about(key_list[4], (D, ADAPT), D ** -0.5, 0.1875, (), jnp.float32)
    adapt_in_bias = scatter_about(key_list[5], (ADAPT,), 0.3, 1.8, (), jnp.float32)
    adapt_out = scatter_about(key_list[6], (ADAPT, 2 * D), (ADAPT // 2) ** -0.5, 0.375, (), jnp.float32)
    adapt_out_bias = scatter_about(key_list[7], (2 * D,), 0.3, 1.8, (), jnp.float32)
    ln1_gain = jnp.clip(1.0 + 0.1 * jax.random.normal(key_list[8], (D,), jnp.float32), 0.5, 1.5).astype(jnp.bfloat16)
    ln1_bias = scatter_about(key_list[9], (D,), 0.3, 1.796875)
    qkv_weight = scatter_about(key_list[10], (D, 3 * D), D ** -0.5, 0.1875, ((0, 4), (1, 8)))
    qkv_bias = scatter_about(key_list[11], (3 * D,), 0.3, 1.796875)
    out_weight = scatter_about(key_list[12], (D, D), HEAD_DIM ** -0.5, 0.75, ((0, 4), (1, 8)))
    out_bias = scatter_about(key_list[13], (D,), 0.3, 1.796875)
    ln2_gain = jnp.clip(1.0 + 0.1 * jax.random.normal(key_list[14], (D,), jnp.float32), 0.5, 1.5).astype(jnp.bfloat16)
    ln2_bias = scatter_about(key_list[15], (D,), 0.3, 1.796875)
    fc_weight = scatter_about(key_list[16], (D, FF), D ** -0.5, 0.1875, ((0, 4), (1, 8)))
    fc_bias = scatter_about(key_list[17], (FF,), 0.3, 1.796875)
    proj_weight = scatter_about(key_list[18], (FF, D), FF ** -0.5, 0.09375, ((0, 4), (1, 8)))
    proj_bias = scatter_about(key_list[19], (D,), 0.3, 1.796875)
    return dict(activations=activations, cotangent=cotangent, segment_ids=segment_ids, prefix_embed=prefix_embed, adapt_in=adapt_in, adapt_in_bias=adapt_in_bias, adapt_out=adapt_out, adapt_out_bias=adapt_out_bias, ln1_gain=ln1_gain, ln1_bias=ln1_bias, qkv_weight=qkv_weight, qkv_bias=qkv_bias, out_weight=out_weight, out_bias=out_bias, ln2_gain=ln2_gain, ln2_bias=ln2_bias, fc_weight=fc_weight, fc_bias=fc_bias, proj_weight=proj_weight, proj_bias=proj_bias)


@jax.custom_vjp
def low(v):
    return lax.optimization_barrier(v.astype(jnp.bfloat16)).astype(jnp.float32)

@jax.custom_vjp
def low_back(v):
    return v

def low_keep(v):
    return (low(v), None)

def low_pass(kept, grad):
    return (grad,)

def back_keep(v):
    return (v, None)

def back_low(kept, grad):
    return (low(grad),)
low.defvjp(low_keep, low_pass)
low_back.defvjp(back_keep, back_low)

def matmul_high(left_op, right_op):
    return jnp.dot(left_op, right_op, precision=lax.Precision.HIGHEST, preferred_element_type=jnp.float32)

def prefix_pairs(prefix_embed, adapt_in, adapt_in_bias, adapt_out, adapt_out_bias):
    squashed = jnp.tanh(matmul_high(prefix_embed, adapt_in) + adapt_in_bias)
    return matmul_high(squashed, adapt_out) + adapt_out_bias

def layer_norm(values, norm_gain, norm_shift):
    centre = values - lax.optimization_barrier(jnp.mean(values, axis=-1, keepdims=True))
    spread = lax.optimization_barrier(jnp.mean(centre * centre, axis=-1, keepdims=True))
    return centre * lax.rsqrt(spread + 1e-05) * norm_gain + norm_shift

def gelu_tanh(values):
    return 0.5 * values * (1.0 + jnp.tanh(0.7978845608028654 * (values + 0.044715 * values * values * values)))

def attend_block(block_start, queries, keys_pad, values_pad, seg_row, seg_pad, pre_keys, pre_values):
    block_rows = min(512, LEN)
    window = SEG_MOST + block_rows
    score_scale = 1.0 / HEAD_DIM ** 0.5
    query_blk = lax.dynamic_slice_in_dim(queries, block_start, block_rows, 0)
    key_blk = lax.dynamic_slice_in_dim(keys_pad, block_start, window, 0)
    value_blk = lax.dynamic_slice_in_dim(values_pad, block_start, window, 0)
    query_seg = lax.dynamic_slice_in_dim(seg_row, block_start, block_rows, 0)
    key_seg = lax.dynamic_slice_in_dim(seg_pad, block_start, window, 0)
    query_pos = block_start + jnp.arange(block_rows, dtype=jnp.int32)
    key_pos = block_start - SEG_MOST + jnp.arange(window, dtype=jnp.int32)
    allowed = (query_seg[:, None] == key_seg[None, :]) & (key_pos[None, :] <= query_pos[:, None])
    row_scores = jnp.einsum('qhd,khd->hqk', query_blk, key_blk, precision=lax.Precision.HIGHEST) * score_scale
    pre_scores = jnp.einsum('qhd,phd->hqp', query_blk, pre_keys, precision=lax.Precision.HIGHEST) * score_scale
    scores = low_back(jnp.concatenate([pre_scores, row_scores], axis=-1))
    keep_mask = jnp.concatenate([jnp.ones((block_rows, PREFIX), dtype=bool), allowed], axis=-1)
    scores = jnp.where(keep_mask[None, :, :], scores, -1e+30)
    row_top = lax.optimization_barrier(jnp.max(scores, axis=-1, keepdims=True))
    expo = jnp.exp(scores - row_top)
    attn_probs = low(expo / lax.optimization_barrier(jnp.sum(expo, axis=-1, keepdims=True)))
    pre_part = jnp.einsum('hqp,phd->qhd', attn_probs[:, :, :PREFIX], pre_values, precision=lax.Precision.HIGHEST)
    row_part = jnp.einsum('hqk,khd->qhd', attn_probs[:, :, PREFIX:], value_blk, precision=lax.Precision.HIGHEST)
    return pre_part + row_part
checked_block = jax.checkpoint(attend_block)

def row_attention(queries, keys, values, seg_row, pre_keys, pre_values):
    block_rows = min(512, LEN)
    keys_pad = jnp.concatenate([jnp.zeros((SEG_MOST, HEADS, HEAD_DIM), jnp.float32), keys], axis=0)
    values_pad = jnp.concatenate([jnp.zeros((SEG_MOST, HEADS, HEAD_DIM), jnp.float32), values], axis=0)
    seg_pad = jnp.concatenate([jnp.full((SEG_MOST,), -1, jnp.int32), seg_row.astype(jnp.int32)], axis=0)
    starts = jnp.arange(LEN // block_rows, dtype=jnp.int32) * block_rows

    def one_block(block_start):
        return checked_block(block_start, queries, keys_pad, values_pad, seg_row, seg_pad, pre_keys, pre_values)
    blocks_out = lax.map(one_block, starts)
    return blocks_out.reshape(LEN, HEADS, HEAD_DIM)

def layer_row(row_in, seg_row, prefix_kv, frozen):
    norm1_gain, norm1_shift, qkv_mat, qkv_vec, out_mat, out_vec, norm2_gain, norm2_shift, fc_mat, fc_vec, proj_mat, proj_vec = frozen
    normed_first = low(layer_norm(row_in, norm1_gain, norm1_shift))
    mixed_qkv = low(low_back(matmul_high(normed_first, qkv_mat) + qkv_vec))
    queries = mixed_qkv[:, :D].reshape(LEN, HEADS, HEAD_DIM)
    keys = mixed_qkv[:, D:2 * D].reshape(LEN, HEADS, HEAD_DIM)
    values = mixed_qkv[:, 2 * D:].reshape(LEN, HEADS, HEAD_DIM)
    pre_keys = prefix_kv[:, :D].reshape(PREFIX, HEADS, HEAD_DIM)
    pre_values = prefix_kv[:, D:].reshape(PREFIX, HEADS, HEAD_DIM)
    attended = row_attention(queries, keys, values, seg_row, pre_keys, pre_values)
    attended = low(low_back(attended.reshape(LEN, D)))
    branch = low_back(matmul_high(attended, out_mat) + out_vec)
    middle = row_in + branch
    normed_second = low(layer_norm(middle, norm2_gain, norm2_shift))
    hidden_pre = low_back(matmul_high(normed_second, fc_mat) + fc_vec)
    hidden = low(gelu_tanh(hidden_pre))
    return middle + matmul_high(hidden, proj_mat) + proj_vec
checked_row = jax.checkpoint(layer_row)

def reference(activations, cotangent, segment_ids, prefix_embed, adapt_in, adapt_in_bias, adapt_out, adapt_out_bias, ln1_gain, ln1_bias, qkv_weight, qkv_bias, out_weight, out_bias, ln2_gain, ln2_bias, fc_weight, fc_bias, proj_weight, proj_bias):
    frozen = (ln1_gain.astype(jnp.float32), ln1_bias.astype(jnp.float32), qkv_weight.astype(jnp.float32), qkv_bias.astype(jnp.float32), out_weight.astype(jnp.float32), out_bias.astype(jnp.float32), ln2_gain.astype(jnp.float32), ln2_bias.astype(jnp.float32), fc_weight.astype(jnp.float32), fc_bias.astype(jnp.float32), proj_weight.astype(jnp.float32), proj_bias.astype(jnp.float32))
    row_count = MB * ROWS
    row_inputs = activations.astype(jnp.float32).reshape(row_count, LEN, D)
    row_segments = segment_ids.reshape(row_count, LEN)
    row_cotangent = cotangent.astype(jnp.float32).reshape(row_count, LEN, D)

    def forward(inputs_all, embed_arg, first_mat, first_vec, second_mat, second_vec):
        prefix_kv = low(prefix_pairs(embed_arg, first_mat, first_vec, second_mat, second_vec))

        def one_row(row_item):
            return checked_row(row_item[0], row_item[1], prefix_kv, frozen)
        return lax.map(one_row, (inputs_all, row_segments))
    outputs, pullback = jax.vjp(forward, row_inputs, prefix_embed, adapt_in, adapt_in_bias, adapt_out, adapt_out_bias)
    grads = pullback(row_cotangent)
    out_shape = (MB, ROWS, LEN, D)
    return (outputs.astype(jnp.bfloat16).reshape(out_shape), grads[0].astype(jnp.bfloat16).reshape(out_shape), grads[1], grads[2], grads[3], grads[4], grads[5])
```

```python
import math

import jax
import jax.numpy as jnp
import numpy as np
from jax import lax
from jax.experimental import pallas as pl
from jax.experimental.pallas import tpu as pltpu
from jax.sharding import PartitionSpec as P

HEADS = 16
SEG_MOST = 512
EPS = 1e-05
MASKED = -1e30
BF = jnp.bfloat16
F32 = jnp.float32
MIB = 1 << 20

VMEM = pltpu.VMEM


def mm(left, right):
    return jnp.dot(left, right, preferred_element_type=F32)


def mm_nt(left, right):
    return lax.dot_general(left, right, (((1,), (1,)), ((), ())), preferred_element_type=F32)


def mm_tn(left, right):
    return lax.dot_general(left, right, (((0,), (0,)), ((), ())), preferred_element_type=F32)


def matmul_high(left_op, right_op):
    return jnp.dot(
        left_op, right_op, precision=lax.Precision.HIGHEST, preferred_element_type=F32
    )


def swapped(value, axis, bit):
    count = lax.axis_size(axis)
    return lax.ppermute(value, axis, [(i, i ^ bit) for i in range(count)])


def moved(value, axis, steps):
    count = lax.axis_size(axis)
    low, high = max(0, -steps), min(count, count - steps)
    return lax.ppermute(value, axis, [(i, i + steps) for i in range(low, high)])


def summed_all(value):
    for axis in ("row", "seq"):
        bit = 1
        while bit < lax.axis_size(axis):
            value = value + swapped(value, axis, bit)
            bit *= 2
    return value


def cat(*parts):
    return jnp.concatenate(parts, axis=0)


X, ZN, ZF, CORE, Y = ("seq", 1), ("seq", 2), ("seq", 4), ("row", 1), ("row", 2)


def plane(block, first, second):
    half = cat(block, swapped(block, *first))
    whole = cat(half, swapped(half, *second))
    return cat(whole, swapped(whole, *CORE))


def gathered(shard, order):
    near = cat(shard, swapped(shard, *ZF))
    across = swapped(near, *ZN)
    return cat(plane(near, *order), plane(across, *order))


def piece_table(x_first):
    rel_row = jnp.arange(4, dtype=jnp.int32)[:, None] ^ lax.axis_index("row")
    rel_seq = jnp.arange(8, dtype=jnp.int32)[None, :] ^ lax.axis_index("seq")
    far, near, across_x = (rel_seq >> 2) & 1, (rel_seq >> 1) & 1, rel_seq & 1
    across_y, core = (rel_row >> 1) & 1, rel_row & 1
    one, two = (across_x, across_y) if x_first else (across_y, across_x)
    return (far | (one << 1) | (two << 2) | (core << 3) | (near << 4)).reshape(32)


def norm_parts(values):
    centre = values - jnp.mean(values, axis=-1, keepdims=True)
    spread = jnp.mean(centre * centre, axis=-1, keepdims=True)
    scale = lax.rsqrt(spread + EPS)
    return centre * scale, scale


def norm_back(values, incoming, gain):
    normal, scale = norm_parts(values)
    e = incoming * gain
    return scale * (
        e
        - jnp.mean(e, axis=-1, keepdims=True)
        - normal * jnp.mean(e * normal, axis=-1, keepdims=True)
    )


def params(limit, semantics=None):
    return pltpu.CompilerParams(vmem_limit_bytes=limit * MIB, dimension_semantics=semantics)


def whole(shape):
    return pl.BlockSpec(shape, lambda *_: (0,) * len(shape))


def piece(rows, cols, where):
    return pl.BlockSpec((1, rows, cols), where)


def qkv_kernel(tab, own, o1, h1, r2, h2, w0, w1, w2, w3, bias, mixed, natural, wide):
    step = pl.program_id(0)
    tokens = own.shape[0]
    for r, w in enumerate((w0, w1, w2, w3)):
        wide[256 * r : 256 * (r + 1), :] = w[0, :, :384]
    natural[...] = wide[...]

    def one(slot, block):
        value = (mm(block, wide[...]) + bias[...].astype(F32)).astype(BF)
        for col in range(3):
            mixed[col, slot] = value[:, 128 * col : 128 * (col + 1)]

    one(0, own[...])

    @pl.when(step >= 2)
    def _():
        for slot, ref in enumerate((o1, h1, r2, h2)):
            one(slot + 1, ref[:tokens, :])


def qkv_call(table, blocks, weights, bias, tokens, width):
    halo_rows = blocks[1].shape[0]
    return pl.pallas_call(
        qkv_kernel,
        grid_spec=pltpu.PrefetchScalarGridSpec(
            num_scalar_prefetch=1,
            grid=(8,),
            in_specs=[whole((tokens, width))]
            + [whole((halo_rows, width))] * 4
            + [
                piece(256, 512, lambda s, tab, r=r: (tab[r * 8 + s], 0, 0))
                for r in range(4)
            ]
            + [pl.BlockSpec((1, 384), lambda s, tab: (0, s))],
            out_specs=[
                pl.BlockSpec((3, 5, tokens, 128), lambda s, tab: (s, 0, 0, 0)),
                pl.BlockSpec((1024, 384), lambda s, tab: (0, s)),
            ],
            scratch_shapes=[VMEM((1024, 384), BF)],
        ),
        out_shape=[
            jax.ShapeDtypeStruct((24, 5, tokens, 128), BF),
            jax.ShapeDtypeStruct((1024, 3072), BF),
        ],
        compiler_params=params(32),
        cost_estimate=pl.CostEstimate(
            flops=2 * tokens * 1024 * 1024 * 11, bytes_accessed=20 * MIB, transcendentals=0
        ),
        name="qkv",
    )(table, *blocks, weights, weights, weights, weights, bias)


def allowed_bias(seg, out):
    query = jnp.broadcast_to(seg[0:1, :], (128, 128))
    key_at = lax.broadcasted_iota(jnp.int32, (128, 128), 0)
    query_at = lax.broadcasted_iota(jnp.int32, (128, 128), 1)
    out[0:128, :] = jnp.where(key_at < 10, 0.0, MASKED)
    for slot in range(5):
        key = jnp.broadcast_to(seg[slot : slot + 1, :], (128, 128)).T
        allowed = key == query
        if slot == 0:
            allowed = allowed & (key_at <= query_at)
        out[128 * (slot + 1) : 128 * (slot + 2), :] = jnp.where(allowed, 0.0, MASKED)


def two_heads(block):
    lane = lax.broadcasted_iota(jnp.int32, block.shape, 1)
    zero = jnp.zeros_like(block)
    return cat(jnp.where(lane < 64, block, zero), jnp.where(lane < 64, zero, block))


def heads_merged(both):
    feature = lax.broadcasted_iota(jnp.int32, (128, 128), 0)
    return jnp.where(feature < 64, both[:, :128], both[:, 128:]).T


def attend_kernel(seg, q, k, v, pk, pv, att, probs, bias):
    allowed_bias(seg[0], bias)

    def pair(p, carry):
        keys = cat(pk[p], *[k[p, slot] for slot in range(5)])
        values = cat(pv[p], *[v[p, slot] for slot in range(5)])
        queries = two_heads(q[p, 0] * 0.125)
        scores = mm_nt(keys, queries) + jnp.concatenate([bias[...], bias[...]], axis=1)
        top = jnp.max(scores, axis=0, keepdims=True)
        expo = jnp.exp(scores - top)
        total = jnp.sum(expo, axis=0, keepdims=True)
        chance = (expo * (1.0 / total)).astype(BF)
        probs[0, p] = chance
        att[:, pl.ds(pl.multiple_of(p * 128, 128), 128)] = heads_merged(
            mm_tn(values, chance)
        ).astype(BF)
        return carry

    lax.fori_loop(0, 8, pair, 0)


def attend_call(seg, mixed, pk, pv, batches, tokens):
    return pl.pallas_call(
        attend_kernel,
        grid=(batches,),
        in_specs=[
            pl.BlockSpec((1, 5, 128), lambda b: (b, 0, 0)),
            pl.BlockSpec((8, 1, 128, 128), lambda b: (0, 0, b, 0)),
            pl.BlockSpec((8, 5, 128, 128), lambda b: (1, 0, b, 0)),
            pl.BlockSpec((8, 5, 128, 128), lambda b: (2, 0, b, 0)),
            whole((8, 128, 128)),
            whole((8, 128, 128)),
        ],
        out_specs=[
            pl.BlockSpec((128, 1024), lambda b: (b, 0)),
            pl.BlockSpec((1, 8, 768, 256), lambda b: (b, 0, 0, 0)),
        ],
        out_shape=[
            jax.ShapeDtypeStruct((tokens, 1024), BF),
            jax.ShapeDtypeStruct((batches, 8, 768, 256), BF),
        ],
        scratch_shapes=[VMEM((768, 128), F32)],
        compiler_params=params(32),
        cost_estimate=pl.CostEstimate(
            flops=24 * 2 * 2 * 768 * 256 * 256,
            bytes_accessed=20 * MIB,
            transcendentals=24 * 768 * 256,
        ),
        name="attend",
    )(seg, mixed, mixed, mixed, pk, pv)


def middle_kernel(tab, att, x, *refs):
    ws, (out_bias, gain, shift, middle, normed, natural, wide, total) = refs[:8], refs[8:]
    step = pl.program_id(0)
    for r in range(4):
        for half in range(2):
            wide[256 * r : 256 * (r + 1), 128 * half : 128 * (half + 1)] = ws[2 * r + half][0]
    natural[...] = wide[...]
    cols = pl.ds(pl.multiple_of(step * 256, 256), 256)
    total[:, cols] = mm(att[...], wide[...])

    @pl.when(step == 3)
    def _():
        value = x[...].astype(F32) + total[...] + out_bias[...].astype(F32)
        middle[...] = value
        normal, _ = norm_parts(value)
        normed[...] = (normal * gain[...].astype(F32) + shift[...].astype(F32)).astype(BF)


def middle_call(table, att, x, weights, out_bias, gain, shift, tokens):
    return pl.pallas_call(
        middle_kernel,
        grid_spec=pltpu.PrefetchScalarGridSpec(
            num_scalar_prefetch=1,
            grid=(4,),
            in_specs=[whole((tokens, 1024))] * 2
            + [
                piece(256, 128, lambda i, tab, r=r, h=h: (tab[r * 8 + 2 * i + h], 0, 3))
                for r in range(4)
                for h in range(2)
            ]
            + [whole((1, 1024))] * 3,
            out_specs=[
                whole((tokens, 1024)),
                whole((tokens, 1024)),
                pl.BlockSpec((1024, 256), lambda i, tab: (0, i)),
            ],
            scratch_shapes=[VMEM((1024, 256), BF), VMEM((tokens, 1024), F32)],
        ),
        out_shape=[
            jax.ShapeDtypeStruct((tokens, 1024), F32),
            jax.ShapeDtypeStruct((tokens, 1024), BF),
            jax.ShapeDtypeStruct((1024, 1024), BF),
        ],
        compiler_params=params(24),
        cost_estimate=pl.CostEstimate(
            flops=2 * tokens * 1024 * 1024, bytes_accessed=8 * MIB, transcendentals=0
        ),
        name="middle",
    )(table, att, x, *[weights] * 8, out_bias, gain, shift)


def hidden_kernel(tab, normed, w0, w1, w2, w3, bias, hidden, slope, wide):
    for r, w in enumerate((w0, w1, w2, w3)):
        wide[256 * r : 256 * (r + 1), :] = w[0]
    v = mm(normed[...], wide[...]) + bias[...].astype(F32)
    square = v * v
    inner = 0.7978845608028654 * v * (1.0 + 0.044715 * square)
    t = jnp.tanh(inner)
    hidden[...] = (0.5 * v * (1.0 + t)).astype(BF)
    slope[...] = (
        0.5 * (1.0 + t)
        + 0.5 * v * (1.0 - t * t) * (0.7978845608028654 * (1.0 + 3 * 0.044715 * square))
    ).astype(BF)


def hidden_call(table, normed, weights, bias, tokens):
    return pl.pallas_call(
        hidden_kernel,
        grid_spec=pltpu.PrefetchScalarGridSpec(
            num_scalar_prefetch=1,
            grid=(8,),
            in_specs=[whole((tokens, 1024))]
            + [
                piece(256, 512, lambda s, tab, r=r: (tab[r * 8 + s], 0, 0))
                for r in range(4)
            ]
            + [pl.BlockSpec((1, 512), lambda s, tab: (0, s))],
            out_specs=[
                pl.BlockSpec((tokens, 512), lambda s, tab: (0, s)),
                pl.BlockSpec((tokens, 512), lambda s, tab: (0, s)),
            ],
            scratch_shapes=[VMEM((1024, 512), BF)],
        ),
        out_shape=[jax.ShapeDtypeStruct((tokens, 4096), BF)] * 2,
        compiler_params=params(24),
        cost_estimate=pl.CostEstimate(
            flops=2 * tokens * 1024 * 4096,
            bytes_accessed=16 * MIB,
            transcendentals=tokens * 4096,
        ),
        name="hidden",
    )(table, normed, *[weights] * 4, bias)


def grad_pre_kernel(tab, cot, *refs):
    ws, (slope, grad_pre, natural) = refs[:8], refs[8:]
    for s in range(8):
        for j in range(4):
            natural[256 * j : 256 * (j + 1), 128 * s : 128 * (s + 1)] = ws[s][
                0, :, 128 * j : 128 * (j + 1)
            ]
    grad_hidden = mm_nt(cot[...], natural[...])
    grad_pre[...] = (grad_hidden * slope[...].astype(F32)).astype(BF)


def grad_pre_call(table, cot, weights, slope, tokens):
    return pl.pallas_call(
        grad_pre_kernel,
        grid_spec=pltpu.PrefetchScalarGridSpec(
            num_scalar_prefetch=1,
            grid=(4,),
            in_specs=[whole((tokens, 1024))]
            + [
                piece(256, 512, lambda r, tab, s=s: (tab[r * 8 + s], 0, 0))
                for s in range(8)
            ]
            + [pl.BlockSpec((tokens, 1024), lambda r, tab: (0, r))],
            out_specs=[
                pl.BlockSpec((tokens, 1024), lambda r, tab: (0, r)),
                pl.BlockSpec((1024, 1024), lambda r, tab: (r, 0)),
            ],
        ),
        out_shape=[
            jax.ShapeDtypeStruct((tokens, 4096), BF),
            jax.ShapeDtypeStruct((4096, 1024), BF),
        ],
        compiler_params=params(24),
        cost_estimate=pl.CostEstimate(
            flops=2 * tokens * 1024 * 4096, bytes_accessed=16 * MIB, transcendentals=0
        ),
        name="grad_pre",
    )(table, cot, *[weights] * 8, slope)


def grad_middle_kernel(
    tab, grad_pre, w0, w1, w2, w3, cot, middle, gain, out_nat, grad_mid, grad_att, wide, total
):
    step = pl.program_id(0)
    for r, w in enumerate((w0, w1, w2, w3)):
        wide[256 * r : 256 * (r + 1), :] = w[0]
    part = mm_nt(grad_pre[...], wide[...])

    @pl.when(step == 0)
    def _():
        total[...] = part

    @pl.when(step > 0)
    def _():
        total[...] += part

    @pl.when(step == 7)
    def _():
        value = cot[...].astype(F32) + norm_back(middle[...], total[...], gain[...].astype(F32))
        grad_mid[...] = value
        grad_att[...] = mm_nt(value.astype(BF), out_nat[...]).astype(BF)


def grad_middle_call(table, grad_pre, weights, cot, middle, gain, out_nat, tokens):
    return pl.pallas_call(
        grad_middle_kernel,
        grid_spec=pltpu.PrefetchScalarGridSpec(
            num_scalar_prefetch=1,
            grid=(8,),
            in_specs=[pl.BlockSpec((tokens, 512), lambda s, tab: (0, s))]
            + [
                piece(256, 512, lambda s, tab, r=r: (tab[r * 8 + s], 0, 0))
                for r in range(4)
            ]
            + [
                whole((tokens, 1024)),
                whole((tokens, 1024)),
                whole((1, 1024)),
                whole((1024, 1024)),
            ],
            out_specs=[whole((tokens, 1024)), whole((tokens, 1024))],
            scratch_shapes=[VMEM((1024, 512), BF), VMEM((tokens, 1024), F32)],
        ),
        out_shape=[
            jax.ShapeDtypeStruct((tokens, 1024), F32),
            jax.ShapeDtypeStruct((tokens, 1024), BF),
        ],
        compiler_params=params(32),
        cost_estimate=pl.CostEstimate(
            flops=2 * tokens * 1024 * 5120, bytes_accessed=16 * MIB, transcendentals=0
        ),
        name="grad_middle",
    )(table, grad_pre, *[weights] * 4, cot, middle, gain, out_nat)


def attend_back_kernel(
    q, k, v, pk, pv, probs, grad_att, att, w_nat, side, near, far, own, grad_pre_kv, dkv
):
    ones = jnp.ones((8, 128), F32)
    lane = lax.broadcasted_iota(jnp.int32, (8, 128), 1)

    def pair(p, carry):
        cols = pl.ds(pl.multiple_of(p * 128, 128), 128)
        cols_v = pl.ds(pl.multiple_of(p * 128 + 1024, 128), 128)
        keys = cat(pk[p], *[k[p, slot] for slot in range(5)])
        values = cat(pv[p], *[v[p, slot] for slot in range(5)])
        queries = two_heads(q[p, 0] * 0.125)
        grad_o = grad_att[:, cols]
        grad_two = two_heads(grad_o)
        product = grad_o.astype(F32) * att[:, cols].astype(F32)
        prec = lax.Precision.HIGHEST
        delta = jnp.concatenate(
            [
                lax.dot_general(
                    jnp.where((lane < 64) == first, ones, 0.0),
                    product,
                    (((1,), (1,)), ((), ())),
                    precision=prec,
                    preferred_element_type=F32,
                )[0:1, :]
                for first in (True, False)
            ],
            axis=1,
        )
        chance = probs[0, p]
        grad_probs = mm_nt(values, grad_two)
        grad_scores = (chance.astype(F32) * (grad_probs - delta)).astype(BF)
        grad_k = mm(grad_scores, queries)
        grad_v = mm(chance, grad_two)
        grad_q = heads_merged(mm_tn(keys, grad_scores)) * 0.125
        own[:, cols] = grad_q.astype(BF)
        grad_pre_kv[0, p] = grad_k[:16]
        grad_pre_kv[1, p] = grad_v[:16]
        for slot in range(5):
            rows = slice(128 * (slot + 1), 128 * (slot + 2))
            if slot == 0:
                own[:, pl.ds(pl.multiple_of(p * 128 + 1024, 128), 128)] = grad_k[rows].astype(BF)
                own[:, pl.ds(pl.multiple_of(p * 128 + 2048, 128), 128)] = grad_v[rows].astype(BF)
            else:
                dkv[slot - 1, :, cols] = grad_k[rows].astype(BF)
                dkv[slot - 1, :, cols_v] = grad_v[rows].astype(BF)
        return carry

    lax.fori_loop(0, 8, pair, 0)
    w_kv = w_nat[:, 1024:]
    side[0] = mm_nt(dkv[0], w_kv).astype(BF)
    side[1] = mm_nt(dkv[2], w_kv).astype(BF)
    near[...] = mm_nt(dkv[1], w_kv).astype(BF)
    far[...] = mm_nt(dkv[3], w_kv).astype(BF)


def attend_back_call(batch, mixed, pk, pv, probs, grad_att, att, w_nat):
    return pl.pallas_call(
        attend_back_kernel,
        grid=(1,),
        in_specs=[
            pl.BlockSpec((8, 1, 128, 128), lambda b: (0, 0, batch, 0)),
            pl.BlockSpec((8, 5, 128, 128), lambda b: (1, 0, batch, 0)),
            pl.BlockSpec((8, 5, 128, 128), lambda b: (2, 0, batch, 0)),
            whole((8, 128, 128)),
            whole((8, 128, 128)),
            pl.BlockSpec((1, 8, 768, 256), lambda b: (batch, 0, 0, 0)),
            pl.BlockSpec((128, 1024), lambda b: (batch, 0)),
            pl.BlockSpec((128, 1024), lambda b: (batch, 0)),
            whole((1024, 3072)),
        ],
        out_specs=[
            whole((2, 128, 1024)),
            whole((128, 1024)),
            whole((128, 1024)),
            whole((128, 3072)),
            whole((2, 8, 16, 128)),
        ],
        out_shape=[
            jax.ShapeDtypeStruct((2, 128, 1024), BF),
            jax.ShapeDtypeStruct((128, 1024), BF),
            jax.ShapeDtypeStruct((128, 1024), BF),
            jax.ShapeDtypeStruct((128, 3072), BF),
            jax.ShapeDtypeStruct((2, 8, 16, 128), F32),
        ],
        scratch_shapes=[VMEM((4, 128, 2048), BF)],
        compiler_params=params(40),
        cost_estimate=pl.CostEstimate(
            flops=8 * 4 * 2 * 768 * 256 * 256 + 2 * 512 * 2048 * 1024,
            bytes_accessed=16 * MIB,
            transcendentals=0,
        ),
        name="attend_back",
    )(mixed, mixed, mixed, pk, pv, probs, grad_att, att, w_nat)


def units_gathered(qkv_weight, out_weight, fc_weight, proj_weight):
    row_count, seq_count = lax.axis_size("row"), lax.axis_size("seq")
    if (row_count, seq_count) == (4, 8):
        first = jnp.concatenate([qkv_weight, out_weight], axis=1)[None]
        third = jnp.concatenate([proj_weight[256 * j : 256 * (j + 1)] for j in range(4)], axis=1)[
            None
        ]
        tables = (piece_table(True), piece_table(True), piece_table(False))
        return (
            gathered(first, (X, Y)),
            gathered(fc_weight[None], (X, Y)),
            gathered(third, (Y, X)),
        ), tables

    def full(shard):
        rows = lax.all_gather(shard, "row", axis=0, tiled=True)
        return lax.all_gather(rows, "seq", axis=1, tiled=True)

    def pieces(matrix):
        rows, cols = matrix.shape
        return (
            matrix.reshape(4, rows // 4, 8, cols // 8)
            .transpose(0, 2, 1, 3)
            .reshape(32, rows // 4, cols // 8)
        )

    proj = pieces(full(proj_weight)).reshape(32, 4, 256, 128)
    identity = jnp.arange(32, dtype=jnp.int32)
    return (
        jnp.concatenate([pieces(full(qkv_weight)), pieces(full(out_weight))], axis=2),
        pieces(full(fc_weight)),
        proj.transpose(0, 2, 1, 3).reshape(32, 256, 512),
    ), (identity,) * 3


def local(
    activations,
    cotangent,
    segment_ids,
    prefix_embed,
    adapt_in,
    adapt_in_bias,
    adapt_out,
    adapt_out_bias,
    ln1_gain,
    ln1_bias,
    qkv_weight,
    qkv_bias,
    out_weight,
    out_bias,
    ln2_gain,
    ln2_bias,
    fc_weight,
    fc_bias,
    proj_weight,
    proj_bias,
):
    batches, rows_dev, tok_dev, width = activations.shape
    tokens = batches * rows_dev * tok_dev
    assert tok_dev == 128 and rows_dev == 1 and lax.axis_size("seq") % 2 == 0
    x_side = lax.axis_index("seq") % 2

    x = activations.reshape(tokens, width)
    cot = cotangent.reshape(tokens, width)

    normal, _ = norm_parts(x.astype(F32))
    normed = (normal * ln1_gain.astype(F32) + ln1_bias.astype(F32)).astype(BF)
    ids = (segment_ids.reshape(1, tokens) + 1).astype(BF)
    sent = cat(normed, jnp.pad(ids, ((0, 7), (0, width - tokens))))
    h1 = moved(sent, "seq", 2)
    h2 = moved(h1, "seq", 2)
    o1 = swapped(h1, *X)
    r2 = swapped(jnp.where(x_side == 0, sent, h2), *X)
    seg = jnp.stack([part[tokens, :tokens] for part in (sent, o1, h1, r2, h2)])
    seg = seg.astype(F32).reshape(5, batches, tok_dev).transpose(1, 0, 2)

    (unit0, unit1, unit2), (tab0, tab1, tab2) = units_gathered(
        qkv_weight, out_weight, fc_weight, proj_weight
    )

    squashed = jnp.tanh(matmul_high(prefix_embed, adapt_in) + adapt_in_bias)
    prefix_kv = matmul_high(squashed, adapt_out) + adapt_out_bias
    count = prefix_kv.shape[0]
    prefix_low = jnp.pad(prefix_kv.astype(BF), ((0, 128 - count), (0, 0)))
    pk = prefix_low[:, :width].reshape(128, 8, 128).transpose(1, 0, 2)
    pv = prefix_low[:, width:].reshape(128, 8, 128).transpose(1, 0, 2)

    mixed, w_nat = qkv_call(
        tab0, (normed, o1, h1, r2, h2), unit0, qkv_bias.reshape(1, -1), tokens, width
    )
    att, probs = attend_call(seg, mixed, pk, pv, batches, tokens)
    middle, normed2, out_nat = middle_call(
        tab0,
        att,
        x,
        unit0,
        out_bias.reshape(1, -1),
        ln2_gain.reshape(1, -1),
        ln2_bias.reshape(1, -1),
        tokens,
    )
    hidden, slope = hidden_call(tab1, normed2, unit1, fc_bias.reshape(1, -1), tokens)
    grad_pre, proj_nat = grad_pre_call(tab2, cot, unit2, slope, tokens)
    grad_mid, grad_att = grad_middle_call(
        tab1, grad_pre, unit1, cot, middle, ln2_gain.reshape(1, -1), out_nat, tokens
    )

    owns, arrived, grad_pre_kv = [], [], 0.0
    for batch in range(batches):
        side, near, far, own, pre_kv = attend_back_call(
            batch, mixed, pk, pv, probs, grad_att, att, w_nat
        )
        grad_pre_kv = grad_pre_kv + pre_kv
        other = swapped(side, *X).astype(F32)
        to_far = far.astype(F32) + jnp.where(x_side == 1, other[1], 0.0)
        passing = moved(to_far.astype(BF), "seq", -2).astype(F32)
        to_near = near.astype(F32) + other[0] + passing
        landed = moved(to_near.astype(BF), "seq", -2).astype(F32)
        arrived.append(landed + jnp.where(x_side == 0, other[1], 0.0))
        owns.append(own)

    grad_normed = mm_nt(cat(*owns), w_nat) + cat(*arrived)
    in_grad = grad_mid + norm_back(x.astype(F32), grad_normed, ln1_gain.astype(F32))
    output = middle + mm(hidden, proj_nat) + proj_bias.astype(F32)

    total = summed_all(grad_pre_kv[:, :, :count])
    grad_kv = total.transpose(2, 0, 1, 3).reshape(count, 2 * width)
    adapt_out_grad = lax.dot_general(
        squashed,
        grad_kv,
        (((0,), (0,)), ((), ())),
        precision=lax.Precision.HIGHEST,
        preferred_element_type=F32,
    )
    grad_z = lax.dot_general(
        grad_kv,
        adapt_out,
        (((1,), (1,)), ((), ())),
        precision=lax.Precision.HIGHEST,
        preferred_element_type=F32,
    ) * (1.0 - squashed * squashed)
    adapt_in_grad = lax.dot_general(
        prefix_embed,
        grad_z,
        (((0,), (0,)), ((), ())),
        precision=lax.Precision.HIGHEST,
        preferred_element_type=F32,
    )
    prefix_grad = lax.dot_general(
        grad_z,
        adapt_in,
        (((1,), (1,)), ((), ())),
        precision=lax.Precision.HIGHEST,
        preferred_element_type=F32,
    )
    shape = activations.shape
    return (
        output.astype(BF).reshape(shape),
        in_grad.astype(BF).reshape(shape),
        prefix_grad,
        adapt_in_grad,
        jnp.sum(grad_z, axis=0),
        adapt_out_grad,
        jnp.sum(grad_kv, axis=0),
    )


def solution(mesh):
    rows = P(None, "row", "seq", None)
    split = P("row", "seq")
    placed = (
        rows,
        rows,
        P(None, "row", "seq"),
        P(),
        P(),
        P(),
        P(),
        P(),
        P(),
        P(),
        split,
        P(),
        split,
        P(),
        P(),
        P(),
        split,
        P(),
        split,
        P(),
    )
    return jax.shard_map(
        local,
        mesh=mesh,
        in_specs=placed,
        out_specs=(rows, rows, P(), P(), P(), P(), P()),
        check_vma=False,
    )
```

```python
import functools

import jax
import jax.numpy as jnp
from jax import lax
from jax.experimental import pallas as pl
from jax.experimental.pallas import tpu as pltpu
from jax.sharding import PartitionSpec as P

EPS = 1e-05
MASKED = -1e30
PREFIX_ROWS = 16
BF = jnp.bfloat16
F32 = jnp.float32
MIB = 1 << 20
HIGHEST = lax.Precision.HIGHEST
VMEM = pltpu.VMEM
ANYWHERE = pl.BlockSpec(memory_space=pl.ANY)
SCALARS = pl.BlockSpec(memory_space=pltpu.SMEM)


def mm(left, right, precision=None):
    return jnp.dot(left, right, precision=precision, preferred_element_type=F32)


def mm_nt(left, right, precision=None):
    return lax.dot_general(
        left, right, (((1,), (1,)), ((), ())), precision=precision, preferred_element_type=F32
    )


def mm_tn(left, right, precision=None):
    return lax.dot_general(
        left, right, (((0,), (0,)), ((), ())), precision=precision, preferred_element_type=F32
    )


def cat(*parts):
    return jnp.concatenate(parts, axis=0)


X, ZN, ZF, CORE, Y = ("seq", 1), ("seq", 2), ("seq", 4), ("row", 1), ("row", 2)


def swapped(value, axis, bit):
    count = lax.axis_size(axis)
    return lax.ppermute(value, axis, [(i, i ^ bit) for i in range(count)])


def moved(value, axis, steps):
    count = lax.axis_size(axis)
    low, high = max(0, -steps), min(count, count - steps)
    return lax.ppermute(value, axis, [(i, i + steps) for i in range(low, high)])


def after(value, *others):
    return lax.optimization_barrier((value,) + others)[0]


def sum_steps(value):
    steps = []
    for axis in ("row", "seq"):
        bit = 1
        while bit < lax.axis_size(axis):
            value = value + swapped(value, axis, bit)
            steps.append(value)
            bit *= 2
    return steps


NATURAL = tuple((r, s) for r in range(4) for s in range(8))


def with_cores(parts):
    out = []
    for array, zs, x, y in parts:
        out.append((array, tuple((2 * y, 2 * z + x) for z in zs)))
        out.append((swapped(array, *CORE), tuple((2 * y + 1, 2 * z + x) for z in zs)))
    return out


def norm_parts(values):
    centre = values - jnp.mean(values, axis=-1, keepdims=True)
    spread = jnp.mean(centre * centre, axis=-1, keepdims=True)
    scale = lax.rsqrt(spread + EPS)
    return centre * scale, scale


def norm_back(values, incoming, gain):
    normal, scale = norm_parts(values)
    e = incoming * gain
    return scale * (
        e
        - jnp.mean(e, axis=-1, keepdims=True)
        - normal * jnp.mean(e * normal, axis=-1, keepdims=True)
    )


def call_params(limit):
    return pltpu.CompilerParams(vmem_limit_bytes=limit * MIB)


def lasting(micros):
    return pl.CostEstimate(
        flops=int(micros * 1e9), bytes_accessed=int(micros * 1e6), transcendentals=0
    )


def whole(shape):
    return pl.BlockSpec(shape, lambda *_: (0,) * len(shape))


def lanes(start, size=128):
    if isinstance(start, int):
        return pl.ds(start, size)
    return pl.ds(pl.multiple_of(start, 128), size)


def each_piece(me, arrays, spots):
    for array, slots in zip(arrays, spots):
        for slot, (row_bits, seq_bits) in enumerate(slots):
            yield array, slot, me[0] ^ row_bits, me[1] ^ seq_bits


def first_norm_kernel(x, ids, gain, shift, sent):
    tokens = x.shape[0]
    normal, _ = norm_parts(x[...].astype(F32))
    sent[:tokens, :] = (normal * gain[...].astype(F32) + shift[...].astype(F32)).astype(BF)
    sent[tokens:, :] = ids[...]


def first_norm_call(x, ids, gain, shift):
    tokens, width = x.shape
    return pl.pallas_call(
        first_norm_kernel,
        out_shape=jax.ShapeDtypeStruct((tokens + 8, width), BF),
        compiler_params=call_params(16),
        cost_estimate=lasting(1),
        name="first_norm",
    )(x, ids, gain, shift)


def prefix_kernel(embed, w_in, b_in, w_out, b_out, squashed, low):
    inner = jnp.tanh(mm(embed[...], w_in[...], HIGHEST) + b_in[...])
    squashed[...] = inner
    pairs = mm(inner, w_out[...], HIGHEST) + b_out[...]
    pairs = cat(pairs, jnp.zeros((PREFIX_ROWS - pairs.shape[0], pairs.shape[1]), F32)).astype(BF)
    for p in range(low.shape[0]):
        low[p] = pairs[:, 128 * p : 128 * (p + 1)]


def prefix_call(embed, w_in, b_in, w_out, b_out):
    return pl.pallas_call(
        prefix_kernel,
        out_shape=[
            jax.ShapeDtypeStruct((embed.shape[0], w_in.shape[1]), F32),
            jax.ShapeDtypeStruct((w_out.shape[1] // 128, PREFIX_ROWS, 128), BF),
        ],
        compiler_params=call_params(24),
        cost_estimate=lasting(1),
        name="prefix",
    )(embed, w_in, b_in, w_out, b_out)


def prefix_back_kernel(
    count, total, squashed, embed, w_in, w_out, prefix_grad, in_grad, in_bias, out_grad, out_bias
):
    grad_kv = jnp.concatenate(
        [total[half, p][:count] for half in range(2) for p in range(8)], axis=1
    )
    inner = squashed[...]
    out_bias[...] = jnp.sum(grad_kv, axis=0, keepdims=True)
    low_kv = grad_kv.astype(BF)
    out_grad[...] = mm_tn(inner.astype(BF), low_kv)
    grad_z = mm_nt(w_out[...].astype(BF), low_kv).T * (1.0 - inner * inner)
    in_bias[...] = jnp.sum(grad_z, axis=0, keepdims=True)
    low_z = grad_z.astype(BF)
    in_grad[...] = mm_tn(embed[...].astype(BF), low_z)
    prefix_grad[...] = mm_nt(w_in[...].astype(BF), low_z).T


def prefix_back_call(total, squashed, embed, w_in, w_out):
    count, width = embed.shape
    hidden = w_in.shape[1]
    return pl.pallas_call(
        functools.partial(prefix_back_kernel, count),
        out_shape=[
            jax.ShapeDtypeStruct((count, width), F32),
            jax.ShapeDtypeStruct((width, hidden), F32),
            jax.ShapeDtypeStruct((1, hidden), F32),
            jax.ShapeDtypeStruct((hidden, 2 * width), F32),
            jax.ShapeDtypeStruct((1, 2 * width), F32),
        ],
        compiler_params=call_params(24),
        cost_estimate=lasting(1),
        name="prefix_back",
    )(total, squashed, embed, w_in, w_out)


def qkv_kernel(spots, me, own, o1, h1, r2, h2, bias, *refs):
    arrays = refs[: len(spots)]
    mixed, natural, wide, sems = refs[len(spots) :]
    step = pl.program_id(0)
    tokens = mixed.shape[2]

    @pl.when(step == 0)
    def _():
        for array, slot, r, s in each_piece(me, arrays, spots):
            pltpu.make_async_copy(
                array.at[slot, :, pl.ds(0, 384)],
                wide.at[
                    s // 2,
                    pl.ds(pl.multiple_of(r * 256, 256), 256),
                    pl.ds(pl.multiple_of((s % 2) * 384, 128), 384),
                ],
                sems.at[s // 2],
            ).start()

    pltpu.make_async_copy(wide.at[step], wide.at[step], sems.at[step]).wait()
    natural[...] = wide[step]

    def one(slot, block):
        value = (mm(block, wide[step]) + bias[...].astype(F32)).astype(BF)
        for col in range(6):
            mixed[col, slot] = value[:, 128 * col : 128 * (col + 1)]

    one(0, own[:tokens, :])

    @pl.when(step >= 1)
    def _():
        for slot, ref in enumerate((o1, h1, r2, h2)):
            one(slot + 1, ref[:tokens, :])


def qkv_call(me, blocks, parts, bias, tokens):
    spots = tuple(part[1] for part in parts)
    return pl.pallas_call(
        functools.partial(qkv_kernel, spots),
        grid=(4,),
        in_specs=[SCALARS]
        + [whole(block.shape) for block in blocks]
        + [pl.BlockSpec((1, 768), lambda s: (0, s))]
        + [ANYWHERE] * len(spots),
        out_specs=[
            pl.BlockSpec((6, 5, tokens, 128), lambda s: (s, 0, 0, 0)),
            pl.BlockSpec((1024, 768), lambda s: (0, s)),
        ],
        out_shape=[
            jax.ShapeDtypeStruct((24, 5, tokens, 128), BF),
            jax.ShapeDtypeStruct((1024, 3072), BF),
        ],
        scratch_shapes=[VMEM((4, 1024, 768), BF), pltpu.SemaphoreType.DMA((4,))],
        compiler_params=call_params(40),
        cost_estimate=lasting(1),
        name="qkv",
    )(me, *blocks, bias, *[part[0] for part in parts])


def allowed_bias(seg, out):
    query = jnp.broadcast_to(seg[0:1, :], (128, 128))
    key_at = lax.broadcasted_iota(jnp.int32, (128, 128), 0)
    query_at = lax.broadcasted_iota(jnp.int32, (128, 128), 1)
    prefix_at = lax.broadcasted_iota(jnp.int32, (PREFIX_ROWS, 256), 0)
    out[0:PREFIX_ROWS, :] = jnp.where(prefix_at < 10, 0.0, MASKED)
    for slot in range(5):
        key = jnp.broadcast_to(seg[slot : slot + 1, :], (128, 128)).T
        allowed = key == query
        if slot == 0:
            allowed = allowed & (key_at <= query_at)
        value = jnp.where(allowed, 0.0, MASKED)
        rows = slice(PREFIX_ROWS + 128 * slot, PREFIX_ROWS + 128 * (slot + 1))
        out[rows, :128] = value
        out[rows, 128:] = value


def two_heads(block):
    lane = lax.broadcasted_iota(jnp.int32, block.shape, 1)
    zero = jnp.zeros_like(block)
    return cat(jnp.where(lane < 64, block, zero), jnp.where(lane < 64, zero, block))


def heads_merged(both):
    feature = lax.broadcasted_iota(jnp.int32, (128, 128), 0)
    return jnp.where(feature < 64, both[:, :128], both[:, 128:]).T


KEYS = PREFIX_ROWS + 5 * 128


def attend_kernel(seg, q, k, v, pk, pv, att, probs, bias):
    allowed_bias(seg[0], bias)
    for p in range(8):
        keys = cat(pk[p], *[k[p, slot] for slot in range(5)])
        values = cat(pv[p], *[v[p, slot] for slot in range(5)])
        scores = mm_nt(keys, two_heads(q[p, 0] * 0.125)) + bias[...]
        top = jnp.max(scores, axis=0, keepdims=True)
        expo = jnp.exp(scores - top)
        total = jnp.sum(expo, axis=0, keepdims=True)
        chance = (expo * (1.0 / total)).astype(BF)
        probs[0, p] = chance
        att[:, lanes(p * 128)] = heads_merged(mm_tn(values, chance)).astype(BF)


def attend_call(seg, mixed, prefix_low, batches, tokens):
    return pl.pallas_call(
        attend_kernel,
        grid=(batches,),
        in_specs=[
            pl.BlockSpec((1, 5, 128), lambda b: (b, 0, 0)),
            pl.BlockSpec((8, 1, 128, 128), lambda b: (0, 0, b, 0)),
            pl.BlockSpec((8, 5, 128, 128), lambda b: (1, 0, b, 0)),
            pl.BlockSpec((8, 5, 128, 128), lambda b: (2, 0, b, 0)),
            pl.BlockSpec((8, PREFIX_ROWS, 128), lambda b: (0, 0, 0)),
            pl.BlockSpec((8, PREFIX_ROWS, 128), lambda b: (1, 0, 0)),
        ],
        out_specs=[
            pl.BlockSpec((128, 1024), lambda b: (b, 0)),
            pl.BlockSpec((1, 8, KEYS, 256), lambda b: (b, 0, 0, 0)),
        ],
        out_shape=[
            jax.ShapeDtypeStruct((tokens, 1024), BF),
            jax.ShapeDtypeStruct((batches, 8, KEYS, 256), BF),
        ],
        scratch_shapes=[VMEM((KEYS, 256), F32)],
        compiler_params=call_params(48),
        cost_estimate=lasting(1),
        name="attend",
    )(seg, mixed, mixed, mixed, prefix_low, prefix_low)


def middle_kernel(spots, me, att, x, out_bias, gain, shift, *refs):
    arrays = refs[: len(spots)]
    middle, normed, natural, sem = refs[len(spots) :]
    for array, slot, r, s in each_piece(me, arrays, spots):
        pltpu.make_async_copy(
            array.at[slot, :, pl.ds(384, 128)],
            natural.at[pl.ds(pl.multiple_of(r * 256, 256), 256), lanes(s * 128)],
            sem,
        ).start()
    pltpu.make_async_copy(natural, natural, sem).wait()
    value = x[...].astype(F32) + mm(att[...], natural[...]) + out_bias[...].astype(F32)
    middle[...] = value
    normal, _ = norm_parts(value)
    normed[...] = (normal * gain[...].astype(F32) + shift[...].astype(F32)).astype(BF)


def middle_call(me, att, x, parts, out_bias, gain, shift):
    spots = tuple(part[1] for part in parts)
    tokens = x.shape[0]
    return pl.pallas_call(
        functools.partial(middle_kernel, spots),
        grid=(1,),
        in_specs=[SCALARS]
        + [whole((tokens, 1024))] * 2
        + [whole((1, 1024))] * 3
        + [ANYWHERE] * len(spots),
        out_specs=[whole((tokens, 1024)), whole((tokens, 1024)), whole((1024, 1024))],
        out_shape=[
            jax.ShapeDtypeStruct((tokens, 1024), F32),
            jax.ShapeDtypeStruct((tokens, 1024), BF),
            jax.ShapeDtypeStruct((1024, 1024), BF),
        ],
        scratch_shapes=[pltpu.SemaphoreType.DMA],
        compiler_params=call_params(40),
        cost_estimate=lasting(1),
        name="middle",
    )(me, att, x, out_bias, gain, shift, *[part[0] for part in parts])


def proj_copies(me, arrays, spots, place, sems):
    for array, slot, r, s in each_piece(me, arrays, spots):
        for j in range(4):
            pltpu.make_async_copy(
                array.at[slot, 1, :, pl.ds(128 * j, 128)],
                place.at[r, pl.ds(256 * j, 256), lanes(s * 128)],
                sems.at[r],
            ).start()


def mlp_kernel(spots, me, normed, cot, middle, gain, fc_bias, out_nat, *refs):
    arrays = refs[: len(spots)]
    hidden, grad_mid, grad_att, slope, proj, fc, total, fc_sems, proj_sems = refs[len(spots) :]
    for array, slot, r, s in each_piece(me, arrays, spots):
        pltpu.make_async_copy(
            array.at[slot, 0],
            fc.at[s, pl.ds(pl.multiple_of(r * 256, 256), 256), :],
            fc_sems.at[s],
        ).start()
    proj_copies(me, arrays, spots, proj, proj_sems)
    for s in range(8):
        pltpu.make_async_copy(fc.at[s], fc.at[s], fc_sems.at[s]).wait()
        cols = pl.ds(512 * s, 512)
        v = mm(normed[...], fc[s]) + fc_bias[:, cols].astype(F32)
        cubic = (0.7978845608028654 * 0.044715) * (v * v)
        t = jnp.tanh(v * (cubic + 0.7978845608028654))
        half = 0.5 * t + 0.5
        hidden[:, cols] = (v * half).astype(BF)
        slope[:, cols] = (
            half + v * (half - half * half) * (6.0 * cubic + 2 * 0.7978845608028654)
        ).astype(BF)
    for r in range(4):
        pltpu.make_async_copy(proj.at[r], proj.at[r], proj_sems.at[r]).wait()
        for s in (2 * r, 2 * r + 1):
            back = mm_nt(cot[...], proj[r, pl.ds(512 * (s % 2), 512), :])
            grad_pre = (back * slope[:, pl.ds(512 * s, 512)].astype(F32)).astype(BF)
            part = mm_nt(grad_pre, fc[s])
            if s == 0:
                total[...] = part
            else:
                total[...] += part
    value = cot[...].astype(F32) + norm_back(middle[...], total[...], gain[...].astype(F32))
    grad_mid[...] = value
    grad_att[...] = mm_nt(value.astype(BF), out_nat[...]).astype(BF)


def mlp_call(me, normed, cot, middle, gain, fc_bias, out_nat, parts):
    spots = tuple(part[1] for part in parts)
    tokens = cot.shape[0]
    return pl.pallas_call(
        functools.partial(mlp_kernel, spots),
        grid=(1,),
        in_specs=[SCALARS]
        + [whole((tokens, 1024))] * 3
        + [whole((1, 1024)), whole((1, 4096)), whole((1024, 1024))]
        + [ANYWHERE] * len(spots),
        out_specs=[
            whole((tokens, 4096)),
            whole((tokens, 1024)),
            whole((tokens, 1024)),
        ],
        out_shape=[
            jax.ShapeDtypeStruct((tokens, 4096), BF),
            jax.ShapeDtypeStruct((tokens, 1024), F32),
            jax.ShapeDtypeStruct((tokens, 1024), BF),
        ],
        scratch_shapes=[
            VMEM((tokens, 4096), BF),
            VMEM((4, 1024, 1024), BF),
            VMEM((8, 1024, 512), BF),
            VMEM((tokens, 1024), F32),
            pltpu.SemaphoreType.DMA((8,)),
            pltpu.SemaphoreType.DMA((4,)),
        ],
        compiler_params=call_params(48),
        cost_estimate=lasting(1),
        name="mlp",
    )(me, normed, cot, middle, gain, fc_bias, out_nat, *[part[0] for part in parts])


def output_kernel(spots, me, hidden, middle, proj_bias, *refs):
    arrays = refs[: len(spots)]
    output, proj, total, sems = refs[len(spots) :]
    proj_copies(me, arrays, spots, proj, sems)
    total[...] = middle[...] + proj_bias[...].astype(F32)
    for r in range(4):
        pltpu.make_async_copy(proj.at[r], proj.at[r], sems.at[r]).wait()
        total[...] += mm(hidden[:, pl.ds(1024 * r, 1024)], proj[r])
    output[...] = total[...].astype(BF)


def output_call(me, hidden, middle, proj_bias, parts):
    spots = tuple(part[1] for part in parts)
    tokens = hidden.shape[0]
    return pl.pallas_call(
        functools.partial(output_kernel, spots),
        grid=(1,),
        in_specs=[SCALARS, whole((tokens, 4096)), whole((tokens, 1024)), whole((1, 1024))]
        + [ANYWHERE] * len(spots),
        out_specs=whole((tokens, 1024)),
        out_shape=jax.ShapeDtypeStruct((tokens, 1024), BF),
        scratch_shapes=[
            VMEM((4, 1024, 1024), BF),
            VMEM((tokens, 1024), F32),
            pltpu.SemaphoreType.DMA((4,)),
        ],
        compiler_params=call_params(48),
        cost_estimate=lasting(1),
        name="output",
    )(me, hidden, middle, proj_bias, *[part[0] for part in parts])


def row_deltas(grad_att, att):
    width = grad_att.shape[1]
    rows = max(8, width // 64)
    head = lax.broadcasted_iota(jnp.int32, (rows, width), 0)
    lane = lax.broadcasted_iota(jnp.int32, (rows, width), 1)
    pick = jnp.where(lane // 64 == head, 1.0, 0.0).astype(BF)
    product = grad_att.astype(F32) * att.astype(F32)
    high = product.astype(BF)
    return mm_nt(pick, high) + mm_nt(pick, (product - high.astype(F32)).astype(BF))


def both_heads(delta, p):
    return jnp.concatenate([delta[2 * p : 2 * p + 1, :], delta[2 * p + 1 : 2 * p + 2, :]], axis=1)


def prefix_part_kernel(q, pv, probs, grad_att, att, grad_pre_kv):
    step = pl.program_id(0)

    @pl.when(step == 0)
    def _():
        grad_pre_kv[...] = jnp.zeros_like(grad_pre_kv)

    delta = row_deltas(grad_att[...], att[...])
    for p in range(8):
        grad_two = two_heads(grad_att[:, 128 * p : 128 * (p + 1)])
        chance = probs[0, p]
        grad_probs = mm_nt(pv[p], grad_two)
        grad_scores = (chance.astype(F32) * (grad_probs - both_heads(delta, p))).astype(BF)
        grad_pre_kv[0, p] += mm(grad_scores, two_heads(q[p, 0] * 0.125))
        grad_pre_kv[1, p] += mm(chance, grad_two)


def prefix_part_call(mixed, prefix_low, probs, grad_att, att):
    return pl.pallas_call(
        prefix_part_kernel,
        grid=(probs.shape[0],),
        in_specs=[
            pl.BlockSpec((8, 1, 128, 128), lambda b: (0, 0, b, 0)),
            pl.BlockSpec((8, PREFIX_ROWS, 128), lambda b: (1, 0, 0)),
            pl.BlockSpec((1, 8, PREFIX_ROWS, 256), lambda b: (b, 0, 0, 0)),
            pl.BlockSpec((128, 1024), lambda b: (b, 0)),
            pl.BlockSpec((128, 1024), lambda b: (b, 0)),
        ],
        out_specs=whole((2, 8, PREFIX_ROWS, 128)),
        out_shape=jax.ShapeDtypeStruct((2, 8, PREFIX_ROWS, 128), F32),
        compiler_params=call_params(48),
        cost_estimate=lasting(1),
        name="prefix_part",
    )(mixed, prefix_low, probs, grad_att, att)


def attend_back_kernel(
    q, k, v, pk, pv, probs, grad_att, att, w_nat, side, near, far, own, dkv, w_kv, sem
):
    step = pl.program_id(0)
    weights = pltpu.make_async_copy(w_nat.at[:, pl.ds(1024, 2048)], w_kv, sem)

    @pl.when(step == 0)
    def _():
        weights.start()

    delta = row_deltas(grad_att[...], att[...])
    for i in range(2):
        p = step * 2 + i
        keys = cat(pk[i], *[k[i, slot] for slot in range(5)])
        values = cat(pv[i], *[v[i, slot] for slot in range(5)])
        queries = two_heads(q[i, 0] * 0.125)
        grad_two = two_heads(grad_att[:, 128 * i : 128 * (i + 1)])
        row_delta = both_heads(delta, i)
        chance = probs[0, i]
        grad_probs = mm_nt(values, grad_two)
        grad_scores = (chance.astype(F32) * (grad_probs - row_delta)).astype(BF)
        grad_k = mm(grad_scores, queries)
        grad_v = mm(chance, grad_two)
        grad_q = heads_merged(mm_tn(keys, grad_scores)) * 0.125
        own[:, lanes(p * 128)] = grad_q.astype(BF)
        for slot in range(5):
            rows = slice(PREFIX_ROWS + 128 * slot, PREFIX_ROWS + 128 * (slot + 1))
            if slot == 0:
                own[:, lanes(p * 128 + 1024)] = grad_k[rows].astype(BF)
                own[:, lanes(p * 128 + 2048)] = grad_v[rows].astype(BF)
            else:
                sent = slice(128 * (slot - 1), 128 * slot)
                dkv[sent, lanes(p * 128)] = grad_k[rows].astype(BF)
                dkv[sent, lanes(p * 128 + 1024)] = grad_v[rows].astype(BF)

    @pl.when(step == 3)
    def _():
        weights.wait()
        part = mm_nt(dkv[...], w_kv[...]).astype(BF)
        side[0] = part[:128]
        near[...] = part[128:256]
        side[1] = part[256:384]
        far[...] = part[384:]


def attend_back_call(batch, mixed, prefix_low, probs, grad_att, att, w_nat):
    return pl.pallas_call(
        attend_back_kernel,
        grid=(4,),
        in_specs=[
            pl.BlockSpec((2, 1, 128, 128), lambda i: (i, 0, batch, 0)),
            pl.BlockSpec((2, 5, 128, 128), lambda i: (4 + i, 0, batch, 0)),
            pl.BlockSpec((2, 5, 128, 128), lambda i: (8 + i, 0, batch, 0)),
            pl.BlockSpec((2, PREFIX_ROWS, 128), lambda i: (i, 0, 0)),
            pl.BlockSpec((2, PREFIX_ROWS, 128), lambda i: (4 + i, 0, 0)),
            pl.BlockSpec((1, 2, KEYS, 256), lambda i: (batch, i, 0, 0)),
            pl.BlockSpec((128, 256), lambda i: (batch, i)),
            pl.BlockSpec((128, 256), lambda i: (batch, i)),
            ANYWHERE,
        ],
        out_specs=[
            whole((2, 128, 1024)),
            whole((128, 1024)),
            whole((128, 1024)),
            whole((128, 3072)),
        ],
        out_shape=[
            jax.ShapeDtypeStruct((2, 128, 1024), BF),
            jax.ShapeDtypeStruct((128, 1024), BF),
            jax.ShapeDtypeStruct((128, 1024), BF),
            jax.ShapeDtypeStruct((128, 3072), BF),
        ],
        scratch_shapes=[VMEM((512, 2048), BF), VMEM((1024, 2048), BF), pltpu.SemaphoreType.DMA],
        compiler_params=call_params(48),
        cost_estimate=lasting(1),
        name="attend_back",
    )(mixed, mixed, mixed, prefix_low, prefix_low, probs, grad_att, att, w_nat)


def own_back_kernel(own, w_nat, result):
    result[...] = mm_nt(own[...], w_nat[...])


def own_back_call(own, w_nat):
    tokens = own.shape[0]
    return pl.pallas_call(
        own_back_kernel,
        grid=(4,),
        in_specs=[whole((tokens, 3072)), pl.BlockSpec((256, 3072), lambda i: (i, 0))],
        out_specs=pl.BlockSpec((tokens, 256), lambda i: (0, i)),
        out_shape=jax.ShapeDtypeStruct((tokens, 1024), F32),
        compiler_params=call_params(48),
        cost_estimate=lasting(1),
        name="own_back",
    )(own, w_nat)


def first_back_kernel(x, grad_own, grad_mid, gain, *refs):
    arrived, in_grad = refs[:-1], refs[-1]
    for batch, parts in enumerate(zip(arrived[0::2], arrived[1::2])):
        rows = slice(128 * batch, 128 * (batch + 1))
        incoming = grad_own[rows, :] + parts[0][...].astype(F32) + parts[1][...].astype(F32)
        back = norm_back(x[rows, :].astype(F32), incoming, gain[...].astype(F32))
        in_grad[rows, :] = (grad_mid[rows, :] + back).astype(BF)


def first_back_call(x, grad_own, grad_mid, gain, arrived):
    return pl.pallas_call(
        first_back_kernel,
        out_shape=jax.ShapeDtypeStruct(x.shape, BF),
        compiler_params=call_params(24),
        cost_estimate=lasting(1),
        name="first_back",
    )(x, grad_own, grad_mid, gain, *arrived)


def full(shard):
    rows = lax.all_gather(shard, "row", axis=0, tiled=True)
    return lax.all_gather(rows, "seq", axis=1, tiled=True)


def pieces(matrix):
    rows, cols = matrix.shape
    return (
        matrix.reshape(4, rows // 4, 8, cols // 8)
        .transpose(0, 2, 1, 3)
        .reshape(32, rows // 4, cols // 8)
    )


def gathered_plainly(sent, x_side, qkv_weight, out_weight, fc_weight, proj_weight):
    proj = pieces(full(proj_weight)).reshape(32, 4, 256, 128)
    proj = proj.transpose(0, 2, 1, 3).reshape(32, 256, 512)
    first = jnp.concatenate([pieces(full(qkv_weight)), pieces(full(out_weight))], axis=2)
    second = jnp.stack([pieces(full(fc_weight)), proj], axis=1)
    h1 = moved(sent, "seq", 2)
    h2 = moved(h1, "seq", 2)
    o1 = swapped(h1, *X)
    r2 = swapped(jnp.where(x_side == 0, sent, h2), *X)
    return (h1, h2, o1, r2), [(first, NATURAL)], second


def gathered_by_swaps(sent, x_side, qkv_weight, out_weight, fc_weight, proj_weight):
    proj = jnp.concatenate([proj_weight[256 * j : 256 * (j + 1)] for j in range(4)], axis=1)
    second = lax.all_gather(jnp.stack([fc_weight, proj]), ("row", "seq"), axis=0)
    first = jnp.concatenate([qkv_weight, out_weight], axis=1)[None]
    v0 = cat(first, swapped(first, *ZF))
    g0 = swapped(v0, *ZN)
    h1 = moved(after(sent, v0), "seq", 2)
    v = cat(v0, g0)
    vx, vy = swapped(v, *X), swapped(v, *Y)
    h2 = moved(after(h1, g0), "seq", 2)
    vd = swapped(after(vx, vy), *Y)
    o1 = swapped(after(h1, vx, vy), *X)
    r2 = swapped(after(jnp.where(x_side == 0, sent, h2), o1), *X)
    zs = (0, 2, 1, 3)
    unit0 = with_cores([(v, zs, 0, 0), (vx, zs, 1, 0), (vy, zs, 0, 1), (vd, zs, 1, 1)])
    return (h1, h2, o1, r2), unit0, second


def local(
    activations,
    cotangent,
    segment_ids,
    prefix_embed,
    adapt_in,
    adapt_in_bias,
    adapt_out,
    adapt_out_bias,
    ln1_gain,
    ln1_bias,
    qkv_weight,
    qkv_bias,
    out_weight,
    out_bias,
    ln2_gain,
    ln2_bias,
    fc_weight,
    fc_bias,
    proj_weight,
    proj_bias,
):
    batches, rows_dev, tok_dev, width = activations.shape
    tokens = batches * rows_dev * tok_dev
    assert tok_dev == 128 and rows_dev == 1 and lax.axis_size("seq") % 2 == 0
    row_me, seq_me = lax.axis_index("row"), lax.axis_index("seq")
    x_side = seq_me % 2

    def flat(vector):
        return vector.reshape(1, -1)

    x = activations.reshape(tokens, width)
    cot = cotangent.reshape(tokens, width)

    ids = (segment_ids.reshape(1, tokens) + 1).astype(BF)
    ids = jnp.pad(ids, ((0, 7), (0, width - tokens)))
    sent = first_norm_call(x, ids, flat(ln1_gain), flat(ln1_bias))

    if (lax.axis_size("row"), lax.axis_size("seq")) == (4, 8):
        (h1, h2, o1, r2), unit0, second = gathered_by_swaps(
            sent, x_side, qkv_weight, out_weight, fc_weight, proj_weight
        )
        me = jnp.stack([row_me, seq_me]).astype(jnp.int32)
    else:
        (h1, h2, o1, r2), unit0, second = gathered_plainly(
            sent, x_side, qkv_weight, out_weight, fc_weight, proj_weight
        )
        me = jnp.zeros((2,), jnp.int32)
    unit1, zero = [(second, NATURAL)], jnp.zeros((2,), jnp.int32)

    seg = jnp.stack([part[tokens, :tokens] for part in (sent, o1, h1, r2, h2)])
    seg = seg.astype(F32).reshape(5, batches, tok_dev).transpose(1, 0, 2)

    squashed, prefix_low = prefix_call(
        prefix_embed, adapt_in, flat(adapt_in_bias), adapt_out, flat(adapt_out_bias)
    )
    mixed, w_nat = qkv_call(me, (sent, o1, h1, r2, h2), unit0, flat(qkv_bias), tokens)
    att, probs = attend_call(seg, mixed, prefix_low, batches, tokens)
    middle, normed2, out_nat = middle_call(
        me, att, x, unit0, flat(out_bias), flat(ln2_gain), flat(ln2_bias)
    )
    hidden, grad_mid, grad_att = mlp_call(
        zero, normed2, cot, middle, flat(ln2_gain), flat(fc_bias), out_nat, unit1
    )

    pre_kv = prefix_part_call(mixed, prefix_low, probs, grad_att, att)
    steps = sum_steps(pre_kv)

    def back(batch, incoming):
        return attend_back_call(batch, mixed, prefix_low, probs, incoming, att, w_nat)

    def to_far(far, other):
        return (far.astype(F32) + jnp.where(x_side == 1, other[1], 0).astype(F32)).astype(BF)

    def to_near(near, other, passing):
        total = near.astype(F32) + other[0].astype(F32) + passing.astype(F32)
        return total.astype(BF)

    side0, near0, far0, own0 = back(0, grad_att)
    other0 = swapped(side0, *X)
    side1, near1, far1, own1 = back(1, after(grad_att, own0, steps[0]))
    other1 = swapped(side1, *X)
    passing0 = moved(to_far(far0, other0), "seq", -2)
    side2, near2, far2, own2 = back(2, after(grad_att, own1, steps[1]))
    other2 = swapped(side2, *X)
    landed0 = moved(to_near(near0, other0, passing0), "seq", -2)
    passing1 = moved(to_far(far1, other1), "seq", -2)
    grad_own = own_back_call(after(cat(own0, own1, own2), other0, steps[2]), w_nat)
    landed1 = moved(to_near(near1, other1, passing1), "seq", -2)
    passing2 = moved(to_far(far2, other2), "seq", -2)
    output = output_call(
        zero, after(hidden, grad_own, steps[3], passing0), middle, flat(proj_bias), unit1
    )
    landed2 = moved(to_near(near2, other2, passing2), "seq", -2)
    prefix_grad, adapt_in_grad, in_bias_grad, adapt_out_grad, out_bias_grad = prefix_back_call(
        after(steps[-1], output), squashed, prefix_embed, adapt_in, adapt_out
    )
    arrived = []
    for landed, other in ((landed0, other0), (landed1, other1), (landed2, other2)):
        arrived += [landed, jnp.where(x_side == 0, other[1], 0)]
    in_grad = first_back_call(x, grad_own, grad_mid, flat(ln1_gain), arrived)
    shape = activations.shape
    return (
        output.reshape(shape),
        in_grad.reshape(shape),
        prefix_grad,
        adapt_in_grad,
        in_bias_grad.reshape(-1),
        adapt_out_grad,
        out_bias_grad.reshape(-1),
    )


def solution(mesh):
    rows = P(None, "row", "seq", None)
    split = P("row", "seq")
    placed = (
        rows,
        rows,
        P(None, "row", "seq"),
        P(),
        P(),
        P(),
        P(),
        P(),
        P(),
        P(),
        split,
        P(),
        split,
        P(),
        P(),
        P(),
        split,
        P(),
        split,
        P(),
    )
    return jax.shard_map(
        local,
        mesh=mesh,
        in_specs=placed,
        out_specs=(rows, rows, P(), P(), P(), P(), P()),
        check_vma=False,
    )
```

```python
import functools

import jax
import jax.numpy as jnp
from jax import lax
from jax.experimental import pallas as pl
from jax.experimental.pallas import tpu as pltpu
from jax.sharding import PartitionSpec as P

EPS = 1e-05
MASKED = -1e30
PREFIX_ROWS = 16
BF = jnp.bfloat16
F32 = jnp.float32
MIB = 1 << 20
HIGHEST = lax.Precision.HIGHEST
VMEM = pltpu.VMEM
ANYWHERE = pl.BlockSpec(memory_space=pl.ANY)
SCALARS = pl.BlockSpec(memory_space=pltpu.SMEM)


def mm(left, right, precision=None):
    return jnp.dot(left, right, precision=precision, preferred_element_type=F32)


def mm_nt(left, right, precision=None):
    return lax.dot_general(
        left, right, (((1,), (1,)), ((), ())), precision=precision, preferred_element_type=F32
    )


def mm_tn(left, right, precision=None):
    return lax.dot_general(
        left, right, (((0,), (0,)), ((), ())), precision=precision, preferred_element_type=F32
    )


def cat(*parts):
    return jnp.concatenate(parts, axis=0)


X, ZN, ZF, CORE, Y = ("seq", 1), ("seq", 2), ("seq", 4), ("row", 1), ("row", 2)


def swapped(value, axis, bit):
    count = lax.axis_size(axis)
    return lax.ppermute(value, axis, [(i, i ^ bit) for i in range(count)])


def moved(value, axis, steps):
    count = lax.axis_size(axis)
    low, high = max(0, -steps), min(count, count - steps)
    return lax.ppermute(value, axis, [(i, i + steps) for i in range(low, high)])


def after(value, *others):
    return lax.optimization_barrier((value,) + others)[0]


NATURAL = tuple((r, s) for r in range(4) for s in range(8))


def with_cores(parts):
    out = []
    for array, zs, x, y in parts:
        out.append((array, tuple((2 * y, 2 * z + x) for z in zs)))
        out.append((swapped(array, *CORE), tuple((2 * y + 1, 2 * z + x) for z in zs)))
    return out


def norm_parts(values):
    centre = values - jnp.mean(values, axis=-1, keepdims=True)
    spread = jnp.mean(centre * centre, axis=-1, keepdims=True)
    scale = lax.rsqrt(spread + EPS)
    return centre * scale, scale


def norm_back(values, incoming, gain):
    normal, scale = norm_parts(values)
    e = incoming * gain
    return scale * (
        e
        - jnp.mean(e, axis=-1, keepdims=True)
        - normal * jnp.mean(e * normal, axis=-1, keepdims=True)
    )


def call_params(limit):
    return pltpu.CompilerParams(vmem_limit_bytes=limit * MIB)


def lasting(micros):
    return pl.CostEstimate(
        flops=int(micros * 1e9), bytes_accessed=int(micros * 1e6), transcendentals=0
    )


def whole(shape):
    return pl.BlockSpec(shape, lambda *_: (0,) * len(shape))


def lanes(start, size=128):
    if isinstance(start, int):
        return pl.ds(start, size)
    return pl.ds(pl.multiple_of(start, 128), size)


def each_piece(me, arrays, spots):
    for array, slots in zip(arrays, spots):
        for slot, (row_bits, seq_bits) in enumerate(slots):
            yield array, slot, me[0] ^ row_bits, me[1] ^ seq_bits


def first_norm_kernel(x, ids, gain, shift, sent):
    tokens = x.shape[0]
    normal, _ = norm_parts(x[...].astype(F32))
    sent[:tokens, :] = (normal * gain[...].astype(F32) + shift[...].astype(F32)).astype(BF)
    sent[tokens:, :] = ids[...]


def first_norm_call(x, ids, gain, shift):
    tokens, width = x.shape
    return pl.pallas_call(
        first_norm_kernel,
        out_shape=jax.ShapeDtypeStruct((tokens + 8, width), BF),
        compiler_params=call_params(16),
        cost_estimate=lasting(1),
        name="first_norm",
    )(x, ids, gain, shift)


def packed_kernel(fc_weight, proj_weight, out_weight, packed):
    packed[:, :512] = fc_weight[...]
    for j in range(4):
        packed[:, 512 + 128 * j : 640 + 128 * j] = proj_weight[256 * j : 256 * (j + 1), :]
    packed[:, 1024:] = out_weight[...]


def packed_call(fc_weight, proj_weight, out_weight):
    return pl.pallas_call(
        packed_kernel,
        out_shape=jax.ShapeDtypeStruct((256, 1152), BF),
        compiler_params=call_params(16),
        cost_estimate=lasting(1),
        name="packed",
    )(fc_weight, proj_weight, out_weight)


def prefix_kernel(embed, w_in, b_in, w_out, b_out, squashed, low):
    inner = jnp.tanh(mm(embed[...], w_in[...], HIGHEST) + b_in[...])
    squashed[...] = inner
    pairs = mm(inner, w_out[...], HIGHEST) + b_out[...]
    pairs = cat(pairs, jnp.zeros((PREFIX_ROWS - pairs.shape[0], pairs.shape[1]), F32)).astype(BF)
    for p in range(low.shape[0]):
        low[p] = pairs[:, 128 * p : 128 * (p + 1)]


def prefix_call(embed, w_in, b_in, w_out, b_out):
    return pl.pallas_call(
        prefix_kernel,
        out_shape=[
            jax.ShapeDtypeStruct((embed.shape[0], w_in.shape[1]), F32),
            jax.ShapeDtypeStruct((w_out.shape[1] // 128, PREFIX_ROWS, 128), BF),
        ],
        compiler_params=call_params(24),
        cost_estimate=lasting(1),
        name="prefix",
    )(embed, w_in, b_in, w_out, b_out)


def prefix_back_kernel(
    count, total, squashed, embed, w_in, w_out, prefix_grad, in_grad, in_bias, out_grad, out_bias
):
    summed = jnp.sum(total[...], axis=0)
    grad_kv = jnp.concatenate([summed[count * p : count * (p + 1)] for p in range(16)], axis=1)
    inner = squashed[...]
    out_bias[...] = jnp.sum(grad_kv, axis=0, keepdims=True)
    low_kv = grad_kv.astype(BF)
    out_grad[...] = mm_tn(inner.astype(BF), low_kv)
    grad_z = mm_nt(w_out[...].astype(BF), low_kv).T * (1.0 - inner * inner)
    in_bias[...] = jnp.sum(grad_z, axis=0, keepdims=True)
    low_z = grad_z.astype(BF)
    in_grad[...] = mm_tn(embed[...].astype(BF), low_z)
    prefix_grad[...] = mm_nt(w_in[...].astype(BF), low_z).T


def prefix_back_call(total, squashed, embed, w_in, w_out):
    count, width = embed.shape
    hidden = w_in.shape[1]
    return pl.pallas_call(
        functools.partial(prefix_back_kernel, count),
        out_shape=[
            jax.ShapeDtypeStruct((count, width), F32),
            jax.ShapeDtypeStruct((width, hidden), F32),
            jax.ShapeDtypeStruct((1, hidden), F32),
            jax.ShapeDtypeStruct((hidden, 2 * width), F32),
            jax.ShapeDtypeStruct((1, 2 * width), F32),
        ],
        compiler_params=call_params(40),
        cost_estimate=lasting(1),
        name="prefix_back",
    )(total, squashed, embed, w_in, w_out)


def qkv_kernel(spots, me, own, o1, h1, r2, h2, bias, *refs):
    arrays = refs[: len(spots)]
    mixed, natural, wide, sems = refs[len(spots) :]
    step = pl.program_id(0)
    tokens = mixed.shape[2]

    @pl.when(step == 0)
    def _():
        for array, slot, r, s in each_piece(me, arrays, spots):
            pltpu.make_async_copy(
                array.at[slot],
                wide.at[
                    s // 2,
                    pl.ds(pl.multiple_of(r * 256, 256), 256),
                    pl.ds(pl.multiple_of((s % 2) * 384, 128), 384),
                ],
                sems.at[s // 2],
            ).start()

    pltpu.make_async_copy(wide.at[step], wide.at[step], sems.at[step]).wait()
    natural[...] = wide[step]

    def one(slot, block):
        value = (mm(block, wide[step]) + bias[...].astype(F32)).astype(BF)
        for col in range(6):
            mixed[col, slot] = value[:, 128 * col : 128 * (col + 1)]

    one(0, own[:tokens, :])

    @pl.when(step >= 1)
    def _():
        for slot, ref in enumerate((o1, h1, r2, h2)):
            one(slot + 1, ref[:tokens, :])


def qkv_call(me, blocks, parts, bias, tokens):
    spots = tuple(part[1] for part in parts)
    return pl.pallas_call(
        functools.partial(qkv_kernel, spots),
        grid=(4,),
        in_specs=[SCALARS]
        + [whole(block.shape) for block in blocks]
        + [pl.BlockSpec((1, 768), lambda s: (0, s))]
        + [ANYWHERE] * len(spots),
        out_specs=[
            pl.BlockSpec((6, 5, tokens, 128), lambda s: (s, 0, 0, 0)),
            pl.BlockSpec((1024, 768), lambda s: (0, s)),
        ],
        out_shape=[
            jax.ShapeDtypeStruct((24, 5, tokens, 128), BF),
            jax.ShapeDtypeStruct((1024, 3072), BF),
        ],
        scratch_shapes=[VMEM((4, 1024, 768), BF), pltpu.SemaphoreType.DMA((4,))],
        compiler_params=call_params(40),
        cost_estimate=lasting(1),
        name="qkv",
    )(me, *blocks, bias, *[part[0] for part in parts])


def allowed_bias(seg, out):
    query = jnp.broadcast_to(seg[0:1, :], (128, 128))
    key_at = lax.broadcasted_iota(jnp.int32, (128, 128), 0)
    query_at = lax.broadcasted_iota(jnp.int32, (128, 128), 1)
    prefix_at = lax.broadcasted_iota(jnp.int32, (PREFIX_ROWS, 256), 0)
    out[0:PREFIX_ROWS, :] = jnp.where(prefix_at < 10, 0.0, MASKED)
    for slot in range(5):
        key = jnp.broadcast_to(seg[slot : slot + 1, :], (128, 128)).T
        allowed = key == query
        if slot == 0:
            allowed = allowed & (key_at <= query_at)
        value = jnp.where(allowed, 0.0, MASKED)
        rows = slice(PREFIX_ROWS + 128 * slot, PREFIX_ROWS + 128 * (slot + 1))
        out[rows, :128] = value
        out[rows, 128:] = value


def two_heads(block):
    lane = lax.broadcasted_iota(jnp.int32, block.shape, 1)
    zero = jnp.zeros_like(block)
    return cat(jnp.where(lane < 64, block, zero), jnp.where(lane < 64, zero, block))


def heads_merged(both):
    feature = lax.broadcasted_iota(jnp.int32, (128, 128), 0)
    return jnp.where(feature < 64, both[:, :128], both[:, 128:]).T


KEYS = PREFIX_ROWS + 5 * 128


def attend_kernel(seg, q, k, v, pk, pv, att, probs, bias):
    allowed_bias(seg[0], bias)
    for p in range(8):
        keys = cat(pk[p], *[k[p, slot] for slot in range(5)])
        values = cat(pv[p], *[v[p, slot] for slot in range(5)])
        scores = mm_nt(keys, two_heads(q[p, 0] * 0.125)) + bias[...]
        top = jnp.max(scores, axis=0, keepdims=True)
        expo = jnp.exp(scores - top)
        total = jnp.sum(expo, axis=0, keepdims=True)
        chance = (expo * (1.0 / total)).astype(BF)
        probs[0, p] = chance
        att[:, lanes(p * 128)] = heads_merged(mm_tn(values, chance)).astype(BF)


def attend_call(seg, mixed, prefix_low, batches, tokens):
    return pl.pallas_call(
        attend_kernel,
        grid=(batches,),
        in_specs=[
            pl.BlockSpec((1, 5, 128), lambda b: (b, 0, 0)),
            pl.BlockSpec((8, 1, 128, 128), lambda b: (0, 0, b, 0)),
            pl.BlockSpec((8, 5, 128, 128), lambda b: (1, 0, b, 0)),
            pl.BlockSpec((8, 5, 128, 128), lambda b: (2, 0, b, 0)),
            pl.BlockSpec((8, PREFIX_ROWS, 128), lambda b: (0, 0, 0)),
            pl.BlockSpec((8, PREFIX_ROWS, 128), lambda b: (1, 0, 0)),
        ],
        out_specs=[
            pl.BlockSpec((128, 1024), lambda b: (b, 0)),
            pl.BlockSpec((1, 8, KEYS, 256), lambda b: (b, 0, 0, 0)),
        ],
        out_shape=[
            jax.ShapeDtypeStruct((tokens, 1024), BF),
            jax.ShapeDtypeStruct((batches, 8, KEYS, 256), BF),
        ],
        scratch_shapes=[VMEM((KEYS, 256), F32)],
        compiler_params=call_params(48),
        cost_estimate=lasting(1),
        name="attend",
    )(seg, mixed, mixed, mixed, prefix_low, prefix_low)


def fc_copy(second, fc, sems, s):
    return pltpu.make_async_copy(second.at[:, s, :, pl.ds(0, 512)], fc.at[s], sems.at[s])


def proj_copy(second, proj, sems, r):
    return pltpu.make_async_copy(second.at[r, :, :, pl.ds(512, 512)], proj.at[r], sems.at[r])


def proj_rows(proj, r, j):
    return jnp.concatenate([proj[r, s, :, 128 * j : 128 * (j + 1)] for s in range(8)], axis=1)


def out_matrix(out):
    return jnp.concatenate([out[:, s].reshape(1024, 128) for s in range(8)], axis=1)


def mlp_kernel(
    att,
    x,
    cot,
    gain,
    shift,
    out_bias,
    fc_bias,
    second,
    hidden_far,
    middle,
    grad_mid,
    grad_att,
    hidden,
    slope,
    proj,
    fc,
    out,
    normed,
    total,
    fc_sems,
    proj_sems,
    sems,
):
    out_in = pltpu.make_async_copy(second.at[:, :, :, pl.ds(1024, 128)], out, sems.at[0])
    out_in.start()
    for s in range(3):
        fc_copy(second, fc, fc_sems, s).start()
    out_in.wait()
    value = x[...].astype(F32) + mm(att[...], out_matrix(out)) + out_bias[...].astype(F32)
    middle[...] = value
    normal, _ = norm_parts(value)
    normed[...] = (normal * gain[...].astype(F32) + shift[...].astype(F32)).astype(BF)
    for s in range(8):
        fc_copy(second, fc, fc_sems, s).wait()
        if s < 5:
            fc_copy(second, fc, fc_sems, s + 3).start()
        else:
            proj_copy(second, proj, proj_sems, s - 5).start()
        cols = pl.ds(512 * s, 512)
        v = mm(normed[...], fc[s].reshape(1024, 512)) + fc_bias[:, cols].astype(F32)
        cubic = (0.7978845608028654 * 0.044715) * (v * v)
        t = jnp.tanh(v * (cubic + 0.7978845608028654))
        half = 0.5 * t + 0.5
        hidden[:, cols] = (v * half).astype(BF)
        slope[:, cols] = (
            half + v * (half - half * half) * (6.0 * cubic + 2 * 0.7978845608028654)
        ).astype(BF)
    proj_copy(second, proj, proj_sems, 3).start()
    kept = pltpu.make_async_copy(hidden, hidden_far, sems.at[1])
    kept.start()
    for r in range(4):
        proj_copy(second, proj, proj_sems, r).wait()
        for half_row in range(2):
            s = 2 * r + half_row
            grad_pre = []
            for j in (2 * half_row, 2 * half_row + 1):
                back = mm_nt(cot[...], proj_rows(proj, r, j))
                cols = pl.ds(1024 * r + 256 * j, 256)
                grad_pre.append((back * slope[:, cols].astype(F32)).astype(BF))
            part = mm_nt(jnp.concatenate(grad_pre, axis=1), fc[s].reshape(1024, 512))
            if s == 0:
                total[...] = part
            else:
                total[...] += part
    value = cot[...].astype(F32) + norm_back(middle[...], total[...], gain[...].astype(F32))
    grad_mid[...] = value
    grad_att[...] = mm_nt(value.astype(BF), out_matrix(out)).astype(BF)
    kept.wait()


def mlp_call(att, x, cot, gain, shift, out_bias, fc_bias, second):
    tokens = cot.shape[0]
    return pl.pallas_call(
        mlp_kernel,
        grid=(1,),
        in_specs=[whole((tokens, 1024))] * 3
        + [whole((1, 1024))] * 3
        + [whole((1, 4096)), ANYWHERE],
        out_specs=[ANYWHERE] + [whole((tokens, 1024))] * 3,
        out_shape=[
            jax.ShapeDtypeStruct((tokens, 4096), BF),
            jax.ShapeDtypeStruct((tokens, 1024), F32),
            jax.ShapeDtypeStruct((tokens, 1024), F32),
            jax.ShapeDtypeStruct((tokens, 1024), BF),
        ],
        scratch_shapes=[
            VMEM((tokens, 4096), BF),
            VMEM((tokens, 4096), BF),
            VMEM((4, 8, 256, 512), BF),
            VMEM((8, 4, 256, 512), BF),
            VMEM((4, 8, 256, 128), BF),
            VMEM((tokens, 1024), BF),
            VMEM((tokens, 1024), F32),
            pltpu.SemaphoreType.DMA((8,)),
            pltpu.SemaphoreType.DMA((4,)),
            pltpu.SemaphoreType.DMA((2,)),
        ],
        compiler_params=call_params(52),
        cost_estimate=lasting(1),
        name="mlp",
    )(att, x, cot, gain, shift, out_bias, fc_bias, second)


def output_kernel(hidden, middle, proj_bias, second, output, proj, total, sems):
    for r in range(4):
        proj_copy(second, proj, sems, r).start()
    total[...] = middle[...] + proj_bias[...].astype(F32)
    for r in range(4):
        proj_copy(second, proj, sems, r).wait()
        rows = jnp.concatenate([proj_rows(proj, r, j) for j in range(4)], axis=0)
        total[...] += mm(hidden[:, pl.ds(1024 * r, 1024)], rows)
    output[...] = total[...].astype(BF)


def output_call(hidden, middle, proj_bias, second):
    tokens = hidden.shape[0]
    return pl.pallas_call(
        output_kernel,
        grid=(1,),
        in_specs=[whole((tokens, 4096)), whole((tokens, 1024)), whole((1, 1024)), ANYWHERE],
        out_specs=whole((tokens, 1024)),
        out_shape=jax.ShapeDtypeStruct((tokens, 1024), BF),
        scratch_shapes=[
            VMEM((4, 8, 256, 512), BF),
            VMEM((tokens, 1024), F32),
            pltpu.SemaphoreType.DMA((4,)),
        ],
        compiler_params=call_params(48),
        cost_estimate=lasting(1),
        name="output",
    )(hidden, middle, proj_bias, second)


def row_deltas(grad_att, att):
    width = grad_att.shape[1]
    rows = max(8, width // 64)
    head = lax.broadcasted_iota(jnp.int32, (rows, width), 0)
    lane = lax.broadcasted_iota(jnp.int32, (rows, width), 1)
    pick = jnp.where(lane // 64 == head, 1.0, 0.0).astype(BF)
    product = grad_att.astype(F32) * att.astype(F32)
    high = product.astype(BF)
    return mm_nt(pick, high) + mm_nt(pick, (product - high.astype(F32)).astype(BF))


def both_heads(delta, p):
    return jnp.concatenate([delta[2 * p : 2 * p + 1, :], delta[2 * p + 1 : 2 * p + 2, :]], axis=1)


def prefix_part_kernel(count, q, pv, probs, grad_att, att, grad_pre_kv):
    batches = probs.shape[0]
    delta = row_deltas(grad_att[...], att[...])
    key = lax.broadcasted_iota(jnp.int32, (2 * PREFIX_ROWS, 128), 0)
    lane = lax.broadcasted_iota(jnp.int32, (2 * PREFIX_ROWS, 128), 1)
    mine = (lane < 64) == (key < PREFIX_ROWS)
    for p in range(8):
        cols = slice(128 * p, 128 * (p + 1))
        grad_o = grad_att[:, cols]
        values = jnp.where(mine, cat(pv[p], pv[p]), jnp.zeros((), BF))
        grad_probs = mm_nt(values, grad_o)
        head = lax.broadcasted_iota(jnp.int32, grad_probs.shape, 0) < PREFIX_ROWS
        row_delta = jnp.where(head, delta[2 * p : 2 * p + 1, :], delta[2 * p + 1 : 2 * p + 2, :])
        chance = jnp.concatenate(
            [cat(probs[b, p, :, :128], probs[b, p, :, 128:]) for b in range(batches)], axis=1
        )
        grad_scores = (chance.astype(F32) * (grad_probs - row_delta)).astype(BF)
        grad_k = jnp.where(mine, mm(grad_scores, q[p, 0] * 0.125), 0.0)
        grad_v = jnp.where(mine, mm(chance, grad_o), 0.0)
        grad_pre_kv[count * p : count * (p + 1), :] = (
            grad_k[:PREFIX_ROWS] + grad_k[PREFIX_ROWS:]
        )[:count]
        grad_pre_kv[count * (p + 8) : count * (p + 9), :] = (
            grad_v[:PREFIX_ROWS] + grad_v[PREFIX_ROWS:]
        )[:count]


def prefix_part_call(count, mixed, prefix_low, probs, grad_att, att):
    batches, tokens = probs.shape[0], att.shape[0]
    return pl.pallas_call(
        functools.partial(prefix_part_kernel, count),
        grid=(1,),
        in_specs=[
            pl.BlockSpec((8, 1, tokens, 128), lambda b: (0, 0, 0, 0)),
            pl.BlockSpec((8, PREFIX_ROWS, 128), lambda b: (1, 0, 0)),
            pl.BlockSpec((batches, 8, PREFIX_ROWS, 256), lambda b: (0, 0, 0, 0)),
            whole((tokens, 1024)),
            whole((tokens, 1024)),
        ],
        out_specs=whole((16 * count, 128)),
        out_shape=jax.ShapeDtypeStruct((16 * count, 128), F32),
        compiler_params=call_params(48),
        cost_estimate=lasting(1),
        name="prefix_part",
    )(mixed, prefix_low, probs, grad_att, att)


def attend_back_kernel(
    q, k, v, pk, pv, probs, grad_att, att, w_nat, side, near, far, own, dkv, w_kv, sem
):
    step = pl.program_id(0)
    weights = pltpu.make_async_copy(w_nat.at[:, pl.ds(1024, 2048)], w_kv, sem)

    @pl.when(step == 0)
    def _():
        weights.start()

    delta = row_deltas(grad_att[...], att[...])
    for i in range(2):
        p = step * 2 + i
        keys = cat(pk[i], *[k[i, slot] for slot in range(5)])
        values = cat(pv[i], *[v[i, slot] for slot in range(5)])
        queries = two_heads(q[i, 0] * 0.125)
        grad_two = two_heads(grad_att[:, 128 * i : 128 * (i + 1)])
        row_delta = both_heads(delta, i)
        chance = probs[0, i]
        grad_probs = mm_nt(values, grad_two)
        grad_scores = (chance.astype(F32) * (grad_probs - row_delta)).astype(BF)
        grad_k = mm(grad_scores, queries)
        grad_v = mm(chance, grad_two)
        grad_q = heads_merged(mm_tn(keys, grad_scores)) * 0.125
        own[:, lanes(p * 128)] = grad_q.astype(BF)
        for slot in range(5):
            rows = slice(PREFIX_ROWS + 128 * slot, PREFIX_ROWS + 128 * (slot + 1))
            if slot == 0:
                own[:, lanes(p * 128 + 1024)] = grad_k[rows].astype(BF)
                own[:, lanes(p * 128 + 2048)] = grad_v[rows].astype(BF)
            else:
                sent = slice(128 * (slot - 1), 128 * slot)
                dkv[sent, lanes(p * 128)] = grad_k[rows].astype(BF)
                dkv[sent, lanes(p * 128 + 1024)] = grad_v[rows].astype(BF)

    @pl.when(step == 3)
    def _():
        weights.wait()
        part = mm_nt(dkv[...], w_kv[...]).astype(BF)
        side[0] = part[:128]
        near[...] = part[128:256]
        side[1] = part[256:384]
        far[...] = part[384:]


def attend_back_call(batch, mixed, prefix_low, probs, grad_att, att, w_nat):
    return pl.pallas_call(
        attend_back_kernel,
        grid=(4,),
        in_specs=[
            pl.BlockSpec((2, 1, 128, 128), lambda i: (i, 0, batch, 0)),
            pl.BlockSpec((2, 5, 128, 128), lambda i: (4 + i, 0, batch, 0)),
            pl.BlockSpec((2, 5, 128, 128), lambda i: (8 + i, 0, batch, 0)),
            pl.BlockSpec((2, PREFIX_ROWS, 128), lambda i: (i, 0, 0)),
            pl.BlockSpec((2, PREFIX_ROWS, 128), lambda i: (4 + i, 0, 0)),
            pl.BlockSpec((1, 2, KEYS, 256), lambda i: (batch, i, 0, 0)),
            pl.BlockSpec((128, 256), lambda i: (batch, i)),
            pl.BlockSpec((128, 256), lambda i: (batch, i)),
            ANYWHERE,
        ],
        out_specs=[
            whole((2, 128, 1024)),
            whole((128, 1024)),
            whole((128, 1024)),
            whole((128, 3072)),
        ],
        out_shape=[
            jax.ShapeDtypeStruct((2, 128, 1024), BF),
            jax.ShapeDtypeStruct((128, 1024), BF),
            jax.ShapeDtypeStruct((128, 1024), BF),
            jax.ShapeDtypeStruct((128, 3072), BF),
        ],
        scratch_shapes=[VMEM((512, 2048), BF), VMEM((1024, 2048), BF), pltpu.SemaphoreType.DMA],
        compiler_params=call_params(48),
        cost_estimate=lasting(1),
        name="attend_back",
    )(mixed, mixed, mixed, prefix_low, prefix_low, probs, grad_att, att, w_nat)


def own_back_kernel(own, w_nat, result):
    result[...] = mm_nt(own[...], w_nat[...])


def own_back_call(own, w_nat):
    tokens = own.shape[0]
    return pl.pallas_call(
        own_back_kernel,
        grid=(4,),
        in_specs=[whole((tokens, 3072)), pl.BlockSpec((256, 3072), lambda i: (i, 0))],
        out_specs=pl.BlockSpec((tokens, 256), lambda i: (0, i)),
        out_shape=jax.ShapeDtypeStruct((tokens, 1024), F32),
        compiler_params=call_params(48),
        cost_estimate=lasting(1),
        name="own_back",
    )(own, w_nat)


def first_back_kernel(x, grad_own, grad_mid, gain, *refs):
    arrived, in_grad = refs[:-1], refs[-1]
    for batch, parts in enumerate(zip(arrived[0::2], arrived[1::2])):
        rows = slice(128 * batch, 128 * (batch + 1))
        incoming = grad_own[rows, :] + parts[0][...].astype(F32) + parts[1][...].astype(F32)
        back = norm_back(x[rows, :].astype(F32), incoming, gain[...].astype(F32))
        in_grad[rows, :] = (grad_mid[rows, :] + back).astype(BF)


def first_back_call(x, grad_own, grad_mid, gain, arrived):
    return pl.pallas_call(
        first_back_kernel,
        out_shape=jax.ShapeDtypeStruct(x.shape, BF),
        compiler_params=call_params(24),
        cost_estimate=lasting(1),
        name="first_back",
    )(x, grad_own, grad_mid, gain, *arrived)


def full(shard):
    rows = lax.all_gather(shard, "row", axis=0, tiled=True)
    return lax.all_gather(rows, "seq", axis=1, tiled=True)


def pieces(matrix):
    rows, cols = matrix.shape
    return (
        matrix.reshape(4, rows // 4, 8, cols // 8)
        .transpose(0, 2, 1, 3)
        .reshape(32, rows // 4, cols // 8)
    )


def side_by_side(fc_weight, proj_weight, out_weight):
    quarter = proj_weight.shape[-2] // 4
    proj = [proj_weight[..., quarter * j : quarter * (j + 1), :] for j in range(4)]
    return jnp.concatenate([fc_weight, *proj, out_weight], axis=-1)


def gathered_plainly(sent, x_side, qkv_weight, out_weight, fc_weight, proj_weight):
    second = side_by_side(*[pieces(full(w)) for w in (fc_weight, proj_weight, out_weight)])
    h1 = moved(sent, "seq", 2)
    h2 = moved(h1, "seq", 2)
    o1 = swapped(h1, *X)
    r2 = swapped(jnp.where(x_side == 0, sent, h2), *X)
    return (h1, h2, o1, r2), [(pieces(full(qkv_weight)), NATURAL)], second


def gathered_by_swaps(sent, x_side, qkv_weight, out_weight, fc_weight, proj_weight):
    second = lax.all_gather(
        packed_call(fc_weight, proj_weight, out_weight), ("row", "seq"), axis=0
    )
    first = qkv_weight[None]
    v0 = cat(first, swapped(first, *ZF))
    g0 = swapped(v0, *ZN)
    h1 = moved(after(sent, v0), "seq", 2)
    v = cat(v0, g0)
    vx, vy = swapped(v, *X), swapped(v, *Y)
    h2 = moved(after(h1, g0), "seq", 2)
    vd = swapped(after(vx, vy), *Y)
    o1 = swapped(after(h1, vx, vy), *X)
    r2 = swapped(after(jnp.where(x_side == 0, sent, h2), o1), *X)
    zs = (0, 2, 1, 3)
    unit0 = with_cores([(v, zs, 0, 0), (vx, zs, 1, 0), (vy, zs, 0, 1), (vd, zs, 1, 1)])
    return (h1, h2, o1, r2), unit0, second


def local(
    activations,
    cotangent,
    segment_ids,
    prefix_embed,
    adapt_in,
    adapt_in_bias,
    adapt_out,
    adapt_out_bias,
    ln1_gain,
    ln1_bias,
    qkv_weight,
    qkv_bias,
    out_weight,
    out_bias,
    ln2_gain,
    ln2_bias,
    fc_weight,
    fc_bias,
    proj_weight,
    proj_bias,
):
    batches, rows_dev, tok_dev, width = activations.shape
    tokens = batches * rows_dev * tok_dev
    assert tok_dev == 128 and rows_dev == 1 and lax.axis_size("seq") % 2 == 0
    row_me, seq_me = lax.axis_index("row"), lax.axis_index("seq")
    x_side = seq_me % 2

    def flat(vector):
        return vector.reshape(1, -1)

    x = activations.reshape(tokens, width)
    cot = cotangent.reshape(tokens, width)

    ids = (segment_ids.reshape(1, tokens) + 1).astype(BF)
    ids = jnp.pad(ids, ((0, 7), (0, width - tokens)))
    sent = first_norm_call(x, ids, flat(ln1_gain), flat(ln1_bias))

    if (lax.axis_size("row"), lax.axis_size("seq")) == (4, 8):
        (h1, h2, o1, r2), unit0, second = gathered_by_swaps(
            sent, x_side, qkv_weight, out_weight, fc_weight, proj_weight
        )
        me = jnp.stack([row_me, seq_me]).astype(jnp.int32)
    else:
        (h1, h2, o1, r2), unit0, second = gathered_plainly(
            sent, x_side, qkv_weight, out_weight, fc_weight, proj_weight
        )
        me = jnp.zeros((2,), jnp.int32)
    second = second.reshape(4, 8, 256, 1152)

    seg = jnp.stack([part[tokens, :tokens] for part in (sent, o1, h1, r2, h2)])
    seg = seg.astype(F32).reshape(5, batches, tok_dev).transpose(1, 0, 2)

    squashed, prefix_low = prefix_call(
        prefix_embed, adapt_in, flat(adapt_in_bias), adapt_out, flat(adapt_out_bias)
    )
    mixed, w_nat = qkv_call(me, (sent, o1, h1, r2, h2), unit0, flat(qkv_bias), tokens)
    att, probs = attend_call(seg, mixed, prefix_low, batches, tokens)
    hidden, middle, grad_mid, grad_att = mlp_call(
        att, x, cot, flat(ln2_gain), flat(ln2_bias), flat(out_bias), flat(fc_bias), second
    )

    count = prefix_embed.shape[0]
    pre_kv = prefix_part_call(count, mixed, prefix_low, probs, grad_att, att)
    if (lax.axis_size("row"), lax.axis_size("seq")) == (4, 8):
        total_kv = lax.all_gather(pre_kv, ("row", "seq"), axis=0)
    else:
        total_kv = lax.psum(pre_kv, ("row", "seq"))[None]

    def back(batch, incoming):
        return attend_back_call(batch, mixed, prefix_low, probs, incoming, att, w_nat)

    def to_far(far, other):
        return (far.astype(F32) + jnp.where(x_side == 1, other[1], 0).astype(F32)).astype(BF)

    def to_near(near, other, passing):
        total = near.astype(F32) + other[0].astype(F32) + passing.astype(F32)
        return total.astype(BF)

    side0, near0, far0, own0 = back(0, after(grad_att, pre_kv))
    other0 = swapped(side0, *X)
    side1, near1, far1, own1 = back(1, after(grad_att, own0))
    other1 = swapped(side1, *X)
    to_far0 = to_far(far0, other0)
    passing0 = moved(to_far0, "seq", -2)
    side2, near2, far2, own2 = back(2, after(grad_att, own1, to_far0))
    other2 = swapped(side2, *X)
    to_far1 = to_far(far1, other1)
    passing1 = moved(to_far1, "seq", -2)
    grad_own = own_back_call(after(cat(own0, own1, own2), to_far1), w_nat)
    landed0 = moved(after(to_near(near0, other0, passing0), grad_own), "seq", -2)
    to_far2 = to_far(far2, other2)
    passing2 = moved(to_far2, "seq", -2)
    output = output_call(
        after(hidden, grad_own, passing1, to_far2), middle, flat(proj_bias), second
    )
    landed1 = moved(after(to_near(near1, other1, passing1), output), "seq", -2)
    landed2 = moved(to_near(near2, other2, passing2), "seq", -2)
    prefix_grad, adapt_in_grad, in_bias_grad, adapt_out_grad, out_bias_grad = prefix_back_call(
        after(total_kv, output, passing2), squashed, prefix_embed, adapt_in, adapt_out
    )
    arrived = []
    for landed, other in ((landed0, other0), (landed1, other1), (landed2, other2)):
        arrived += [landed, jnp.where(x_side == 0, other[1], 0)]
    in_grad = first_back_call(after(x, prefix_grad), grad_own, grad_mid, flat(ln1_gain), arrived)
    shape = activations.shape
    return (
        output.reshape(shape),
        in_grad.reshape(shape),
        prefix_grad,
        adapt_in_grad,
        in_bias_grad.reshape(-1),
        adapt_out_grad,
        out_bias_grad.reshape(-1),
    )


def solution(mesh):
    rows = P(None, "row", "seq", None)
    split = P("row", "seq")
    placed = (
        rows,
        rows,
        P(None, "row", "seq"),
        P(),
        P(),
        P(),
        P(),
        P(),
        P(),
        P(),
        split,
        P(),
        split,
        P(),
        P(),
        P(),
        split,
        P(),
        split,
        P(),
    )
    return jax.shard_map(
        local,
        mesh=mesh,
        in_specs=placed,
        out_specs=(rows, rows, P(), P(), P(), P(), P()),
        check_vma=False,
    )
```

```python
import functools

import jax
import jax.numpy as jnp
from jax import lax
from jax.experimental import pallas as pl
from jax.experimental.pallas import tpu as pltpu
from jax.sharding import PartitionSpec as P

EPS = 1e-05
MASKED = -1e30
PREFIX_ROWS = 16
BF = jnp.bfloat16
F32 = jnp.float32
MIB = 1 << 20
HIGHEST = lax.Precision.HIGHEST
VMEM = pltpu.VMEM
ANYWHERE = pl.BlockSpec(memory_space=pl.ANY)
SCALARS = pl.BlockSpec(memory_space=pltpu.SMEM)


def mm(left, right, precision=None):
    return jnp.dot(left, right, precision=precision, preferred_element_type=F32)


def mm_nt(left, right, precision=None):
    return lax.dot_general(
        left, right, (((1,), (1,)), ((), ())), precision=precision, preferred_element_type=F32
    )


def mm_tn(left, right, precision=None):
    return lax.dot_general(
        left, right, (((0,), (0,)), ((), ())), precision=precision, preferred_element_type=F32
    )


def cat(*parts):
    return jnp.concatenate(parts, axis=0)


X, ZN, ZF, CORE, Y = ("seq", 1), ("seq", 2), ("seq", 4), ("row", 1), ("row", 2)


def swapped(value, axis, bit):
    count = lax.axis_size(axis)
    return lax.ppermute(value, axis, [(i, i ^ bit) for i in range(count)])


def moved(value, axis, steps):
    count = lax.axis_size(axis)
    low, high = max(0, -steps), min(count, count - steps)
    return lax.ppermute(value, axis, [(i, i + steps) for i in range(low, high)])


def after(value, *others):
    return lax.optimization_barrier((value,) + others)[0]


NATURAL = tuple((r, s) for r in range(4) for s in range(8))


def with_cores(parts):
    out = []
    for array, zs, x, y in parts:
        out.append((array, tuple((2 * y, 2 * z + x) for z in zs)))
        out.append((swapped(array, *CORE), tuple((2 * y + 1, 2 * z + x) for z in zs)))
    return out


def norm_parts(values):
    centre = values - jnp.mean(values, axis=-1, keepdims=True)
    spread = jnp.mean(centre * centre, axis=-1, keepdims=True)
    scale = lax.rsqrt(spread + EPS)
    return centre * scale, scale


def norm_back(values, incoming, gain):
    normal, scale = norm_parts(values)
    e = incoming * gain
    return scale * (
        e
        - jnp.mean(e, axis=-1, keepdims=True)
        - normal * jnp.mean(e * normal, axis=-1, keepdims=True)
    )


def call_params(limit):
    return pltpu.CompilerParams(vmem_limit_bytes=limit * MIB)


def lasting(micros):
    return pl.CostEstimate(
        flops=int(micros * 1e9), bytes_accessed=int(micros * 1e6), transcendentals=0
    )


def whole(shape):
    return pl.BlockSpec(shape, lambda *_: (0,) * len(shape))


def lanes(start, size=128):
    if isinstance(start, int):
        return pl.ds(start, size)
    return pl.ds(pl.multiple_of(start, 128), size)


def each_piece(me, arrays, spots):
    for array, slots in zip(arrays, spots):
        for slot, (row_bits, seq_bits) in enumerate(slots):
            yield array, slot, me[0] ^ row_bits, me[1] ^ seq_bits


def first_norm_kernel(x, ids, gain, shift, sent):
    tokens = x.shape[0]
    normal, _ = norm_parts(x[...].astype(F32))
    sent[:tokens, :] = (normal * gain[...].astype(F32) + shift[...].astype(F32)).astype(BF)
    sent[tokens:, :] = ids[...]


def first_norm_call(x, ids, gain, shift):
    tokens, width = x.shape
    return pl.pallas_call(
        first_norm_kernel,
        out_shape=jax.ShapeDtypeStruct((tokens + 8, width), BF),
        compiler_params=call_params(16),
        cost_estimate=lasting(1),
        name="first_norm",
    )(x, ids, gain, shift)


def packed_kernel(fc_weight, proj_weight, out_weight, packed):
    packed[:, :512] = fc_weight[...]
    for j in range(4):
        packed[:, 512 + 128 * j : 640 + 128 * j] = proj_weight[256 * j : 256 * (j + 1), :]
    packed[:, 1024:] = out_weight[...]


def packed_call(fc_weight, proj_weight, out_weight):
    return pl.pallas_call(
        packed_kernel,
        out_shape=jax.ShapeDtypeStruct((256, 1152), BF),
        compiler_params=call_params(56),
        cost_estimate=lasting(1),
        name="packed",
    )(fc_weight, proj_weight, out_weight)


def prefix_kernel(embed, w_in, b_in, w_out, b_out, squashed, low):
    inner = jnp.tanh(mm(embed[...], w_in[...], HIGHEST) + b_in[...])
    squashed[...] = inner
    pairs = mm(inner, w_out[...], HIGHEST) + b_out[...]
    pairs = cat(pairs, jnp.zeros((PREFIX_ROWS - pairs.shape[0], pairs.shape[1]), F32)).astype(BF)
    for p in range(low.shape[0]):
        low[p] = pairs[:, 128 * p : 128 * (p + 1)]


def prefix_call(embed, w_in, b_in, w_out, b_out):
    return pl.pallas_call(
        prefix_kernel,
        out_shape=[
            jax.ShapeDtypeStruct((embed.shape[0], w_in.shape[1]), F32),
            jax.ShapeDtypeStruct((w_out.shape[1] // 128, PREFIX_ROWS, 128), BF),
        ],
        compiler_params=call_params(24),
        cost_estimate=lasting(1),
        name="prefix",
    )(embed, w_in, b_in, w_out, b_out)


def prefix_back_kernel(
    total,
    squashed,
    embed,
    w_in_far,
    w_out_far,
    prefix_grad,
    in_grad_far,
    in_bias,
    out_grad_far,
    out_bias,
    w_in,
    w_out,
    in_grad,
    out_grad,
    sems,
):
    count = embed.shape[0]
    w_out_copy = pltpu.make_async_copy(w_out_far, w_out, sems.at[0])
    w_in_copy = pltpu.make_async_copy(w_in_far, w_in, sems.at[1])
    w_out_copy.start()
    w_in_copy.start()
    summed = jnp.sum(total[...], axis=0)
    grad_kv = jnp.concatenate([summed[count * p : count * (p + 1)] for p in range(16)], axis=1)
    inner = squashed[...]
    out_bias[...] = jnp.sum(grad_kv, axis=0, keepdims=True)
    low_kv = grad_kv.astype(BF)
    out_grad[...] = mm_tn(inner.astype(BF), low_kv)
    out_copy = pltpu.make_async_copy(out_grad, out_grad_far, sems.at[2])
    out_copy.start()
    w_out_copy.wait()
    grad_z = mm_nt(w_out[...].astype(BF), low_kv).T * (1.0 - inner * inner)
    in_bias[...] = jnp.sum(grad_z, axis=0, keepdims=True)
    low_z = grad_z.astype(BF)
    in_grad[...] = mm_tn(embed[...].astype(BF), low_z)
    in_copy = pltpu.make_async_copy(in_grad, in_grad_far, sems.at[3])
    in_copy.start()
    w_in_copy.wait()
    prefix_grad[...] = mm_nt(w_in[...].astype(BF), low_z).T
    out_copy.wait()
    in_copy.wait()


def prefix_back_call(total, squashed, embed, w_in, w_out):
    count, width = embed.shape
    hidden = w_in.shape[1]
    return pl.pallas_call(
        prefix_back_kernel,
        grid=(1,),
        in_specs=[
            whole(total.shape),
            whole(squashed.shape),
            whole(embed.shape),
            ANYWHERE,
            ANYWHERE,
        ],
        out_specs=[
            whole((count, width)),
            ANYWHERE,
            whole((1, hidden)),
            ANYWHERE,
            whole((1, 2 * width)),
        ],
        out_shape=[
            jax.ShapeDtypeStruct((count, width), F32),
            jax.ShapeDtypeStruct((width, hidden), F32),
            jax.ShapeDtypeStruct((1, hidden), F32),
            jax.ShapeDtypeStruct((hidden, 2 * width), F32),
            jax.ShapeDtypeStruct((1, 2 * width), F32),
        ],
        scratch_shapes=[
            VMEM((width, hidden), F32),
            VMEM((hidden, 2 * width), F32),
            VMEM((width, hidden), F32),
            VMEM((hidden, 2 * width), F32),
            pltpu.SemaphoreType.DMA((4,)),
        ],
        compiler_params=call_params(56),
        cost_estimate=lasting(1),
        name="prefix_back",
    )(total, squashed, embed, w_in, w_out)


def packed_kernel(fc_weight, proj_weight, out_weight, packed):
    packed[:, :512] = fc_weight[...]
    for j in range(4):
        packed[:, 512 + 128 * j : 640 + 128 * j] = proj_weight[256 * j : 256 * (j + 1), :]
    packed[:, 1024:] = out_weight[...]


def packed_call(fc_weight, proj_weight, out_weight):
    return pl.pallas_call(
        packed_kernel,
        out_shape=jax.ShapeDtypeStruct((256, 1152), BF),
        compiler_params=call_params(56),
        cost_estimate=lasting(1),
        name="packed",
    )(fc_weight, proj_weight, out_weight)


def prefix_kernel(embed, w_in, b_in, w_out, b_out, squashed, low):
    inner = jnp.tanh(mm(embed[...], w_in[...], HIGHEST) + b_in[...])
    squashed[...] = inner
    pairs = mm(inner, w_out[...], HIGHEST) + b_out[...]
    pairs = cat(pairs, jnp.zeros((PREFIX_ROWS - pairs.shape[0], pairs.shape[1]), F32)).astype(BF)
    for p in range(low.shape[0]):
        low[p] = pairs[:, 128 * p : 128 * (p + 1)]


def prefix_call(embed, w_in, b_in, w_out, b_out):
    return pl.pallas_call(
        prefix_kernel,
        out_shape=[
            jax.ShapeDtypeStruct((embed.shape[0], w_in.shape[1]), F32),
            jax.ShapeDtypeStruct((w_out.shape[1] // 128, PREFIX_ROWS, 128), BF),
        ],
        compiler_params=call_params(24),
        cost_estimate=lasting(1),
        name="prefix",
    )(embed, w_in, b_in, w_out, b_out)


def prefix_back_kernel(
    count, total, squashed, embed, w_in, w_out, prefix_grad, in_grad, in_bias, out_grad, out_bias
):
    summed = jnp.sum(total[...], axis=0)
    grad_kv = jnp.concatenate([summed[count * p : count * (p + 1)] for p in range(16)], axis=1)
    inner = squashed[...]
    out_bias[...] = jnp.sum(grad_kv, axis=0, keepdims=True)
    low_kv = grad_kv.astype(BF)
    out_grad[...] = mm_tn(inner.astype(BF), low_kv)
    grad_z = mm_nt(w_out[...].astype(BF), low_kv).T * (1.0 - inner * inner)
    in_bias[...] = jnp.sum(grad_z, axis=0, keepdims=True)
    low_z = grad_z.astype(BF)
    in_grad[...] = mm_tn(embed[...].astype(BF), low_z)
    prefix_grad[...] = mm_nt(w_in[...].astype(BF), low_z).T


def prefix_back_call(total, squashed, embed, w_in, w_out):
    count, width = embed.shape
    hidden = w_in.shape[1]
    return pl.pallas_call(
        functools.partial(prefix_back_kernel, count),
        out_shape=[
            jax.ShapeDtypeStruct((count, width), F32),
            jax.ShapeDtypeStruct((width, hidden), F32),
            jax.ShapeDtypeStruct((1, hidden), F32),
            jax.ShapeDtypeStruct((hidden, 2 * width), F32),
            jax.ShapeDtypeStruct((1, 2 * width), F32),
        ],
        compiler_params=call_params(56),
        cost_estimate=lasting(1),
        name="prefix_back",
    )(total, squashed, embed, w_in, w_out)


def qkv_kernel(spots, me, own, o1, h1, r2, h2, bias, *refs):
    arrays = refs[: len(spots)]
    mixed, natural, wide, sems = refs[len(spots) :]
    step = pl.program_id(0)
    tokens = mixed.shape[2]

    @pl.when(step == 0)
    def _():
        for array, slot, r, s in each_piece(me, arrays, spots):
            pltpu.make_async_copy(
                array.at[slot],
                wide.at[
                    s // 2,
                    pl.ds(pl.multiple_of(r * 256, 256), 256),
                    pl.ds(pl.multiple_of((s % 2) * 384, 128), 384),
                ],
                sems.at[s // 2],
            ).start()

    pltpu.make_async_copy(wide.at[step], wide.at[step], sems.at[step]).wait()
    natural[...] = wide[step]

    def one(slot, block):
        value = (mm(block, wide[step]) + bias[...].astype(F32)).astype(BF)
        for col in range(6):
            mixed[col, slot] = value[:, 128 * col : 128 * (col + 1)]

    one(0, own[:tokens, :])

    @pl.when(step >= 1)
    def _():
        for slot, ref in enumerate((o1, h1, r2, h2)):
            one(slot + 1, ref[:tokens, :])


def qkv_call(me, blocks, parts, bias, tokens):
    spots = tuple(part[1] for part in parts)
    return pl.pallas_call(
        functools.partial(qkv_kernel, spots),
        grid=(4,),
        in_specs=[SCALARS]
        + [whole(block.shape) for block in blocks]
        + [pl.BlockSpec((1, 768), lambda s: (0, s))]
        + [ANYWHERE] * len(spots),
        out_specs=[
            pl.BlockSpec((6, 5, tokens, 128), lambda s: (s, 0, 0, 0)),
            pl.BlockSpec((1024, 768), lambda s: (0, s)),
        ],
        out_shape=[
            jax.ShapeDtypeStruct((24, 5, tokens, 128), BF),
            jax.ShapeDtypeStruct((1024, 3072), BF),
        ],
        scratch_shapes=[VMEM((4, 1024, 768), BF), pltpu.SemaphoreType.DMA((4,))],
        compiler_params=call_params(40),
        cost_estimate=lasting(1),
        name="qkv",
    )(me, *blocks, bias, *[part[0] for part in parts])


def allowed_bias(seg, out):
    query = jnp.broadcast_to(seg[0:1, :], (128, 128))
    key_at = lax.broadcasted_iota(jnp.int32, (128, 128), 0)
    query_at = lax.broadcasted_iota(jnp.int32, (128, 128), 1)
    prefix_at = lax.broadcasted_iota(jnp.int32, (PREFIX_ROWS, 256), 0)
    out[0:PREFIX_ROWS, :] = jnp.where(prefix_at < 10, 0.0, MASKED)
    for slot in range(5):
        key = jnp.broadcast_to(seg[slot : slot + 1, :], (128, 128)).T
        allowed = key == query
        if slot == 0:
            allowed = allowed & (key_at <= query_at)
        value = jnp.where(allowed, 0.0, MASKED)
        rows = slice(PREFIX_ROWS + 128 * slot, PREFIX_ROWS + 128 * (slot + 1))
        out[rows, :128] = value
        out[rows, 128:] = value


def two_heads(block):
    lane = lax.broadcasted_iota(jnp.int32, block.shape, 1)
    zero = jnp.zeros_like(block)
    return cat(jnp.where(lane < 64, block, zero), jnp.where(lane < 64, zero, block))


def heads_merged(both):
    feature = lax.broadcasted_iota(jnp.int32, (128, 128), 0)
    return jnp.where(feature < 64, both[:, :128], both[:, 128:]).T


KEYS = PREFIX_ROWS + 5 * 128


def attend_kernel(seg, q, k, v, pk, pv, att, probs, bias):
    allowed_bias(seg[0], bias)
    for p in range(8):
        keys = cat(pk[p], *[k[p, slot] for slot in range(5)])
        values = cat(pv[p], *[v[p, slot] for slot in range(5)])
        scores = mm_nt(keys, two_heads(q[p, 0] * 0.125)) + bias[...]
        top = jnp.max(scores, axis=0, keepdims=True)
        expo = jnp.exp(scores - top)
        total = jnp.sum(expo, axis=0, keepdims=True)
        chance = (expo * (1.0 / total)).astype(BF)
        probs[0, p] = chance
        att[:, lanes(p * 128)] = heads_merged(mm_tn(values, chance)).astype(BF)


def attend_call(seg, mixed, prefix_low, batches, tokens):
    return pl.pallas_call(
        attend_kernel,
        grid=(batches,),
        in_specs=[
            pl.BlockSpec((1, 5, 128), lambda b: (b, 0, 0)),
            pl.BlockSpec((8, 1, 128, 128), lambda b: (0, 0, b, 0)),
            pl.BlockSpec((8, 5, 128, 128), lambda b: (1, 0, b, 0)),
            pl.BlockSpec((8, 5, 128, 128), lambda b: (2, 0, b, 0)),
            pl.BlockSpec((8, PREFIX_ROWS, 128), lambda b: (0, 0, 0)),
            pl.BlockSpec((8, PREFIX_ROWS, 128), lambda b: (1, 0, 0)),
        ],
        out_specs=[
            pl.BlockSpec((128, 1024), lambda b: (b, 0)),
            pl.BlockSpec((1, 8, KEYS, 256), lambda b: (b, 0, 0, 0)),
        ],
        out_shape=[
            jax.ShapeDtypeStruct((tokens, 1024), BF),
            jax.ShapeDtypeStruct((batches, 8, KEYS, 256), BF),
        ],
        scratch_shapes=[VMEM((KEYS, 256), F32)],
        compiler_params=call_params(48),
        cost_estimate=lasting(1),
        name="attend",
    )(seg, mixed, mixed, mixed, prefix_low, prefix_low)


def fc_copy(second, fc, sems, s):
    return pltpu.make_async_copy(second.at[:, s, :, pl.ds(0, 512)], fc.at[s], sems.at[s])


def proj_copy(second, proj, sems, r):
    return pltpu.make_async_copy(second.at[r, :, :, pl.ds(512, 512)], proj.at[r], sems.at[r])


def proj_rows(proj, r, j):
    return jnp.concatenate([proj[r, s, :, 128 * j : 128 * (j + 1)] for s in range(8)], axis=1)


def out_matrix(out):
    return jnp.concatenate([out[:, s].reshape(1024, 128) for s in range(8)], axis=1)


def row_deltas(grad_att, att):
    width = grad_att.shape[1]
    rows = max(8, width // 64)
    head = lax.broadcasted_iota(jnp.int32, (rows, width), 0)
    lane = lax.broadcasted_iota(jnp.int32, (rows, width), 1)
    pick = jnp.where(lane // 64 == head, 1.0, 0.0).astype(BF)
    product = grad_att.astype(F32) * att.astype(F32)
    high = product.astype(BF)
    return mm_nt(pick, high) + mm_nt(pick, (product - high.astype(F32)).astype(BF))


def both_heads(delta, p):
    return jnp.concatenate([delta[2 * p : 2 * p + 1, :], delta[2 * p + 1 : 2 * p + 2, :]], axis=1)


def prefix_part(q, pv, probs, grad_att, att, grad_pre_kv):
    batches, count = probs.shape[0], grad_pre_kv.shape[0] // 16
    delta = row_deltas(grad_att[...], att[...])
    key = lax.broadcasted_iota(jnp.int32, (2 * PREFIX_ROWS, 128), 0)
    lane = lax.broadcasted_iota(jnp.int32, (2 * PREFIX_ROWS, 128), 1)
    mine = (lane < 64) == (key < PREFIX_ROWS)
    for p in range(8):
        cols = slice(128 * p, 128 * (p + 1))
        grad_o = grad_att[:, cols]
        values = jnp.where(mine, cat(pv[p], pv[p]), jnp.zeros((), BF))
        grad_probs = mm_nt(values, grad_o)
        head = lax.broadcasted_iota(jnp.int32, grad_probs.shape, 0) < PREFIX_ROWS
        row_delta = jnp.where(head, delta[2 * p : 2 * p + 1, :], delta[2 * p + 1 : 2 * p + 2, :])
        chance = jnp.concatenate(
            [cat(probs[b, p, :, :128], probs[b, p, :, 128:]) for b in range(batches)], axis=1
        )
        grad_scores = (chance.astype(F32) * (grad_probs - row_delta)).astype(BF)
        grad_k = jnp.where(mine, mm(grad_scores, q[p] * 0.125), 0.0)
        grad_v = jnp.where(mine, mm(chance, grad_o), 0.0)
        grad_pre_kv[count * p : count * (p + 1), :] = (
            grad_k[:PREFIX_ROWS] + grad_k[PREFIX_ROWS:]
        )[:count]
        grad_pre_kv[count * (p + 8) : count * (p + 9), :] = (
            grad_v[:PREFIX_ROWS] + grad_v[PREFIX_ROWS:]
        )[:count]


def mlp_kernel(
    att,
    x,
    cot,
    gain,
    shift,
    out_bias,
    fc_bias,
    pv,
    second,
    mixed,
    probs,
    hidden_far,
    middle,
    grad_mid,
    grad_att,
    grad_pre_kv,
    q,
    chances,
    hidden,
    slope,
    proj,
    fc,
    out,
    normed,
    total,
    fc_sems,
    proj_sems,
    sems,
):
    out_in = pltpu.make_async_copy(second.at[:, :, :, pl.ds(1024, 128)], out, sems.at[0])
    out_in.start()
    q_in = pltpu.make_async_copy(mixed.at[pl.ds(0, 8), 0], q, sems.at[2])
    q_in.start()
    chance_in = pltpu.make_async_copy(
        probs.at[:, :, pl.ds(0, PREFIX_ROWS), :], chances, sems.at[3]
    )
    chance_in.start()
    for s in range(3):
        fc_copy(second, fc, fc_sems, s).start()
    out_in.wait()
    value = x[...].astype(F32) + mm(att[...], out_matrix(out)) + out_bias[...].astype(F32)
    middle[...] = value
    normal, _ = norm_parts(value)
    normed[...] = (normal * gain[...].astype(F32) + shift[...].astype(F32)).astype(BF)
    for s in range(8):
        fc_copy(second, fc, fc_sems, s).wait()
        if s < 5:
            fc_copy(second, fc, fc_sems, s + 3).start()
        else:
            proj_copy(second, proj, proj_sems, s - 5).start()
        cols = pl.ds(512 * s, 512)
        v = mm(normed[...], fc[s].reshape(1024, 512)) + fc_bias[:, cols].astype(F32)
        cubic = (0.7978845608028654 * 0.044715) * (v * v)
        t = jnp.tanh(v * (cubic + 0.7978845608028654))
        half = 0.5 * t + 0.5
        hidden[:, cols] = (v * half).astype(BF)
        slope[:, cols] = (
            half + v * (half - half * half) * (6.0 * cubic + 2 * 0.7978845608028654)
        ).astype(BF)
    proj_copy(second, proj, proj_sems, 3).start()
    kept = pltpu.make_async_copy(hidden, hidden_far, sems.at[1])
    kept.start()
    for r in range(4):
        proj_copy(second, proj, proj_sems, r).wait()
        for half_row in range(2):
            s = 2 * r + half_row
            grad_pre = []
            for j in (2 * half_row, 2 * half_row + 1):
                back = mm_nt(cot[...], proj_rows(proj, r, j))
                cols = pl.ds(1024 * r + 256 * j, 256)
                grad_pre.append((back * slope[:, cols].astype(F32)).astype(BF))
            part = mm_nt(jnp.concatenate(grad_pre, axis=1), fc[s].reshape(1024, 512))
            if s == 0:
                total[...] = part
            else:
                total[...] += part
    value = cot[...].astype(F32) + norm_back(middle[...], total[...], gain[...].astype(F32))
    grad_mid[...] = value
    grad_att[...] = mm_nt(value.astype(BF), out_matrix(out)).astype(BF)
    kept.wait()
    q_in.wait()
    chance_in.wait()
    prefix_part(q, pv, chances, grad_att, att, grad_pre_kv)


def mlp_call(count, att, x, cot, gain, shift, out_bias, fc_bias, prefix_low, second, mixed, probs):
    tokens, batches = cot.shape[0], probs.shape[0]
    return pl.pallas_call(
        mlp_kernel,
        grid=(1,),
        in_specs=[whole((tokens, 1024))] * 3
        + [whole((1, 1024))] * 3
        + [whole((1, 4096)), pl.BlockSpec((8, PREFIX_ROWS, 128), lambda i: (1, 0, 0))]
        + [ANYWHERE] * 3,
        out_specs=[ANYWHERE] + [whole((tokens, 1024))] * 3 + [whole((16 * count, 128))],
        out_shape=[
            jax.ShapeDtypeStruct((tokens, 4096), BF),
            jax.ShapeDtypeStruct((tokens, 1024), F32),
            jax.ShapeDtypeStruct((tokens, 1024), F32),
            jax.ShapeDtypeStruct((tokens, 1024), BF),
            jax.ShapeDtypeStruct((16 * count, 128), F32),
        ],
        scratch_shapes=[
            VMEM((8, tokens, 128), BF),
            VMEM((batches, 8, PREFIX_ROWS, 256), BF),
            VMEM((tokens, 4096), BF),
            VMEM((tokens, 4096), BF),
            VMEM((4, 8, 256, 512), BF),
            VMEM((8, 4, 256, 512), BF),
            VMEM((4, 8, 256, 128), BF),
            VMEM((tokens, 1024), BF),
            VMEM((tokens, 1024), F32),
            pltpu.SemaphoreType.DMA((8,)),
            pltpu.SemaphoreType.DMA((4,)),
            pltpu.SemaphoreType.DMA((4,)),
        ],
        compiler_params=call_params(52),
        cost_estimate=lasting(1),
        name="mlp",
    )(att, x, cot, gain, shift, out_bias, fc_bias, prefix_low, second, mixed, probs)


def output_kernel(hidden, middle, proj_bias, second, output, proj, total, sems):
    for r in range(4):
        proj_copy(second, proj, sems, r).start()
    total[...] = middle[...] + proj_bias[...].astype(F32)
    for r in range(4):
        proj_copy(second, proj, sems, r).wait()
        rows = jnp.concatenate([proj_rows(proj, r, j) for j in range(4)], axis=0)
        total[...] += mm(hidden[:, pl.ds(1024 * r, 1024)], rows)
    output[...] = total[...].astype(BF)


def output_call(hidden, middle, proj_bias, second):
    tokens = hidden.shape[0]
    return pl.pallas_call(
        output_kernel,
        grid=(1,),
        in_specs=[whole((tokens, 4096)), whole((tokens, 1024)), whole((1, 1024)), ANYWHERE],
        out_specs=whole((tokens, 1024)),
        out_shape=jax.ShapeDtypeStruct((tokens, 1024), BF),
        scratch_shapes=[
            VMEM((4, 8, 256, 512), BF),
            VMEM((tokens, 1024), F32),
            pltpu.SemaphoreType.DMA((4,)),
        ],
        compiler_params=call_params(52),
        cost_estimate=lasting(1),
        name="output",
    )(hidden, middle, proj_bias, second)


def attend_back_kernel(
    q, k, v, pk, pv, probs, grad_att, att, w_nat, side0, side1, near, far, own, dkv, w_kv, sem
):
    step = pl.program_id(0)
    weights = pltpu.make_async_copy(w_nat.at[:, pl.ds(1024, 2048)], w_kv, sem)

    @pl.when(step == 0)
    def _():
        weights.start()

    delta = row_deltas(grad_att[...], att[...])
    for i in range(2):
        p = step * 2 + i
        keys = cat(pk[i], *[k[i, slot] for slot in range(5)])
        values = cat(pv[i], *[v[i, slot] for slot in range(5)])
        queries = two_heads(q[i, 0] * 0.125)
        grad_two = two_heads(grad_att[:, 128 * i : 128 * (i + 1)])
        row_delta = both_heads(delta, i)
        chance = probs[0, i]
        grad_probs = mm_nt(values, grad_two)
        grad_scores = (chance.astype(F32) * (grad_probs - row_delta)).astype(BF)
        grad_k = mm(grad_scores, queries)
        grad_v = mm(chance, grad_two)
        grad_q = heads_merged(mm_tn(keys, grad_scores)) * 0.125
        own[:, lanes(p * 128)] = grad_q.astype(BF)
        for slot in range(5):
            rows = slice(PREFIX_ROWS + 128 * slot, PREFIX_ROWS + 128 * (slot + 1))
            if slot == 0:
                own[:, lanes(p * 128 + 1024)] = grad_k[rows].astype(BF)
                own[:, lanes(p * 128 + 2048)] = grad_v[rows].astype(BF)
            else:
                sent = slice(128 * (slot - 1), 128 * slot)
                dkv[sent, lanes(p * 128)] = grad_k[rows].astype(BF)
                dkv[sent, lanes(p * 128 + 1024)] = grad_v[rows].astype(BF)

    @pl.when(step == 3)
    def _():
        weights.wait()
        part = mm_nt(dkv[...], w_kv[...]).astype(BF)
        side0[...] = part[:128]
        near[...] = part[128:256]
        side1[...] = part[256:384]
        far[...] = part[384:]


def attend_back_call(batch, mixed, prefix_low, probs, grad_att, att, w_nat):
    return pl.pallas_call(
        attend_back_kernel,
        grid=(4,),
        in_specs=[
            pl.BlockSpec((2, 1, 128, 128), lambda i: (i, 0, batch, 0)),
            pl.BlockSpec((2, 5, 128, 128), lambda i: (4 + i, 0, batch, 0)),
            pl.BlockSpec((2, 5, 128, 128), lambda i: (8 + i, 0, batch, 0)),
            pl.BlockSpec((2, PREFIX_ROWS, 128), lambda i: (i, 0, 0)),
            pl.BlockSpec((2, PREFIX_ROWS, 128), lambda i: (4 + i, 0, 0)),
            pl.BlockSpec((1, 2, KEYS, 256), lambda i: (batch, i, 0, 0)),
            pl.BlockSpec((128, 256), lambda i: (batch, i)),
            pl.BlockSpec((128, 256), lambda i: (batch, i)),
            ANYWHERE,
        ],
        out_specs=[
            whole((128, 1024)),
            whole((128, 1024)),
            whole((128, 1024)),
            whole((128, 1024)),
            whole((128, 3072)),
        ],
        out_shape=[
            jax.ShapeDtypeStruct((128, 1024), BF),
            jax.ShapeDtypeStruct((128, 1024), BF),
            jax.ShapeDtypeStruct((128, 1024), BF),
            jax.ShapeDtypeStruct((128, 1024), BF),
            jax.ShapeDtypeStruct((128, 3072), BF),
        ],
        scratch_shapes=[VMEM((512, 2048), BF), VMEM((1024, 2048), BF), pltpu.SemaphoreType.DMA],
        compiler_params=call_params(48),
        cost_estimate=lasting(1),
        name="attend_back",
    )(mixed, mixed, mixed, prefix_low, prefix_low, probs, grad_att, att, w_nat)


def own_back_kernel(own0, own1, own2, w_nat, result, owns):
    @pl.when(pl.program_id(0) == 0)
    def _():
        for batch, own in enumerate((own0, own1, own2)):
            owns[128 * batch : 128 * (batch + 1), :] = own[...]

    result[...] = mm_nt(owns[...], w_nat[...])


def own_back_call(owns, w_nat):
    tokens = 128 * len(owns)
    return pl.pallas_call(
        own_back_kernel,
        grid=(4,),
        in_specs=[whole((128, 3072))] * 3 + [pl.BlockSpec((256, 3072), lambda i: (i, 0))],
        out_specs=pl.BlockSpec((tokens, 256), lambda i: (0, i)),
        out_shape=jax.ShapeDtypeStruct((tokens, 1024), F32),
        scratch_shapes=[VMEM((tokens, 3072), BF)],
        compiler_params=call_params(52),
        cost_estimate=lasting(1),
        name="own_back",
    )(*owns, w_nat)


def first_back_kernel(me, x, grad_own, grad_mid, gain, *refs):
    in_grad = refs[-1]
    first = jnp.where(me[0] % 2 == 0, 1.0, 0.0)
    for batch in range(len(refs) // 2):
        landed, other = refs[2 * batch], refs[2 * batch + 1]
        rows = slice(128 * batch, 128 * (batch + 1))
        incoming = grad_own[rows, :] + landed[...].astype(F32) + first * other[...].astype(F32)
        back = norm_back(x[rows, :].astype(F32), incoming, gain[...].astype(F32))
        in_grad[rows, :] = (grad_mid[rows, :] + back).astype(BF)


def first_back_call(seq_me, x, grad_own, grad_mid, gain, parts):
    def spec(part):
        if part.ndim == 2:
            return whole((128, 1024))
        return pl.BlockSpec((None, 128, 1024), lambda i: (1, 0, 0))

    return pl.pallas_call(
        first_back_kernel,
        grid=(1,),
        in_specs=[SCALARS] + [whole(x.shape)] * 3 + [whole((1, 1024))] + [spec(p) for p in parts],
        out_specs=whole(x.shape),
        out_shape=jax.ShapeDtypeStruct(x.shape, BF),
        compiler_params=call_params(48),
        cost_estimate=lasting(1),
        name="first_back",
    )(seq_me, x, grad_own, grad_mid, gain, *parts)


def full(shard):
    rows = lax.all_gather(shard, "row", axis=0, tiled=True)
    return lax.all_gather(rows, "seq", axis=1, tiled=True)


def pieces(matrix):
    rows, cols = matrix.shape
    return (
        matrix.reshape(4, rows // 4, 8, cols // 8)
        .transpose(0, 2, 1, 3)
        .reshape(32, rows // 4, cols // 8)
    )


def side_by_side(fc_weight, proj_weight, out_weight):
    quarter = proj_weight.shape[-2] // 4
    proj = [proj_weight[..., quarter * j : quarter * (j + 1), :] for j in range(4)]
    return jnp.concatenate([fc_weight, *proj, out_weight], axis=-1)


def gathered_plainly(sent, x_side, qkv_weight, out_weight, fc_weight, proj_weight):
    second = side_by_side(*[pieces(full(w)) for w in (fc_weight, proj_weight, out_weight)])
    h1 = moved(sent, "seq", 2)
    h2 = moved(h1, "seq", 2)
    o1 = swapped(h1, *X)
    r2 = swapped(jnp.where(x_side == 0, sent, h2), *X)
    return (h1, h2, o1, r2), [(pieces(full(qkv_weight)), NATURAL)], second


def gathered_by_swaps(sent, x_side, qkv_weight, out_weight, fc_weight, proj_weight):
    second = lax.all_gather(
        packed_call(fc_weight, proj_weight, out_weight), ("row", "seq"), axis=0
    )
    first = qkv_weight[None]
    v0 = cat(first, swapped(first, *ZF))
    g0 = swapped(v0, *ZN)
    h1 = moved(after(sent, v0), "seq", 2)
    v = cat(v0, g0)
    vx, vy = swapped(v, *X), swapped(v, *Y)
    h2 = moved(after(h1, g0), "seq", 2)
    vd = swapped(after(vx, vy), *Y)
    o1 = swapped(after(h1, vx, vy), *X)
    r2 = swapped(after(jnp.where(x_side == 0, sent, h2), o1), *X)
    zs = (0, 2, 1, 3)
    unit0 = with_cores([(v, zs, 0, 0), (vx, zs, 1, 0), (vy, zs, 0, 1), (vd, zs, 1, 1)])
    return (h1, h2, o1, r2), unit0, second


def local(
    activations,
    cotangent,
    segment_ids,
    prefix_embed,
    adapt_in,
    adapt_in_bias,
    adapt_out,
    adapt_out_bias,
    ln1_gain,
    ln1_bias,
    qkv_weight,
    qkv_bias,
    out_weight,
    out_bias,
    ln2_gain,
    ln2_bias,
    fc_weight,
    fc_bias,
    proj_weight,
    proj_bias,
):
    batches, rows_dev, tok_dev, width = activations.shape
    tokens = batches * rows_dev * tok_dev
    assert tok_dev == 128 and rows_dev == 1 and lax.axis_size("seq") % 2 == 0
    row_me, seq_me = lax.axis_index("row"), lax.axis_index("seq")
    x_side = seq_me % 2

    def flat(vector):
        return vector.reshape(1, -1)

    x = activations.reshape(tokens, width)
    cot = cotangent.reshape(tokens, width)

    ids = (segment_ids.reshape(1, tokens) + 1).astype(BF)
    ids = jnp.pad(ids, ((0, 7), (0, width - tokens)))
    sent = first_norm_call(x, ids, flat(ln1_gain), flat(ln1_bias))

    if (lax.axis_size("row"), lax.axis_size("seq")) == (4, 8):
        (h1, h2, o1, r2), unit0, second = gathered_by_swaps(
            sent, x_side, qkv_weight, out_weight, fc_weight, proj_weight
        )
        me = jnp.stack([row_me, seq_me]).astype(jnp.int32)
    else:
        (h1, h2, o1, r2), unit0, second = gathered_plainly(
            sent, x_side, qkv_weight, out_weight, fc_weight, proj_weight
        )
        me = jnp.zeros((2,), jnp.int32)
    second = second.reshape(4, 8, 256, 1152)

    seg = jnp.stack([part[tokens, :tokens] for part in (sent, o1, h1, r2, h2)])
    seg = seg.astype(F32).reshape(5, batches, tok_dev).transpose(1, 0, 2)

    squashed, prefix_low = prefix_call(
        prefix_embed, adapt_in, flat(adapt_in_bias), adapt_out, flat(adapt_out_bias)
    )
    mixed, w_nat = qkv_call(me, (sent, o1, h1, r2, h2), unit0, flat(qkv_bias), tokens)
    att, probs = attend_call(seg, mixed, prefix_low, batches, tokens)
    hidden, middle, grad_mid, grad_att, pre_kv = mlp_call(
        prefix_embed.shape[0],
        att,
        x,
        cot,
        flat(ln2_gain),
        flat(ln2_bias),
        flat(out_bias),
        flat(fc_bias),
        prefix_low,
        second,
        mixed,
        probs,
    )

    if (lax.axis_size("row"), lax.axis_size("seq")) == (4, 8):
        total_kv = lax.all_gather(pre_kv, ("row", "seq"), axis=0)
    else:
        total_kv = lax.psum(pre_kv, ("row", "seq"))[None]

    def back(batch, incoming):
        return attend_back_call(batch, mixed, prefix_low, probs, incoming, att, w_nat)

    def to_far(far, other):
        return (far.astype(F32) + jnp.where(x_side == 1, other, 0).astype(F32)).astype(BF)

    def to_near(near, other, passing):
        return (near.astype(F32) + other.astype(F32) + passing.astype(F32)).astype(BF)

    sides0, sides1, near0, far0, own0 = back(0, grad_att)
    other01 = swapped(sides1, *X)
    other00 = swapped(sides0, *X)
    sides2, sides3, near1, far1, own1 = back(1, after(grad_att, own0))
    other11 = swapped(sides3, *X)
    other10 = swapped(sides2, *X)
    to_far0 = to_far(far0, other01)
    passing0 = moved(to_far0, "seq", -2)
    sides4, sides5, near2, far2, own2 = back(2, after(grad_att, own1, to_far0, other00))
    other21 = swapped(sides5, *X)
    other20 = swapped(sides4, *X)
    to_far1 = to_far(after(far1, own2), other11)
    passing1 = moved(to_far1, "seq", -2)
    to_near0 = to_near(near0, other00, passing0)
    landed0 = moved(to_near0, "seq", -2)
    grad_own = own_back_call((after(own0, to_near0, to_far1), own1, own2), w_nat)
    to_far2 = to_far(after(far2, grad_own), other21)
    passing2 = moved(to_far2, "seq", -2)
    to_near1 = to_near(near1, other10, passing1)
    landed1 = moved(to_near1, "seq", -2)
    output = output_call(
        after(hidden, grad_own, to_near1, to_far2), middle, flat(proj_bias), second
    )
    landed2 = moved(after(to_near(near2, other20, passing2), output), "seq", -2)
    prefix_grad, adapt_in_grad, in_bias_grad, adapt_out_grad, out_bias_grad = prefix_back_call(
        after(total_kv, output, passing2), squashed, prefix_embed, adapt_in, adapt_out
    )
    parts = (landed0, other01, landed1, other11, landed2, other21)
    in_grad = first_back_call(
        seq_me.reshape(1), after(x, prefix_grad), grad_own, grad_mid, flat(ln1_gain), parts
    )
    shape = activations.shape
    return (
        output.reshape(shape),
        in_grad.reshape(shape),
        prefix_grad,
        adapt_in_grad,
        in_bias_grad.reshape(-1),
        adapt_out_grad,
        out_bias_grad.reshape(-1),
    )


def solution(mesh):
    rows = P(None, "row", "seq", None)
    split = P("row", "seq")
    placed = (
        rows,
        rows,
        P(None, "row", "seq"),
        P(),
        P(),
        P(),
        P(),
        P(),
        P(),
        P(),
        split,
        P(),
        split,
        P(),
        P(),
        P(),
        split,
        P(),
        split,
        P(),
    )
    return jax.shard_map(
        local,
        mesh=mesh,
        in_specs=placed,
        out_specs=(rows, rows, P(), P(), P(), P(), P()),
        check_vma=False,
    )
```

```python
import functools

import jax
import jax.numpy as jnp
from jax import lax
from jax.experimental import pallas as pl
from jax.experimental.pallas import tpu as pltpu
from jax.sharding import PartitionSpec as P

EPS = 1e-05
MASKED = -1e30
PREFIX_ROWS = 16
BF = jnp.bfloat16
F32 = jnp.float32
MIB = 1 << 20
HIGHEST = lax.Precision.HIGHEST
VMEM = pltpu.VMEM
ANYWHERE = pl.BlockSpec(memory_space=pl.ANY)
SCALARS = pl.BlockSpec(memory_space=pltpu.SMEM)


def mm(left, right, precision=None):
    return jnp.dot(left, right, precision=precision, preferred_element_type=F32)


def mm_nt(left, right, precision=None):
    return lax.dot_general(
        left, right, (((1,), (1,)), ((), ())), precision=precision, preferred_element_type=F32
    )


def mm_tn(left, right, precision=None):
    return lax.dot_general(
        left, right, (((0,), (0,)), ((), ())), precision=precision, preferred_element_type=F32
    )


def cat(*parts):
    return jnp.concatenate(parts, axis=0)


X, ZN, ZF, CORE, Y = ("seq", 1), ("seq", 2), ("seq", 4), ("row", 1), ("row", 2)


def swapped(value, axis, bit):
    count = lax.axis_size(axis)
    return lax.ppermute(value, axis, [(i, i ^ bit) for i in range(count)])


def moved(value, axis, steps):
    count = lax.axis_size(axis)
    low, high = max(0, -steps), min(count, count - steps)
    return lax.ppermute(value, axis, [(i, i + steps) for i in range(low, high)])


def after(value, *others):
    return lax.optimization_barrier((value,) + others)[0]


NATURAL = tuple((r, s) for r in range(4) for s in range(8))


def with_cores(parts):
    out = []
    for array, zs, x, y in parts:
        out.append((array, tuple((2 * y, 2 * z + x) for z in zs)))
        out.append((swapped(array, *CORE), tuple((2 * y + 1, 2 * z + x) for z in zs)))
    return out


def norm_parts(values):
    centre = values - jnp.mean(values, axis=-1, keepdims=True)
    spread = jnp.mean(centre * centre, axis=-1, keepdims=True)
    scale = lax.rsqrt(spread + EPS)
    return centre * scale, scale


def norm_back(values, incoming, gain):
    normal, scale = norm_parts(values)
    e = incoming * gain
    return scale * (
        e
        - jnp.mean(e, axis=-1, keepdims=True)
        - normal * jnp.mean(e * normal, axis=-1, keepdims=True)
    )


def call_params(limit):
    return pltpu.CompilerParams(vmem_limit_bytes=limit * MIB)


def lasting(micros):
    return pl.CostEstimate(
        flops=int(micros * 1e9), bytes_accessed=int(micros * 1e6), transcendentals=0
    )


def whole(shape):
    return pl.BlockSpec(shape, lambda *_: (0,) * len(shape))


def lanes(start, size=128):
    if isinstance(start, int):
        return pl.ds(start, size)
    return pl.ds(pl.multiple_of(start, 128), size)


def each_piece(me, arrays, spots):
    for array, slots in zip(arrays, spots):
        for slot, (row_bits, seq_bits) in enumerate(slots):
            yield array, slot, me[0] ^ row_bits, me[1] ^ seq_bits


def first_norm_kernel(x, ids, gain, shift, sent):
    tokens = x.shape[0]
    normal, _ = norm_parts(x[...].astype(F32))
    sent[:tokens, :] = (normal * gain[...].astype(F32) + shift[...].astype(F32)).astype(BF)
    sent[tokens:, :] = ids[...]


def first_norm_call(x, ids, gain, shift):
    tokens, width = x.shape
    return pl.pallas_call(
        first_norm_kernel,
        out_shape=jax.ShapeDtypeStruct((tokens + 8, width), BF),
        compiler_params=call_params(16),
        cost_estimate=lasting(1),
        name="first_norm",
    )(x, ids, gain, shift)


def packed_kernel(fc_weight, proj_weight, out_weight, packed):
    packed[:, :512] = fc_weight[...]
    for j in range(4):
        packed[:, 512 + 128 * j : 640 + 128 * j] = proj_weight[256 * j : 256 * (j + 1), :]
    packed[:, 1024:] = out_weight[...]


def packed_call(fc_weight, proj_weight, out_weight):
    return pl.pallas_call(
        packed_kernel,
        out_shape=jax.ShapeDtypeStruct((256, 1152), BF),
        compiler_params=call_params(56),
        cost_estimate=lasting(1),
        name="packed",
    )(fc_weight, proj_weight, out_weight)


def prefix_kernel(embed, w_in, b_in, w_out, b_out, squashed, low):
    inner = jnp.tanh(mm(embed[...], w_in[...], HIGHEST) + b_in[...])
    squashed[...] = inner
    pairs = mm(inner, w_out[...], HIGHEST) + b_out[...]
    pairs = cat(pairs, jnp.zeros((PREFIX_ROWS - pairs.shape[0], pairs.shape[1]), F32)).astype(BF)
    for p in range(low.shape[0]):
        low[p] = pairs[:, 128 * p : 128 * (p + 1)]


def prefix_call(embed, w_in, b_in, w_out, b_out):
    return pl.pallas_call(
        prefix_kernel,
        out_shape=[
            jax.ShapeDtypeStruct((embed.shape[0], w_in.shape[1]), F32),
            jax.ShapeDtypeStruct((w_out.shape[1] // 128, PREFIX_ROWS, 128), BF),
        ],
        compiler_params=call_params(24),
        cost_estimate=lasting(1),
        name="prefix",
    )(embed, w_in, b_in, w_out, b_out)


def prefix_back_kernel(
    total,
    squashed,
    embed,
    w_in_far,
    w_out_far,
    prefix_grad,
    in_grad_far,
    in_bias,
    out_grad_far,
    out_bias,
    w_in,
    w_out,
    in_grad,
    out_grad,
    sems,
):
    count = embed.shape[0]
    w_out_copy = pltpu.make_async_copy(w_out_far, w_out, sems.at[0])
    w_in_copy = pltpu.make_async_copy(w_in_far, w_in, sems.at[1])
    w_out_copy.start()
    w_in_copy.start()
    summed = jnp.sum(total[...], axis=0)
    grad_kv = jnp.concatenate([summed[count * p : count * (p + 1)] for p in range(16)], axis=1)
    inner = squashed[...]
    out_bias[...] = jnp.sum(grad_kv, axis=0, keepdims=True)
    low_kv = grad_kv.astype(BF)
    out_grad[...] = mm_tn(inner.astype(BF), low_kv)
    out_copy = pltpu.make_async_copy(out_grad, out_grad_far, sems.at[2])
    out_copy.start()
    w_out_copy.wait()
    grad_z = mm_nt(w_out[...].astype(BF), low_kv).T * (1.0 - inner * inner)
    in_bias[...] = jnp.sum(grad_z, axis=0, keepdims=True)
    low_z = grad_z.astype(BF)
    in_grad[...] = mm_tn(embed[...].astype(BF), low_z)
    in_copy = pltpu.make_async_copy(in_grad, in_grad_far, sems.at[3])
    in_copy.start()
    w_in_copy.wait()
    prefix_grad[...] = mm_nt(w_in[...].astype(BF), low_z).T
    out_copy.wait()
    in_copy.wait()


def prefix_back_call(total, squashed, embed, w_in, w_out):
    count, width = embed.shape
    hidden = w_in.shape[1]
    return pl.pallas_call(
        prefix_back_kernel,
        grid=(1,),
        in_specs=[
            whole(total.shape),
            whole(squashed.shape),
            whole(embed.shape),
            ANYWHERE,
            ANYWHERE,
        ],
        out_specs=[
            whole((count, width)),
            ANYWHERE,
            whole((1, hidden)),
            ANYWHERE,
            whole((1, 2 * width)),
        ],
        out_shape=[
            jax.ShapeDtypeStruct((count, width), F32),
            jax.ShapeDtypeStruct((width, hidden), F32),
            jax.ShapeDtypeStruct((1, hidden), F32),
            jax.ShapeDtypeStruct((hidden, 2 * width), F32),
            jax.ShapeDtypeStruct((1, 2 * width), F32),
        ],
        scratch_shapes=[
            VMEM((width, hidden), F32),
            VMEM((hidden, 2 * width), F32),
            VMEM((width, hidden), F32),
            VMEM((hidden, 2 * width), F32),
            pltpu.SemaphoreType.DMA((4,)),
        ],
        compiler_params=call_params(56),
        cost_estimate=lasting(1),
        name="prefix_back",
    )(total, squashed, embed, w_in, w_out)


def packed_kernel(fc_weight, proj_weight, out_weight, packed):
    packed[:, :512] = fc_weight[...]
    for j in range(4):
        packed[:, 512 + 128 * j : 640 + 128 * j] = proj_weight[256 * j : 256 * (j + 1), :]
    packed[:, 1024:] = out_weight[...]


def packed_call(fc_weight, proj_weight, out_weight):
    return pl.pallas_call(
        packed_kernel,
        out_shape=jax.ShapeDtypeStruct((256, 1152), BF),
        compiler_params=call_params(56),
        cost_estimate=lasting(1),
        name="packed",
    )(fc_weight, proj_weight, out_weight)


def prefix_kernel(embed, w_in, b_in, w_out, b_out, squashed, low):
    inner = jnp.tanh(mm(embed[...], w_in[...], HIGHEST) + b_in[...])
    squashed[...] = inner
    pairs = mm(inner, w_out[...], HIGHEST) + b_out[...]
    pairs = cat(pairs, jnp.zeros((PREFIX_ROWS - pairs.shape[0], pairs.shape[1]), F32)).astype(BF)
    for p in range(low.shape[0]):
        low[p] = pairs[:, 128 * p : 128 * (p + 1)]


def prefix_call(embed, w_in, b_in, w_out, b_out):
    return pl.pallas_call(
        prefix_kernel,
        out_shape=[
            jax.ShapeDtypeStruct((embed.shape[0], w_in.shape[1]), F32),
            jax.ShapeDtypeStruct((w_out.shape[1] // 128, PREFIX_ROWS, 128), BF),
        ],
        compiler_params=call_params(24),
        cost_estimate=lasting(1),
        name="prefix",
    )(embed, w_in, b_in, w_out, b_out)


def prefix_back_kernel(
    count, total, squashed, embed, w_in, w_out, prefix_grad, in_grad, in_bias, out_grad, out_bias
):
    summed = jnp.sum(total[...], axis=0)
    grad_kv = jnp.concatenate([summed[count * p : count * (p + 1)] for p in range(16)], axis=1)
    inner = squashed[...]
    out_bias[...] = jnp.sum(grad_kv, axis=0, keepdims=True)
    low_kv = grad_kv.astype(BF)
    out_grad[...] = mm_tn(inner.astype(BF), low_kv)
    grad_z = mm_nt(w_out[...].astype(BF), low_kv).T * (1.0 - inner * inner)
    in_bias[...] = jnp.sum(grad_z, axis=0, keepdims=True)
    low_z = grad_z.astype(BF)
    in_grad[...] = mm_tn(embed[...].astype(BF), low_z)
    prefix_grad[...] = mm_nt(w_in[...].astype(BF), low_z).T


def prefix_back_call(total, squashed, embed, w_in, w_out):
    count, width = embed.shape
    hidden = w_in.shape[1]
    return pl.pallas_call(
        functools.partial(prefix_back_kernel, count),
        out_shape=[
            jax.ShapeDtypeStruct((count, width), F32),
            jax.ShapeDtypeStruct((width, hidden), F32),
            jax.ShapeDtypeStruct((1, hidden), F32),
            jax.ShapeDtypeStruct((hidden, 2 * width), F32),
            jax.ShapeDtypeStruct((1, 2 * width), F32),
        ],
        compiler_params=call_params(56),
        cost_estimate=lasting(1),
        name="prefix_back",
    )(total, squashed, embed, w_in, w_out)


def qkv_kernel(spots, me, own, o1, h1, r2, h2, bias, *refs):
    arrays = refs[: len(spots)]
    mixed, natural, wide, sems = refs[len(spots) :]
    step = pl.program_id(0)
    tokens = mixed.shape[2]

    @pl.when(step == 0)
    def _():
        for array, slot, r, s in each_piece(me, arrays, spots):
            pltpu.make_async_copy(
                array.at[slot],
                wide.at[
                    s // 2,
                    pl.ds(pl.multiple_of(r * 256, 256), 256),
                    pl.ds(pl.multiple_of((s % 2) * 384, 128), 384),
                ],
                sems.at[s // 2],
            ).start()

    pltpu.make_async_copy(wide.at[step], wide.at[step], sems.at[step]).wait()
    natural[...] = wide[step]

    def one(slot, block):
        value = (mm(block, wide[step]) + bias[...].astype(F32)).astype(BF)
        for col in range(6):
            mixed[col, slot] = value[:, 128 * col : 128 * (col + 1)]

    one(0, own[:tokens, :])

    @pl.when(step >= 1)
    def _():
        for slot, ref in enumerate((o1, h1, r2, h2)):
            one(slot + 1, ref[:tokens, :])


def qkv_call(me, blocks, parts, bias, tokens):
    spots = tuple(part[1] for part in parts)
    return pl.pallas_call(
        functools.partial(qkv_kernel, spots),
        grid=(4,),
        in_specs=[SCALARS]
        + [whole(block.shape) for block in blocks]
        + [pl.BlockSpec((1, 768), lambda s: (0, s))]
        + [ANYWHERE] * len(spots),
        out_specs=[
            pl.BlockSpec((6, 5, tokens, 128), lambda s: (s, 0, 0, 0)),
            pl.BlockSpec((1024, 768), lambda s: (0, s)),
        ],
        out_shape=[
            jax.ShapeDtypeStruct((24, 5, tokens, 128), BF),
            jax.ShapeDtypeStruct((1024, 3072), BF),
        ],
        scratch_shapes=[VMEM((4, 1024, 768), BF), pltpu.SemaphoreType.DMA((4,))],
        compiler_params=call_params(40),
        cost_estimate=lasting(1),
        name="qkv",
    )(me, *blocks, bias, *[part[0] for part in parts])


def allowed_bias(seg, out):
    query = jnp.broadcast_to(seg[0:1, :], (128, 128))
    key_at = lax.broadcasted_iota(jnp.int32, (128, 128), 0)
    query_at = lax.broadcasted_iota(jnp.int32, (128, 128), 1)
    prefix_at = lax.broadcasted_iota(jnp.int32, (PREFIX_ROWS, 256), 0)
    out[0:PREFIX_ROWS, :] = jnp.where(prefix_at < 10, 0.0, MASKED)
    for slot in range(5):
        key = jnp.broadcast_to(seg[slot : slot + 1, :], (128, 128)).T
        allowed = key == query
        if slot == 0:
            allowed = allowed & (key_at <= query_at)
        value = jnp.where(allowed, 0.0, MASKED)
        rows = slice(PREFIX_ROWS + 128 * slot, PREFIX_ROWS + 128 * (slot + 1))
        out[rows, :128] = value
        out[rows, 128:] = value


def two_heads(block):
    lane = lax.broadcasted_iota(jnp.int32, block.shape, 1)
    zero = jnp.zeros_like(block)
    return cat(jnp.where(lane < 64, block, zero), jnp.where(lane < 64, zero, block))


def heads_merged(both):
    feature = lax.broadcasted_iota(jnp.int32, (128, 128), 0)
    return jnp.where(feature < 64, both[:, :128], both[:, 128:]).T


KEYS = PREFIX_ROWS + 5 * 128


def attend_kernel(seg, q, k, v, pk, pv, att, probs, bias):
    allowed_bias(seg[0], bias)
    for p in range(8):
        keys = cat(pk[p], *[k[p, slot] for slot in range(5)])
        values = cat(pv[p], *[v[p, slot] for slot in range(5)])
        scores = mm_nt(keys, two_heads(q[p, 0] * 0.125)) + bias[...]
        top = jnp.max(scores, axis=0, keepdims=True)
        expo = jnp.exp(scores - top)
        total = jnp.sum(expo, axis=0, keepdims=True)
        chance = (expo * (1.0 / total)).astype(BF)
        probs[0, p] = chance
        att[:, lanes(p * 128)] = heads_merged(mm_tn(values, chance)).astype(BF)


def attend_call(seg, mixed, prefix_low, batches, tokens):
    return pl.pallas_call(
        attend_kernel,
        grid=(batches,),
        in_specs=[
            pl.BlockSpec((1, 5, 128), lambda b: (b, 0, 0)),
            pl.BlockSpec((8, 1, 128, 128), lambda b: (0, 0, b, 0)),
            pl.BlockSpec((8, 5, 128, 128), lambda b: (1, 0, b, 0)),
            pl.BlockSpec((8, 5, 128, 128), lambda b: (2, 0, b, 0)),
            pl.BlockSpec((8, PREFIX_ROWS, 128), lambda b: (0, 0, 0)),
            pl.BlockSpec((8, PREFIX_ROWS, 128), lambda b: (1, 0, 0)),
        ],
        out_specs=[
            pl.BlockSpec((128, 1024), lambda b: (b, 0)),
            pl.BlockSpec((1, 8, KEYS, 256), lambda b: (b, 0, 0, 0)),
        ],
        out_shape=[
            jax.ShapeDtypeStruct((tokens, 1024), BF),
            jax.ShapeDtypeStruct((batches, 8, KEYS, 256), BF),
        ],
        scratch_shapes=[VMEM((KEYS, 256), F32)],
        compiler_params=call_params(48),
        cost_estimate=lasting(1),
        name="attend",
    )(seg, mixed, mixed, mixed, prefix_low, prefix_low)


def fc_copy(second, fc, sems, s):
    return pltpu.make_async_copy(second.at[:, s, :, pl.ds(0, 512)], fc.at[s], sems.at[s])


def proj_copy(second, proj, sems, r):
    return pltpu.make_async_copy(second.at[r, :, :, pl.ds(512, 512)], proj.at[r], sems.at[r])


def proj_rows(proj, r, j):
    return jnp.concatenate([proj[r, s, :, 128 * j : 128 * (j + 1)] for s in range(8)], axis=1)


def out_matrix(out):
    return jnp.concatenate([out[:, s].reshape(1024, 128) for s in range(8)], axis=1)


def row_deltas(grad_att, att):
    width = grad_att.shape[1]
    rows = max(8, width // 64)
    head = lax.broadcasted_iota(jnp.int32, (rows, width), 0)
    lane = lax.broadcasted_iota(jnp.int32, (rows, width), 1)
    pick = jnp.where(lane // 64 == head, 1.0, 0.0).astype(BF)
    product = grad_att.astype(F32) * att.astype(F32)
    high = product.astype(BF)
    return mm_nt(pick, high) + mm_nt(pick, (product - high.astype(F32)).astype(BF))


def both_heads(delta, p):
    return jnp.concatenate([delta[2 * p : 2 * p + 1, :], delta[2 * p + 1 : 2 * p + 2, :]], axis=1)


def prefix_part(q, pv, probs, grad_att, att, grad_pre_kv):
    batches, count = probs.shape[0], grad_pre_kv.shape[0] // 16
    delta = row_deltas(grad_att[...], att[...])
    key = lax.broadcasted_iota(jnp.int32, (2 * PREFIX_ROWS, 128), 0)
    lane = lax.broadcasted_iota(jnp.int32, (2 * PREFIX_ROWS, 128), 1)
    mine = (lane < 64) == (key < PREFIX_ROWS)
    for p in range(8):
        cols = slice(128 * p, 128 * (p + 1))
        grad_o = grad_att[:, cols]
        values = jnp.where(mine, cat(pv[p], pv[p]), jnp.zeros((), BF))
        grad_probs = mm_nt(values, grad_o)
        head = lax.broadcasted_iota(jnp.int32, grad_probs.shape, 0) < PREFIX_ROWS
        row_delta = jnp.where(head, delta[2 * p : 2 * p + 1, :], delta[2 * p + 1 : 2 * p + 2, :])
        chance = jnp.concatenate(
            [cat(probs[b, p, :, :128], probs[b, p, :, 128:]) for b in range(batches)], axis=1
        )
        grad_scores = (chance.astype(F32) * (grad_probs - row_delta)).astype(BF)
        grad_k = jnp.where(mine, mm(grad_scores, q[p] * 0.125), 0.0)
        grad_v = jnp.where(mine, mm(chance, grad_o), 0.0)
        grad_pre_kv[count * p : count * (p + 1), :] = (
            grad_k[:PREFIX_ROWS] + grad_k[PREFIX_ROWS:]
        )[:count]
        grad_pre_kv[count * (p + 8) : count * (p + 9), :] = (
            grad_v[:PREFIX_ROWS] + grad_v[PREFIX_ROWS:]
        )[:count]


def mlp_kernel(
    att,
    x,
    cot,
    gain,
    shift,
    out_bias,
    fc_bias,
    pv,
    second,
    mixed,
    probs,
    hidden_far,
    middle_far,
    grad_mid,
    grad_att,
    grad_pre_kv,
    q,
    chances,
    middle,
    hidden,
    slope,
    proj,
    fc,
    out,
    normed,
    total,
    fc_sems,
    proj_sems,
    sems,
):
    out_in = pltpu.make_async_copy(second.at[:, :, :, pl.ds(1024, 128)], out, sems.at[0])
    out_in.start()
    q_in = pltpu.make_async_copy(mixed.at[pl.ds(0, 8), 0], q, sems.at[2])
    q_in.start()
    chance_in = pltpu.make_async_copy(
        probs.at[:, :, pl.ds(0, PREFIX_ROWS), :], chances, sems.at[3]
    )
    chance_in.start()
    for s in range(3):
        fc_copy(second, fc, fc_sems, s).start()
    out_in.wait()
    value = x[...].astype(F32) + mm(att[...], out_matrix(out)) + out_bias[...].astype(F32)
    middle[...] = value
    middle_out = pltpu.make_async_copy(middle, middle_far, sems.at[4])
    middle_out.start()
    normal, _ = norm_parts(value)
    normed[...] = (normal * gain[...].astype(F32) + shift[...].astype(F32)).astype(BF)
    def gelu(v, rows, cols):
        cubic = (0.7978845608028654 * 0.044715) * (v * v)
        t = jnp.tanh(v * (cubic + 0.7978845608028654))
        half = 0.5 * t + 0.5
        hidden[rows, cols] = (v * half).astype(BF)
        slope[rows, cols] = (
            half + v * (half - half * half) * (6.0 * cubic + 2 * 0.7978845608028654)
        ).astype(BF)

    last = None
    for s in range(8):
        fc_copy(second, fc, fc_sems, s).wait()
        if s < 5:
            fc_copy(second, fc, fc_sems, s + 3).start()
        else:
            proj_copy(second, proj, proj_sems, s - 5).start()
        for n in range(2):
            for m in range(normed.shape[0] // 128):
                cols = pl.ds(512 * s + 256 * n, 256)
                rows = pl.ds(128 * m, 128)
                w = fc[s, :, :, 256 * n : 256 * (n + 1)].reshape(1024, 256)
                v = mm(normed[rows, :], w) + fc_bias[:, cols].astype(F32)
                if last is not None:
                    gelu(*last)
                last = (v, rows, cols)
    gelu(*last)
    proj_copy(second, proj, proj_sems, 3).start()
    kept = pltpu.make_async_copy(hidden, hidden_far, sems.at[1])
    kept.start()
    for r in range(4):
        proj_copy(second, proj, proj_sems, r).wait()
        for half_row in range(2):
            s = 2 * r + half_row
            grad_pre = []
            for j in (2 * half_row, 2 * half_row + 1):
                back = mm_nt(cot[...], proj_rows(proj, r, j))
                cols = pl.ds(1024 * r + 256 * j, 256)
                grad_pre.append((back * slope[:, cols].astype(F32)).astype(BF))
            part = mm_nt(jnp.concatenate(grad_pre, axis=1), fc[s].reshape(1024, 512))
            if s == 0:
                total[...] = part
            else:
                total[...] += part
    value = cot[...].astype(F32) + norm_back(middle[...], total[...], gain[...].astype(F32))
    grad_mid[...] = value
    grad_att[...] = mm_nt(value.astype(BF), out_matrix(out)).astype(BF)
    kept.wait()
    middle_out.wait()
    q_in.wait()
    chance_in.wait()
    prefix_part(q, pv, chances, grad_att, att, grad_pre_kv)


def mlp_call(count, att, x, cot, gain, shift, out_bias, fc_bias, prefix_low, second, mixed, probs):
    tokens, batches = cot.shape[0], probs.shape[0]
    return pl.pallas_call(
        mlp_kernel,
        grid=(1,),
        in_specs=[whole((tokens, 1024))] * 3
        + [whole((1, 1024))] * 3
        + [whole((1, 4096)), pl.BlockSpec((8, PREFIX_ROWS, 128), lambda i: (1, 0, 0))]
        + [ANYWHERE] * 3,
        out_specs=[ANYWHERE] * 2 + [whole((tokens, 1024))] * 2 + [whole((16 * count, 128))],
        out_shape=[
            jax.ShapeDtypeStruct((tokens, 4096), BF),
            jax.ShapeDtypeStruct((tokens, 1024), F32),
            jax.ShapeDtypeStruct((tokens, 1024), F32),
            jax.ShapeDtypeStruct((tokens, 1024), BF),
            jax.ShapeDtypeStruct((16 * count, 128), F32),
        ],
        scratch_shapes=[
            VMEM((8, tokens, 128), BF),
            VMEM((batches, 8, PREFIX_ROWS, 256), BF),
            VMEM((tokens, 1024), F32),
            VMEM((tokens, 4096), BF),
            VMEM((tokens, 4096), BF),
            VMEM((4, 8, 256, 512), BF),
            VMEM((8, 4, 256, 512), BF),
            VMEM((4, 8, 256, 128), BF),
            VMEM((tokens, 1024), BF),
            VMEM((tokens, 1024), F32),
            pltpu.SemaphoreType.DMA((8,)),
            pltpu.SemaphoreType.DMA((4,)),
            pltpu.SemaphoreType.DMA((5,)),
        ],
        compiler_params=call_params(52),
        cost_estimate=lasting(1),
        name="mlp",
    )(att, x, cot, gain, shift, out_bias, fc_bias, prefix_low, second, mixed, probs)


def output_kernel(hidden, middle, proj_bias, second, output, proj, total, sems):
    for r in range(4):
        proj_copy(second, proj, sems, r).start()
    total[...] = middle[...] + proj_bias[...].astype(F32)
    for r in range(4):
        proj_copy(second, proj, sems, r).wait()
        rows = jnp.concatenate([proj_rows(proj, r, j) for j in range(4)], axis=0)
        total[...] += mm(hidden[:, pl.ds(1024 * r, 1024)], rows)
    output[...] = total[...].astype(BF)


def output_call(hidden, middle, proj_bias, second):
    tokens = hidden.shape[0]
    return pl.pallas_call(
        output_kernel,
        grid=(1,),
        in_specs=[whole((tokens, 4096)), whole((tokens, 1024)), whole((1, 1024)), ANYWHERE],
        out_specs=whole((tokens, 1024)),
        out_shape=jax.ShapeDtypeStruct((tokens, 1024), BF),
        scratch_shapes=[
            VMEM((4, 8, 256, 512), BF),
            VMEM((tokens, 1024), F32),
            pltpu.SemaphoreType.DMA((4,)),
        ],
        compiler_params=call_params(52),
        cost_estimate=lasting(1),
        name="output",
    )(hidden, middle, proj_bias, second)


def attend_back_kernel(
    q, k, v, pk, pv, probs, grad_att, att, w_nat, side0, side1, near, far, own, dkv, w_kv, sem
):
    step = pl.program_id(0)
    weights = pltpu.make_async_copy(w_nat.at[:, pl.ds(1024, 2048)], w_kv, sem)

    @pl.when(step == 0)
    def _():
        weights.start()

    delta = row_deltas(grad_att[...], att[...])
    for i in range(4):
        p = step * 4 + i
        keys = cat(pk[i], *[k[i, slot] for slot in range(5)])
        values = cat(pv[i], *[v[i, slot] for slot in range(5)])
        queries = two_heads(q[i, 0] * 0.125)
        grad_two = two_heads(grad_att[:, 128 * i : 128 * (i + 1)])
        row_delta = both_heads(delta, i)
        chance = probs[0, i]
        grad_probs = mm_nt(values, grad_two)
        grad_scores = (chance.astype(F32) * (grad_probs - row_delta)).astype(BF)
        grad_k = mm(grad_scores, queries)
        grad_v = mm(chance, grad_two)
        grad_q = heads_merged(mm_tn(keys, grad_scores)) * 0.125
        own[:, lanes(p * 128)] = grad_q.astype(BF)
        for slot in range(5):
            rows = slice(PREFIX_ROWS + 128 * slot, PREFIX_ROWS + 128 * (slot + 1))
            if slot == 0:
                own[:, lanes(p * 128 + 1024)] = grad_k[rows].astype(BF)
                own[:, lanes(p * 128 + 2048)] = grad_v[rows].astype(BF)
            else:
                sent = slice(128 * (slot - 1), 128 * slot)
                dkv[sent, lanes(p * 128)] = grad_k[rows].astype(BF)
                dkv[sent, lanes(p * 128 + 1024)] = grad_v[rows].astype(BF)

    @pl.when(step == 1)
    def _():
        weights.wait()
        part = mm_nt(dkv[...], w_kv[...]).astype(BF)
        side0[...] = part[:128]
        near[...] = part[128:256]
        side1[...] = part[256:384]
        far[...] = part[384:]


def attend_back_call(batch, mixed, prefix_low, probs, grad_att, att, w_nat):
    return pl.pallas_call(
        attend_back_kernel,
        grid=(2,),
        in_specs=[
            pl.BlockSpec((4, 1, 128, 128), lambda i: (i, 0, batch, 0)),
            pl.BlockSpec((4, 5, 128, 128), lambda i: (2 + i, 0, batch, 0)),
            pl.BlockSpec((4, 5, 128, 128), lambda i: (4 + i, 0, batch, 0)),
            pl.BlockSpec((4, PREFIX_ROWS, 128), lambda i: (i, 0, 0)),
            pl.BlockSpec((4, PREFIX_ROWS, 128), lambda i: (2 + i, 0, 0)),
            pl.BlockSpec((1, 4, KEYS, 256), lambda i: (batch, i, 0, 0)),
            pl.BlockSpec((128, 512), lambda i: (batch, i)),
            pl.BlockSpec((128, 512), lambda i: (batch, i)),
            ANYWHERE,
        ],
        out_specs=[
            whole((128, 1024)),
            whole((128, 1024)),
            whole((128, 1024)),
            whole((128, 1024)),
            whole((128, 3072)),
        ],
        out_shape=[
            jax.ShapeDtypeStruct((128, 1024), BF),
            jax.ShapeDtypeStruct((128, 1024), BF),
            jax.ShapeDtypeStruct((128, 1024), BF),
            jax.ShapeDtypeStruct((128, 1024), BF),
            jax.ShapeDtypeStruct((128, 3072), BF),
        ],
        scratch_shapes=[VMEM((512, 2048), BF), VMEM((1024, 2048), BF), pltpu.SemaphoreType.DMA],
        compiler_params=call_params(48),
        cost_estimate=lasting(1),
        name="attend_back",
    )(mixed, mixed, mixed, prefix_low, prefix_low, probs, grad_att, att, w_nat)


def own_back_kernel(own0, own1, own2, w_nat, result, owns):
    @pl.when(pl.program_id(0) == 0)
    def _():
        for batch, own in enumerate((own0, own1, own2)):
            owns[128 * batch : 128 * (batch + 1), :] = own[...]

    result[...] = mm_nt(owns[...], w_nat[...])


def own_back_call(owns, w_nat):
    tokens = 128 * len(owns)
    return pl.pallas_call(
        own_back_kernel,
        grid=(4,),
        in_specs=[whole((128, 3072))] * 3 + [pl.BlockSpec((256, 3072), lambda i: (i, 0))],
        out_specs=pl.BlockSpec((tokens, 256), lambda i: (0, i)),
        out_shape=jax.ShapeDtypeStruct((tokens, 1024), F32),
        scratch_shapes=[VMEM((tokens, 3072), BF)],
        compiler_params=call_params(52),
        cost_estimate=lasting(1),
        name="own_back",
    )(*owns, w_nat)


def first_back_kernel(me, x, grad_own, grad_mid, gain, *refs):
    in_grad = refs[-1]
    first = jnp.where(me[0] % 2 == 0, 1.0, 0.0)
    for batch in range(len(refs) // 2):
        landed, other = refs[2 * batch], refs[2 * batch + 1]
        rows = slice(128 * batch, 128 * (batch + 1))
        incoming = grad_own[rows, :] + landed[...].astype(F32) + first * other[...].astype(F32)
        back = norm_back(x[rows, :].astype(F32), incoming, gain[...].astype(F32))
        in_grad[rows, :] = (grad_mid[rows, :] + back).astype(BF)


def first_back_call(seq_me, x, grad_own, grad_mid, gain, parts):
    def spec(part):
        if part.ndim == 2:
            return whole((128, 1024))
        return pl.BlockSpec((None, 128, 1024), lambda i: (1, 0, 0))

    return pl.pallas_call(
        first_back_kernel,
        grid=(1,),
        in_specs=[SCALARS] + [whole(x.shape)] * 3 + [whole((1, 1024))] + [spec(p) for p in parts],
        out_specs=whole(x.shape),
        out_shape=jax.ShapeDtypeStruct(x.shape, BF),
        compiler_params=call_params(48),
        cost_estimate=lasting(1),
        name="first_back",
    )(seq_me, x, grad_own, grad_mid, gain, *parts)


def full(shard):
    rows = lax.all_gather(shard, "row", axis=0, tiled=True)
    return lax.all_gather(rows, "seq", axis=1, tiled=True)


def pieces(matrix):
    rows, cols = matrix.shape
    return (
        matrix.reshape(4, rows // 4, 8, cols // 8)
        .transpose(0, 2, 1, 3)
        .reshape(32, rows // 4, cols // 8)
    )


def side_by_side(fc_weight, proj_weight, out_weight):
    quarter = proj_weight.shape[-2] // 4
    proj = [proj_weight[..., quarter * j : quarter * (j + 1), :] for j in range(4)]
    return jnp.concatenate([fc_weight, *proj, out_weight], axis=-1)


def gathered_plainly(sent, x_side, qkv_weight, out_weight, fc_weight, proj_weight):
    second = side_by_side(*[pieces(full(w)) for w in (fc_weight, proj_weight, out_weight)])
    h1 = moved(sent, "seq", 2)
    h2 = moved(h1, "seq", 2)
    o1 = swapped(h1, *X)
    r2 = swapped(jnp.where(x_side == 0, sent, h2), *X)
    return (h1, h2, o1, r2), [(pieces(full(qkv_weight)), NATURAL)], second


def gathered_by_swaps(sent, x_side, qkv_weight, out_weight, fc_weight, proj_weight):
    second = lax.all_gather(
        packed_call(fc_weight, proj_weight, out_weight), ("row", "seq"), axis=0
    )
    first = qkv_weight[None]
    v0 = cat(first, swapped(first, *ZF))
    g0 = swapped(v0, *ZN)
    h1 = moved(after(sent, v0), "seq", 2)
    v = cat(v0, g0)
    vx, vy = swapped(v, *X), swapped(v, *Y)
    h2 = moved(after(h1, g0), "seq", 2)
    vd = swapped(after(vx, vy), *Y)
    o1 = swapped(after(h1, vx, vy), *X)
    r2 = swapped(after(jnp.where(x_side == 0, sent, h2), o1), *X)
    zs = (0, 2, 1, 3)
    unit0 = with_cores([(v, zs, 0, 0), (vx, zs, 1, 0), (vy, zs, 0, 1), (vd, zs, 1, 1)])
    return (h1, h2, o1, r2), unit0, second


def local(
    activations,
    cotangent,
    segment_ids,
    prefix_embed,
    adapt_in,
    adapt_in_bias,
    adapt_out,
    adapt_out_bias,
    ln1_gain,
    ln1_bias,
    qkv_weight,
    qkv_bias,
    out_weight,
    out_bias,
    ln2_gain,
    ln2_bias,
    fc_weight,
    fc_bias,
    proj_weight,
    proj_bias,
):
    batches, rows_dev, tok_dev, width = activations.shape
    tokens = batches * rows_dev * tok_dev
    assert tok_dev == 128 and rows_dev == 1 and lax.axis_size("seq") % 2 == 0
    row_me, seq_me = lax.axis_index("row"), lax.axis_index("seq")
    x_side = seq_me % 2

    def flat(vector):
        return vector.reshape(1, -1)

    x = activations.reshape(tokens, width)
    cot = cotangent.reshape(tokens, width)

    ids = (segment_ids.reshape(1, tokens) + 1).astype(BF)
    ids = jnp.pad(ids, ((0, 7), (0, width - tokens)))
    sent = first_norm_call(x, ids, flat(ln1_gain), flat(ln1_bias))

    if (lax.axis_size("row"), lax.axis_size("seq")) == (4, 8):
        (h1, h2, o1, r2), unit0, second = gathered_by_swaps(
            sent, x_side, qkv_weight, out_weight, fc_weight, proj_weight
        )
        me = jnp.stack([row_me, seq_me]).astype(jnp.int32)
    else:
        (h1, h2, o1, r2), unit0, second = gathered_plainly(
            sent, x_side, qkv_weight, out_weight, fc_weight, proj_weight
        )
        me = jnp.zeros((2,), jnp.int32)
    second = second.reshape(4, 8, 256, 1152)

    seg = jnp.stack([part[tokens, :tokens] for part in (sent, o1, h1, r2, h2)])
    seg = seg.astype(F32).reshape(5, batches, tok_dev).transpose(1, 0, 2)

    squashed, prefix_low = prefix_call(
        prefix_embed, adapt_in, flat(adapt_in_bias), adapt_out, flat(adapt_out_bias)
    )
    mixed, w_nat = qkv_call(me, (sent, o1, h1, r2, h2), unit0, flat(qkv_bias), tokens)
    att, probs = attend_call(seg, mixed, prefix_low, batches, tokens)
    hidden, middle, grad_mid, grad_att, pre_kv = mlp_call(
        prefix_embed.shape[0],
        att,
        x,
        cot,
        flat(ln2_gain),
        flat(ln2_bias),
        flat(out_bias),
        flat(fc_bias),
        prefix_low,
        second,
        mixed,
        probs,
    )

    if (lax.axis_size("row"), lax.axis_size("seq")) == (4, 8):
        total_kv = lax.all_gather(pre_kv, ("row", "seq"), axis=0)
    else:
        total_kv = lax.psum(pre_kv, ("row", "seq"))[None]

    def back(batch, incoming):
        return attend_back_call(batch, mixed, prefix_low, probs, incoming, att, w_nat)

    def to_far(far, other):
        return (far.astype(F32) + jnp.where(x_side == 1, other, 0).astype(F32)).astype(BF)

    def to_near(near, other, passing):
        return (near.astype(F32) + other.astype(F32) + passing.astype(F32)).astype(BF)

    sides0, sides1, near0, far0, own0 = back(0, grad_att)
    other01 = swapped(sides1, *X)
    other00 = swapped(sides0, *X)
    sides2, sides3, near1, far1, own1 = back(1, after(grad_att, own0))
    other11 = swapped(sides3, *X)
    other10 = swapped(sides2, *X)
    to_far0 = to_far(far0, other01)
    passing0 = moved(to_far0, "seq", -2)
    sides4, sides5, near2, far2, own2 = back(2, after(grad_att, own1, to_far0, other00))
    other21 = swapped(sides5, *X)
    other20 = swapped(sides4, *X)
    to_far1 = to_far(after(far1, own2), other11)
    passing1 = moved(to_far1, "seq", -2)
    to_near0 = to_near(near0, other00, passing0)
    landed0 = moved(to_near0, "seq", -2)
    grad_own = own_back_call((after(own0, to_near0, to_far1), own1, own2), w_nat)
    to_far2 = to_far(after(far2, grad_own), other21)
    passing2 = moved(to_far2, "seq", -2)
    to_near1 = to_near(near1, other10, passing1)
    landed1 = moved(to_near1, "seq", -2)
    output = output_call(
        after(hidden, grad_own, to_near1, to_far2), middle, flat(proj_bias), second
    )
    landed2 = moved(after(to_near(near2, other20, passing2), output), "seq", -2)
    prefix_grad, adapt_in_grad, in_bias_grad, adapt_out_grad, out_bias_grad = prefix_back_call(
        after(total_kv, output, passing2), squashed, prefix_embed, adapt_in, adapt_out
    )
    parts = (landed0, other01, landed1, other11, landed2, other21)
    in_grad = first_back_call(
        seq_me.reshape(1), after(x, prefix_grad), grad_own, grad_mid, flat(ln1_gain), parts
    )
    shape = activations.shape
    return (
        output.reshape(shape),
        in_grad.reshape(shape),
        prefix_grad,
        adapt_in_grad,
        in_bias_grad.reshape(-1),
        adapt_out_grad,
        out_bias_grad.reshape(-1),
    )


def solution(mesh):
    rows = P(None, "row", "seq", None)
    split = P("row", "seq")
    placed = (
        rows,
        rows,
        P(None, "row", "seq"),
        P(),
        P(),
        P(),
        P(),
        P(),
        P(),
        P(),
        split,
        P(),
        split,
        P(),
        P(),
        P(),
        split,
        P(),
        split,
        P(),
    )
    return jax.shard_map(
        local,
        mesh=mesh,
        in_specs=placed,
        out_specs=(rows, rows, P(), P(), P(), P(), P()),
        check_vma=False,
    )
```

```python
import functools

import jax
import jax.numpy as jnp
from jax import lax
from jax.experimental import pallas as pl
from jax.experimental.pallas import tpu as pltpu
from jax.sharding import PartitionSpec as P

EPS = 1e-05
MASKED = -1e30
PREFIX_ROWS = 16
BF = jnp.bfloat16
F32 = jnp.float32
MIB = 1 << 20
HIGHEST = lax.Precision.HIGHEST
VMEM = pltpu.VMEM
ANYWHERE = pl.BlockSpec(memory_space=pl.ANY)
SCALARS = pl.BlockSpec(memory_space=pltpu.SMEM)


def mm(left, right, precision=None):
    return jnp.dot(left, right, precision=precision, preferred_element_type=F32)


def mm_nt(left, right, precision=None):
    return lax.dot_general(
        left, right, (((1,), (1,)), ((), ())), precision=precision, preferred_element_type=F32
    )


def mm_tn(left, right, precision=None):
    return lax.dot_general(
        left, right, (((0,), (0,)), ((), ())), precision=precision, preferred_element_type=F32
    )


def cat(*parts):
    return jnp.concatenate(parts, axis=0)


X, ZN, ZF, CORE, Y = ("seq", 1), ("seq", 2), ("seq", 4), ("row", 1), ("row", 2)


def swapped(value, axis, bit):
    count = lax.axis_size(axis)
    return lax.ppermute(value, axis, [(i, i ^ bit) for i in range(count)])


def moved(value, axis, steps):
    count = lax.axis_size(axis)
    low, high = max(0, -steps), min(count, count - steps)
    return lax.ppermute(value, axis, [(i, i + steps) for i in range(low, high)])


def after(value, *others):
    return lax.optimization_barrier((value,) + others)[0]


NATURAL = tuple((r, s) for r in range(4) for s in range(8))


def with_cores(parts):
    out = []
    for array, zs, x, y in parts:
        out.append((array, tuple((2 * y, 2 * z + x) for z in zs)))
        out.append((swapped(array, *CORE), tuple((2 * y + 1, 2 * z + x) for z in zs)))
    return out


def norm_parts(values):
    centre = values - jnp.mean(values, axis=-1, keepdims=True)
    spread = jnp.mean(centre * centre, axis=-1, keepdims=True)
    scale = lax.rsqrt(spread + EPS)
    return centre * scale, scale


def norm_back(values, incoming, gain):
    normal, scale = norm_parts(values)
    e = incoming * gain
    return scale * (
        e
        - jnp.mean(e, axis=-1, keepdims=True)
        - normal * jnp.mean(e * normal, axis=-1, keepdims=True)
    )


def call_params(limit):
    return pltpu.CompilerParams(vmem_limit_bytes=limit * MIB)


def lasting(micros):
    return pl.CostEstimate(
        flops=int(micros * 1e9), bytes_accessed=int(micros * 1e6), transcendentals=0
    )


def whole(shape):
    return pl.BlockSpec(shape, lambda *_: (0,) * len(shape))


def lanes(start, size=128):
    if isinstance(start, int):
        return pl.ds(start, size)
    return pl.ds(pl.multiple_of(start, 128), size)


def each_piece(me, arrays, spots):
    for array, slots in zip(arrays, spots):
        for slot, (row_bits, seq_bits) in enumerate(slots):
            yield array, slot, me[0] ^ row_bits, me[1] ^ seq_bits


def first_norm_kernel(x, ids, gain, shift, sent):
    tokens = x.shape[0]
    normal, _ = norm_parts(x[...].astype(F32))
    sent[:tokens, :] = (normal * gain[...].astype(F32) + shift[...].astype(F32)).astype(BF)
    sent[tokens:, :] = ids[...]


def first_norm_call(x, ids, gain, shift):
    tokens, width = x.shape
    return pl.pallas_call(
        first_norm_kernel,
        out_shape=jax.ShapeDtypeStruct((tokens + 8, width), BF),
        compiler_params=call_params(16),
        cost_estimate=lasting(1),
        name="first_norm",
    )(x, ids, gain, shift)


def packed_kernel(fc_weight, proj_weight, out_weight, packed):
    packed[:, :512] = fc_weight[...]
    for j in range(4):
        packed[:, 512 + 128 * j : 640 + 128 * j] = proj_weight[256 * j : 256 * (j + 1), :]
    packed[:, 1024:] = out_weight[...]


def packed_call(fc_weight, proj_weight, out_weight):
    return pl.pallas_call(
        packed_kernel,
        out_shape=jax.ShapeDtypeStruct((256, 1152), BF),
        compiler_params=call_params(56),
        cost_estimate=lasting(1),
        name="packed",
    )(fc_weight, proj_weight, out_weight)


def prefix_kernel(embed, w_in, b_in, w_out, b_out, squashed, low):
    inner = jnp.tanh(mm(embed[...], w_in[...], HIGHEST) + b_in[...])
    squashed[...] = inner
    pairs = mm(inner, w_out[...], HIGHEST) + b_out[...]
    pairs = cat(pairs, jnp.zeros((PREFIX_ROWS - pairs.shape[0], pairs.shape[1]), F32)).astype(BF)
    for p in range(low.shape[0]):
        low[p] = pairs[:, 128 * p : 128 * (p + 1)]


def prefix_call(embed, w_in, b_in, w_out, b_out):
    return pl.pallas_call(
        prefix_kernel,
        out_shape=[
            jax.ShapeDtypeStruct((embed.shape[0], w_in.shape[1]), F32),
            jax.ShapeDtypeStruct((w_out.shape[1] // 128, PREFIX_ROWS, 128), BF),
        ],
        compiler_params=call_params(24),
        cost_estimate=lasting(1),
        name="prefix",
    )(embed, w_in, b_in, w_out, b_out)


def prefix_back_kernel(
    total,
    squashed,
    embed,
    w_in_far,
    w_out_far,
    prefix_grad,
    in_grad_far,
    in_bias,
    out_grad_far,
    out_bias,
    w_in,
    w_out,
    in_grad,
    out_grad,
    sems,
):
    count = embed.shape[0]
    w_out_copy = pltpu.make_async_copy(w_out_far, w_out, sems.at[0])
    w_in_copy = pltpu.make_async_copy(w_in_far, w_in, sems.at[1])
    w_out_copy.start()
    w_in_copy.start()
    summed = jnp.sum(total[...], axis=0)
    grad_kv = jnp.concatenate([summed[count * p : count * (p + 1)] for p in range(16)], axis=1)
    inner = squashed[...]
    out_bias[...] = jnp.sum(grad_kv, axis=0, keepdims=True)
    low_kv = grad_kv.astype(BF)
    out_grad[...] = mm_tn(inner.astype(BF), low_kv)
    out_copy = pltpu.make_async_copy(out_grad, out_grad_far, sems.at[2])
    out_copy.start()
    w_out_copy.wait()
    grad_z = mm_nt(w_out[...].astype(BF), low_kv).T * (1.0 - inner * inner)
    in_bias[...] = jnp.sum(grad_z, axis=0, keepdims=True)
    low_z = grad_z.astype(BF)
    in_grad[...] = mm_tn(embed[...].astype(BF), low_z)
    in_copy = pltpu.make_async_copy(in_grad, in_grad_far, sems.at[3])
    in_copy.start()
    w_in_copy.wait()
    prefix_grad[...] = mm_nt(w_in[...].astype(BF), low_z).T
    out_copy.wait()
    in_copy.wait()


def prefix_back_call(total, squashed, embed, w_in, w_out):
    count, width = embed.shape
    hidden = w_in.shape[1]
    return pl.pallas_call(
        prefix_back_kernel,
        grid=(1,),
        in_specs=[
            whole(total.shape),
            whole(squashed.shape),
            whole(embed.shape),
            ANYWHERE,
            ANYWHERE,
        ],
        out_specs=[
            whole((count, width)),
            ANYWHERE,
            whole((1, hidden)),
            ANYWHERE,
            whole((1, 2 * width)),
        ],
        out_shape=[
            jax.ShapeDtypeStruct((count, width), F32),
            jax.ShapeDtypeStruct((width, hidden), F32),
            jax.ShapeDtypeStruct((1, hidden), F32),
            jax.ShapeDtypeStruct((hidden, 2 * width), F32),
            jax.ShapeDtypeStruct((1, 2 * width), F32),
        ],
        scratch_shapes=[
            VMEM((width, hidden), F32),
            VMEM((hidden, 2 * width), F32),
            VMEM((width, hidden), F32),
            VMEM((hidden, 2 * width), F32),
            pltpu.SemaphoreType.DMA((4,)),
        ],
        compiler_params=call_params(56),
        cost_estimate=lasting(1),
        name="prefix_back",
    )(total, squashed, embed, w_in, w_out)


def packed_kernel(fc_weight, proj_weight, out_weight, packed):
    packed[:, :512] = fc_weight[...]
    for j in range(4):
        packed[:, 512 + 128 * j : 640 + 128 * j] = proj_weight[256 * j : 256 * (j + 1), :]
    packed[:, 1024:] = out_weight[...]


def packed_call(fc_weight, proj_weight, out_weight):
    return pl.pallas_call(
        packed_kernel,
        out_shape=jax.ShapeDtypeStruct((256, 1152), BF),
        compiler_params=call_params(56),
        cost_estimate=lasting(1),
        name="packed",
    )(fc_weight, proj_weight, out_weight)


def prefix_kernel(embed, w_in, b_in, w_out, b_out, squashed, low):
    inner = jnp.tanh(mm(embed[...], w_in[...], HIGHEST) + b_in[...])
    squashed[...] = inner
    pairs = mm(inner, w_out[...], HIGHEST) + b_out[...]
    pairs = cat(pairs, jnp.zeros((PREFIX_ROWS - pairs.shape[0], pairs.shape[1]), F32)).astype(BF)
    for p in range(low.shape[0]):
        low[p] = pairs[:, 128 * p : 128 * (p + 1)]


def prefix_call(embed, w_in, b_in, w_out, b_out):
    return pl.pallas_call(
        prefix_kernel,
        out_shape=[
            jax.ShapeDtypeStruct((embed.shape[0], w_in.shape[1]), F32),
            jax.ShapeDtypeStruct((w_out.shape[1] // 128, PREFIX_ROWS, 128), BF),
        ],
        compiler_params=call_params(24),
        cost_estimate=lasting(1),
        name="prefix",
    )(embed, w_in, b_in, w_out, b_out)


def prefix_back_kernel(
    count, total, squashed, embed, w_in, w_out, prefix_grad, in_grad, in_bias, out_grad, out_bias
):
    summed = jnp.sum(total[...], axis=0)
    grad_kv = jnp.concatenate([summed[count * p : count * (p + 1)] for p in range(16)], axis=1)
    inner = squashed[...]
    out_bias[...] = jnp.sum(grad_kv, axis=0, keepdims=True)
    low_kv = grad_kv.astype(BF)
    out_grad[...] = mm_tn(inner.astype(BF), low_kv)
    grad_z = mm_nt(w_out[...].astype(BF), low_kv).T * (1.0 - inner * inner)
    in_bias[...] = jnp.sum(grad_z, axis=0, keepdims=True)
    low_z = grad_z.astype(BF)
    in_grad[...] = mm_tn(embed[...].astype(BF), low_z)
    prefix_grad[...] = mm_nt(w_in[...].astype(BF), low_z).T


def prefix_back_call(total, squashed, embed, w_in, w_out):
    count, width = embed.shape
    hidden = w_in.shape[1]
    return pl.pallas_call(
        functools.partial(prefix_back_kernel, count),
        out_shape=[
            jax.ShapeDtypeStruct((count, width), F32),
            jax.ShapeDtypeStruct((width, hidden), F32),
            jax.ShapeDtypeStruct((1, hidden), F32),
            jax.ShapeDtypeStruct((hidden, 2 * width), F32),
            jax.ShapeDtypeStruct((1, 2 * width), F32),
        ],
        compiler_params=call_params(56),
        cost_estimate=lasting(1),
        name="prefix_back",
    )(total, squashed, embed, w_in, w_out)


def qkv_kernel(spots, me, own, o1, h1, r2, h2, bias, *refs):
    arrays = refs[: len(spots)]
    mixed, natural, wide, sems = refs[len(spots) :]
    step = pl.program_id(0)
    tokens = mixed.shape[2]

    @pl.when(step == 0)
    def _():
        for array, slot, r, s in each_piece(me, arrays, spots):
            pltpu.make_async_copy(
                array.at[slot],
                wide.at[
                    s // 2,
                    pl.ds(pl.multiple_of(r * 256, 256), 256),
                    pl.ds(pl.multiple_of((s % 2) * 384, 128), 384),
                ],
                sems.at[s // 2],
            ).start()

    pltpu.make_async_copy(wide.at[step], wide.at[step], sems.at[step]).wait()
    natural[...] = wide[step]

    def one(slot, block):
        value = (mm(block, wide[step]) + bias[...].astype(F32)).astype(BF)
        for col in range(6):
            mixed[col, slot] = value[:, 128 * col : 128 * (col + 1)]

    one(0, own[:tokens, :])

    @pl.when(step >= 1)
    def _():
        for slot, ref in enumerate((o1, h1, r2, h2)):
            one(slot + 1, ref[:tokens, :])


def qkv_call(me, blocks, parts, bias, tokens):
    spots = tuple(part[1] for part in parts)
    return pl.pallas_call(
        functools.partial(qkv_kernel, spots),
        grid=(4,),
        in_specs=[SCALARS]
        + [whole(block.shape) for block in blocks]
        + [pl.BlockSpec((1, 768), lambda s: (0, s))]
        + [ANYWHERE] * len(spots),
        out_specs=[
            pl.BlockSpec((6, 5, tokens, 128), lambda s: (s, 0, 0, 0)),
            pl.BlockSpec((1024, 768), lambda s: (0, s)),
        ],
        out_shape=[
            jax.ShapeDtypeStruct((24, 5, tokens, 128), BF),
            jax.ShapeDtypeStruct((1024, 3072), BF),
        ],
        scratch_shapes=[VMEM((4, 1024, 768), BF), pltpu.SemaphoreType.DMA((4,))],
        compiler_params=call_params(40),
        cost_estimate=lasting(1),
        name="qkv",
    )(me, *blocks, bias, *[part[0] for part in parts])


def allowed_bias(seg, out):
    query = jnp.broadcast_to(seg[0:1, :], (128, 128))
    key_at = lax.broadcasted_iota(jnp.int32, (128, 128), 0)
    query_at = lax.broadcasted_iota(jnp.int32, (128, 128), 1)
    prefix_at = lax.broadcasted_iota(jnp.int32, (PREFIX_ROWS, 256), 0)
    out[0:PREFIX_ROWS, :] = jnp.where(prefix_at < 10, 0.0, MASKED)
    for slot in range(5):
        key = jnp.broadcast_to(seg[slot : slot + 1, :], (128, 128)).T
        allowed = key == query
        if slot == 0:
            allowed = allowed & (key_at <= query_at)
        value = jnp.where(allowed, 0.0, MASKED)
        rows = slice(PREFIX_ROWS + 128 * slot, PREFIX_ROWS + 128 * (slot + 1))
        out[rows, :128] = value
        out[rows, 128:] = value


def two_heads(block):
    lane = lax.broadcasted_iota(jnp.int32, block.shape, 1)
    zero = jnp.zeros_like(block)
    return cat(jnp.where(lane < 64, block, zero), jnp.where(lane < 64, zero, block))


def heads_merged(both):
    feature = lax.broadcasted_iota(jnp.int32, (128, 128), 0)
    return jnp.where(feature < 64, both[:, :128], both[:, 128:]).T


KEYS = PREFIX_ROWS + 5 * 128


def attend_kernel(seg, q, k, v, pk, pv, att, probs, bias):
    @pl.when(pl.program_id(1) == 0)
    def _():
        allowed_bias(seg[0], bias)

    for p in range(4):
        keys = cat(pk[p], *[k[p, slot] for slot in range(5)])
        values = cat(pv[p], *[v[p, slot] for slot in range(5)])
        scores = mm_nt(keys, two_heads(q[p, 0] * 0.125)) + bias[...]
        top = jnp.max(scores, axis=0, keepdims=True)
        expo = jnp.exp(scores - top)
        total = jnp.sum(expo, axis=0, keepdims=True)
        chance = (expo * (1.0 / total)).astype(BF)
        probs[0, p] = chance
        att[:, lanes(p * 128)] = heads_merged(mm_tn(values, chance)).astype(BF)


def attend_call(seg, mixed, prefix_low, batches, tokens):
    return pl.pallas_call(
        attend_kernel,
        grid=(batches, 2),
        in_specs=[
            pl.BlockSpec((1, 5, 128), lambda b, i: (b, 0, 0)),
            pl.BlockSpec((4, 1, 128, 128), lambda b, i: (i, 0, b, 0)),
            pl.BlockSpec((4, 5, 128, 128), lambda b, i: (2 + i, 0, b, 0)),
            pl.BlockSpec((4, 5, 128, 128), lambda b, i: (4 + i, 0, b, 0)),
            pl.BlockSpec((4, PREFIX_ROWS, 128), lambda b, i: (i, 0, 0)),
            pl.BlockSpec((4, PREFIX_ROWS, 128), lambda b, i: (2 + i, 0, 0)),
        ],
        out_specs=[
            pl.BlockSpec((128, 512), lambda b, i: (b, i)),
            pl.BlockSpec((1, 4, KEYS, 256), lambda b, i: (b, i, 0, 0)),
        ],
        out_shape=[
            jax.ShapeDtypeStruct((tokens, 1024), BF),
            jax.ShapeDtypeStruct((batches, 8, KEYS, 256), BF),
        ],
        scratch_shapes=[VMEM((KEYS, 256), F32)],
        compiler_params=call_params(48),
        cost_estimate=lasting(1),
        name="attend",
    )(seg, mixed, mixed, mixed, prefix_low, prefix_low)


def fc_copy(second, fc, sems, s):
    return pltpu.make_async_copy(second.at[:, s, :, pl.ds(0, 512)], fc.at[s], sems.at[s])


def proj_copy(second, proj, sems, r):
    return pltpu.make_async_copy(second.at[r, :, :, pl.ds(512, 512)], proj.at[r], sems.at[r])


def proj_rows(proj, r, j):
    return jnp.concatenate([proj[r, s, :, 128 * j : 128 * (j + 1)] for s in range(8)], axis=1)


def out_matrix(out):
    return jnp.concatenate([out[:, s].reshape(1024, 128) for s in range(8)], axis=1)


def row_deltas(grad_att, att):
    width = grad_att.shape[1]
    rows = max(8, width // 64)
    head = lax.broadcasted_iota(jnp.int32, (rows, width), 0)
    lane = lax.broadcasted_iota(jnp.int32, (rows, width), 1)
    pick = jnp.where(lane // 64 == head, 1.0, 0.0).astype(BF)
    product = grad_att.astype(F32) * att.astype(F32)
    high = product.astype(BF)
    return mm_nt(pick, high) + mm_nt(pick, (product - high.astype(F32)).astype(BF))


def both_heads(delta, p):
    return jnp.concatenate([delta[2 * p : 2 * p + 1, :], delta[2 * p + 1 : 2 * p + 2, :]], axis=1)


def prefix_part(q, pv, probs, grad_att, att, grad_pre_kv):
    batches, count = probs.shape[0], grad_pre_kv.shape[0] // 16
    delta = row_deltas(grad_att[...], att[...])
    key = lax.broadcasted_iota(jnp.int32, (2 * PREFIX_ROWS, 128), 0)
    lane = lax.broadcasted_iota(jnp.int32, (2 * PREFIX_ROWS, 128), 1)
    mine = (lane < 64) == (key < PREFIX_ROWS)
    for p in range(8):
        cols = slice(128 * p, 128 * (p + 1))
        grad_o = grad_att[:, cols]
        values = jnp.where(mine, cat(pv[p], pv[p]), jnp.zeros((), BF))
        grad_probs = mm_nt(values, grad_o)
        head = lax.broadcasted_iota(jnp.int32, grad_probs.shape, 0) < PREFIX_ROWS
        row_delta = jnp.where(head, delta[2 * p : 2 * p + 1, :], delta[2 * p + 1 : 2 * p + 2, :])
        chance = jnp.concatenate(
            [cat(probs[b, p, :, :128], probs[b, p, :, 128:]) for b in range(batches)], axis=1
        )
        grad_scores = (chance.astype(F32) * (grad_probs - row_delta)).astype(BF)
        grad_k = jnp.where(mine, mm(grad_scores, q[p] * 0.125), 0.0)
        grad_v = jnp.where(mine, mm(chance, grad_o), 0.0)
        grad_pre_kv[count * p : count * (p + 1), :] = (
            grad_k[:PREFIX_ROWS] + grad_k[PREFIX_ROWS:]
        )[:count]
        grad_pre_kv[count * (p + 8) : count * (p + 9), :] = (
            grad_v[:PREFIX_ROWS] + grad_v[PREFIX_ROWS:]
        )[:count]


def mlp_kernel(
    att,
    x,
    cot,
    gain,
    shift,
    out_bias,
    fc_bias,
    pv,
    second,
    mixed,
    probs,
    hidden_far,
    middle_far,
    grad_mid,
    grad_att,
    grad_pre_kv,
    q,
    chances,
    middle,
    hidden,
    slope,
    proj,
    fc,
    out,
    normed,
    total,
    fc_sems,
    proj_sems,
    sems,
):
    out_in = pltpu.make_async_copy(second.at[:, :, :, pl.ds(1024, 128)], out, sems.at[0])
    out_in.start()
    q_in = pltpu.make_async_copy(mixed.at[pl.ds(0, 8), 0], q, sems.at[2])
    q_in.start()
    chance_in = pltpu.make_async_copy(
        probs.at[:, :, pl.ds(0, PREFIX_ROWS), :], chances, sems.at[3]
    )
    chance_in.start()
    for s in range(3):
        fc_copy(second, fc, fc_sems, s).start()
    out_in.wait()
    value = x[...].astype(F32) + mm(att[...], out_matrix(out)) + out_bias[...].astype(F32)
    middle[...] = value
    middle_out = pltpu.make_async_copy(middle, middle_far, sems.at[4])
    middle_out.start()
    normal, _ = norm_parts(value)
    normed[...] = (normal * gain[...].astype(F32) + shift[...].astype(F32)).astype(BF)
    def gelu(v, rows, cols):
        cubic = (0.7978845608028654 * 0.044715) * (v * v)
        t = jnp.tanh(v * (cubic + 0.7978845608028654))
        half = 0.5 * t + 0.5
        hidden[rows, cols] = (v * half).astype(BF)
        slope[rows, cols] = (
            half + v * (half - half * half) * (6.0 * cubic + 2 * 0.7978845608028654)
        ).astype(BF)

    last = None
    for s in range(8):
        fc_copy(second, fc, fc_sems, s).wait()
        if s < 5:
            fc_copy(second, fc, fc_sems, s + 3).start()
        else:
            proj_copy(second, proj, proj_sems, s - 5).start()
        for n in range(2):
            for m in range(normed.shape[0] // 128):
                cols = pl.ds(512 * s + 256 * n, 256)
                rows = pl.ds(128 * m, 128)
                w = fc[s, :, :, 256 * n : 256 * (n + 1)].reshape(1024, 256)
                v = mm(normed[rows, :], w) + fc_bias[:, cols].astype(F32)
                if last is not None:
                    gelu(*last)
                last = (v, rows, cols)
    gelu(*last)
    proj_copy(second, proj, proj_sems, 3).start()
    kept = pltpu.make_async_copy(hidden, hidden_far, sems.at[1])
    kept.start()
    for r in range(4):
        proj_copy(second, proj, proj_sems, r).wait()
        for half_row in range(2):
            s = 2 * r + half_row
            grad_pre = []
            for j in (2 * half_row, 2 * half_row + 1):
                back = mm_nt(cot[...], proj_rows(proj, r, j))
                cols = pl.ds(1024 * r + 256 * j, 256)
                grad_pre.append((back * slope[:, cols].astype(F32)).astype(BF))
            part = mm_nt(jnp.concatenate(grad_pre, axis=1), fc[s].reshape(1024, 512))
            if s == 0:
                total[...] = part
            else:
                total[...] += part
    value = cot[...].astype(F32) + norm_back(middle[...], total[...], gain[...].astype(F32))
    grad_mid[...] = value
    grad_att[...] = mm_nt(value.astype(BF), out_matrix(out)).astype(BF)
    kept.wait()
    middle_out.wait()
    q_in.wait()
    chance_in.wait()
    prefix_part(q, pv, chances, grad_att, att, grad_pre_kv)


def mlp_call(count, att, x, cot, gain, shift, out_bias, fc_bias, prefix_low, second, mixed, probs):
    tokens, batches = cot.shape[0], probs.shape[0]
    return pl.pallas_call(
        mlp_kernel,
        grid=(1,),
        in_specs=[whole((tokens, 1024))] * 3
        + [whole((1, 1024))] * 3
        + [whole((1, 4096)), pl.BlockSpec((8, PREFIX_ROWS, 128), lambda i: (1, 0, 0))]
        + [ANYWHERE] * 3,
        out_specs=[ANYWHERE] * 2 + [whole((tokens, 1024))] * 2 + [whole((16 * count, 128))],
        out_shape=[
            jax.ShapeDtypeStruct((tokens, 4096), BF),
            jax.ShapeDtypeStruct((tokens, 1024), F32),
            jax.ShapeDtypeStruct((tokens, 1024), F32),
            jax.ShapeDtypeStruct((tokens, 1024), BF),
            jax.ShapeDtypeStruct((16 * count, 128), F32),
        ],
        scratch_shapes=[
            VMEM((8, tokens, 128), BF),
            VMEM((batches, 8, PREFIX_ROWS, 256), BF),
            VMEM((tokens, 1024), F32),
            VMEM((tokens, 4096), BF),
            VMEM((tokens, 4096), BF),
            VMEM((4, 8, 256, 512), BF),
            VMEM((8, 4, 256, 512), BF),
            VMEM((4, 8, 256, 128), BF),
            VMEM((tokens, 1024), BF),
            VMEM((tokens, 1024), F32),
            pltpu.SemaphoreType.DMA((8,)),
            pltpu.SemaphoreType.DMA((4,)),
            pltpu.SemaphoreType.DMA((5,)),
        ],
        compiler_params=call_params(52),
        cost_estimate=lasting(1),
        name="mlp",
    )(att, x, cot, gain, shift, out_bias, fc_bias, prefix_low, second, mixed, probs)


def output_kernel(hidden, middle, proj_bias, second, output, proj, total, sems):
    for r in range(4):
        proj_copy(second, proj, sems, r).start()
    total[...] = middle[...] + proj_bias[...].astype(F32)
    for r in range(4):
        proj_copy(second, proj, sems, r).wait()
        rows = jnp.concatenate([proj_rows(proj, r, j) for j in range(4)], axis=0)
        total[...] += mm(hidden[:, pl.ds(1024 * r, 1024)], rows)
    output[...] = total[...].astype(BF)


def output_call(hidden, middle, proj_bias, second):
    tokens = hidden.shape[0]
    return pl.pallas_call(
        output_kernel,
        grid=(1,),
        in_specs=[whole((tokens, 4096)), whole((tokens, 1024)), whole((1, 1024)), ANYWHERE],
        out_specs=whole((tokens, 1024)),
        out_shape=jax.ShapeDtypeStruct((tokens, 1024), BF),
        scratch_shapes=[
            VMEM((4, 8, 256, 512), BF),
            VMEM((tokens, 1024), F32),
            pltpu.SemaphoreType.DMA((4,)),
        ],
        compiler_params=call_params(52),
        cost_estimate=lasting(1),
        name="output",
    )(hidden, middle, proj_bias, second)


def attend_back_kernel(
    q, k, v, pk, pv, probs, grad_att, att, w_nat, side0, side1, near, far, own, dkv, w_kv, sem
):
    step = pl.program_id(0)
    weights = pltpu.make_async_copy(w_nat.at[:, pl.ds(1024, 2048)], w_kv, sem)

    @pl.when(step == 0)
    def _():
        weights.start()

    delta = row_deltas(grad_att[...], att[...])
    for i in range(4):
        p = step * 4 + i
        keys = cat(pk[i], *[k[i, slot] for slot in range(5)])
        values = cat(pv[i], *[v[i, slot] for slot in range(5)])
        queries = two_heads(q[i, 0] * 0.125)
        grad_two = two_heads(grad_att[:, 128 * i : 128 * (i + 1)])
        row_delta = both_heads(delta, i)
        chance = probs[0, i]
        grad_probs = mm_nt(values, grad_two)
        grad_scores = (chance.astype(F32) * (grad_probs - row_delta)).astype(BF)
        grad_k = mm(grad_scores, queries)
        grad_v = mm(chance, grad_two)
        grad_q = heads_merged(mm_tn(keys, grad_scores)) * 0.125
        own[:, lanes(p * 128)] = grad_q.astype(BF)
        for slot in range(5):
            rows = slice(PREFIX_ROWS + 128 * slot, PREFIX_ROWS + 128 * (slot + 1))
            if slot == 0:
                own[:, lanes(p * 128 + 1024)] = grad_k[rows].astype(BF)
                own[:, lanes(p * 128 + 2048)] = grad_v[rows].astype(BF)
            else:
                sent = slice(128 * (slot - 1), 128 * slot)
                dkv[sent, lanes(p * 128)] = grad_k[rows].astype(BF)
                dkv[sent, lanes(p * 128 + 1024)] = grad_v[rows].astype(BF)

    @pl.when(step == 1)
    def _():
        weights.wait()
        part = mm_nt(dkv[...], w_kv[...]).astype(BF)
        side0[...] = part[:128]
        near[...] = part[128:256]
        side1[...] = part[256:384]
        far[...] = part[384:]


def attend_back_call(batch, mixed, prefix_low, probs, grad_att, att, w_nat):
    return pl.pallas_call(
        attend_back_kernel,
        grid=(2,),
        in_specs=[
            pl.BlockSpec((4, 1, 128, 128), lambda i: (i, 0, batch, 0)),
            pl.BlockSpec((4, 5, 128, 128), lambda i: (2 + i, 0, batch, 0)),
            pl.BlockSpec((4, 5, 128, 128), lambda i: (4 + i, 0, batch, 0)),
            pl.BlockSpec((4, PREFIX_ROWS, 128), lambda i: (i, 0, 0)),
            pl.BlockSpec((4, PREFIX_ROWS, 128), lambda i: (2 + i, 0, 0)),
            pl.BlockSpec((1, 4, KEYS, 256), lambda i: (batch, i, 0, 0)),
            pl.BlockSpec((128, 512), lambda i: (batch, i)),
            pl.BlockSpec((128, 512), lambda i: (batch, i)),
            ANYWHERE,
        ],
        out_specs=[
            whole((128, 1024)),
            whole((128, 1024)),
            whole((128, 1024)),
            whole((128, 1024)),
            whole((128, 3072)),
        ],
        out_shape=[
            jax.ShapeDtypeStruct((128, 1024), BF),
            jax.ShapeDtypeStruct((128, 1024), BF),
            jax.ShapeDtypeStruct((128, 1024), BF),
            jax.ShapeDtypeStruct((128, 1024), BF),
            jax.ShapeDtypeStruct((128, 3072), BF),
        ],
        scratch_shapes=[VMEM((512, 2048), BF), VMEM((1024, 2048), BF), pltpu.SemaphoreType.DMA],
        compiler_params=call_params(48),
        cost_estimate=lasting(1),
        name="attend_back",
    )(mixed, mixed, mixed, prefix_low, prefix_low, probs, grad_att, att, w_nat)


def own_back_kernel(own0, own1, own2, w_nat, result, owns):
    @pl.when(pl.program_id(0) == 0)
    def _():
        for batch, own in enumerate((own0, own1, own2)):
            owns[128 * batch : 128 * (batch + 1), :] = own[...]

    result[...] = mm_nt(owns[...], w_nat[...])


def own_back_call(owns, w_nat):
    tokens = 128 * len(owns)
    return pl.pallas_call(
        own_back_kernel,
        grid=(4,),
        in_specs=[whole((128, 3072))] * 3 + [pl.BlockSpec((256, 3072), lambda i: (i, 0))],
        out_specs=pl.BlockSpec((tokens, 256), lambda i: (0, i)),
        out_shape=jax.ShapeDtypeStruct((tokens, 1024), F32),
        scratch_shapes=[VMEM((tokens, 3072), BF)],
        compiler_params=call_params(52),
        cost_estimate=lasting(1),
        name="own_back",
    )(*owns, w_nat)


def first_back_kernel(me, x, grad_own, grad_mid, gain, *refs):
    in_grad = refs[-1]
    first = jnp.where(me[0] % 2 == 0, 1.0, 0.0)
    for batch in range(len(refs) // 2):
        landed, other = refs[2 * batch], refs[2 * batch + 1]
        rows = slice(128 * batch, 128 * (batch + 1))
        incoming = grad_own[rows, :] + landed[...].astype(F32) + first * other[...].astype(F32)
        back = norm_back(x[rows, :].astype(F32), incoming, gain[...].astype(F32))
        in_grad[rows, :] = (grad_mid[rows, :] + back).astype(BF)


def first_back_call(seq_me, x, grad_own, grad_mid, gain, parts):
    def spec(part):
        if part.ndim == 2:
            return whole((128, 1024))
        return pl.BlockSpec((None, 128, 1024), lambda i: (1, 0, 0))

    return pl.pallas_call(
        first_back_kernel,
        grid=(1,),
        in_specs=[SCALARS] + [whole(x.shape)] * 3 + [whole((1, 1024))] + [spec(p) for p in parts],
        out_specs=whole(x.shape),
        out_shape=jax.ShapeDtypeStruct(x.shape, BF),
        compiler_params=call_params(48),
        cost_estimate=lasting(1),
        name="first_back",
    )(seq_me, x, grad_own, grad_mid, gain, *parts)


def full(shard):
    rows = lax.all_gather(shard, "row", axis=0, tiled=True)
    return lax.all_gather(rows, "seq", axis=1, tiled=True)


def pieces(matrix):
    rows, cols = matrix.shape
    return (
        matrix.reshape(4, rows // 4, 8, cols // 8)
        .transpose(0, 2, 1, 3)
        .reshape(32, rows // 4, cols // 8)
    )


def side_by_side(fc_weight, proj_weight, out_weight):
    quarter = proj_weight.shape[-2] // 4
    proj = [proj_weight[..., quarter * j : quarter * (j + 1), :] for j in range(4)]
    return jnp.concatenate([fc_weight, *proj, out_weight], axis=-1)


def gathered_plainly(sent, x_side, qkv_weight, out_weight, fc_weight, proj_weight):
    second = side_by_side(*[pieces(full(w)) for w in (fc_weight, proj_weight, out_weight)])
    h1 = moved(sent, "seq", 2)
    h2 = moved(h1, "seq", 2)
    o1 = swapped(h1, *X)
    r2 = swapped(jnp.where(x_side == 0, sent, h2), *X)
    return (h1, h2, o1, r2), [(pieces(full(qkv_weight)), NATURAL)], second


def gathered_by_swaps(sent, x_side, qkv_weight, out_weight, fc_weight, proj_weight):
    second = lax.all_gather(
        packed_call(fc_weight, proj_weight, out_weight), ("row", "seq"), axis=0
    )
    first = qkv_weight[None]
    v0 = cat(first, swapped(first, *ZF))
    g0 = swapped(v0, *ZN)
    h1 = moved(after(sent, v0), "seq", 2)
    v = cat(v0, g0)
    vx, vy = swapped(v, *X), swapped(v, *Y)
    h2 = moved(after(h1, g0), "seq", 2)
    vd = swapped(after(vx, vy), *Y)
    o1 = swapped(after(h1, vx, vy), *X)
    r2 = swapped(after(jnp.where(x_side == 0, sent, h2), o1), *X)
    zs = (0, 2, 1, 3)
    unit0 = with_cores([(v, zs, 0, 0), (vx, zs, 1, 0), (vy, zs, 0, 1), (vd, zs, 1, 1)])
    return (h1, h2, o1, r2), unit0, second


def local(
    activations,
    cotangent,
    segment_ids,
    prefix_embed,
    adapt_in,
    adapt_in_bias,
    adapt_out,
    adapt_out_bias,
    ln1_gain,
    ln1_bias,
    qkv_weight,
    qkv_bias,
    out_weight,
    out_bias,
    ln2_gain,
    ln2_bias,
    fc_weight,
    fc_bias,
    proj_weight,
    proj_bias,
):
    batches, rows_dev, tok_dev, width = activations.shape
    tokens = batches * rows_dev * tok_dev
    assert tok_dev == 128 and rows_dev == 1 and lax.axis_size("seq") % 2 == 0
    row_me, seq_me = lax.axis_index("row"), lax.axis_index("seq")
    x_side = seq_me % 2

    def flat(vector):
        return vector.reshape(1, -1)

    x = activations.reshape(tokens, width)
    cot = cotangent.reshape(tokens, width)

    ids = (segment_ids.reshape(1, tokens) + 1).astype(BF)
    ids = jnp.pad(ids, ((0, 7), (0, width - tokens)))
    sent = first_norm_call(x, ids, flat(ln1_gain), flat(ln1_bias))

    if (lax.axis_size("row"), lax.axis_size("seq")) == (4, 8):
        (h1, h2, o1, r2), unit0, second = gathered_by_swaps(
            sent, x_side, qkv_weight, out_weight, fc_weight, proj_weight
        )
        me = jnp.stack([row_me, seq_me]).astype(jnp.int32)
    else:
        (h1, h2, o1, r2), unit0, second = gathered_plainly(
            sent, x_side, qkv_weight, out_weight, fc_weight, proj_weight
        )
        me = jnp.zeros((2,), jnp.int32)
    second = second.reshape(4, 8, 256, 1152)

    seg = jnp.stack([part[tokens, :tokens] for part in (sent, o1, h1, r2, h2)])
    seg = seg.astype(F32).reshape(5, batches, tok_dev).transpose(1, 0, 2)

    squashed, prefix_low = prefix_call(
        prefix_embed, adapt_in, flat(adapt_in_bias), adapt_out, flat(adapt_out_bias)
    )
    mixed, w_nat = qkv_call(me, (sent, o1, h1, r2, h2), unit0, flat(qkv_bias), tokens)
    att, probs = attend_call(seg, mixed, prefix_low, batches, tokens)
    hidden, middle, grad_mid, grad_att, pre_kv = mlp_call(
        prefix_embed.shape[0],
        att,
        x,
        cot,
        flat(ln2_gain),
        flat(ln2_bias),
        flat(out_bias),
        flat(fc_bias),
        prefix_low,
        second,
        mixed,
        probs,
    )

    if (lax.axis_size("row"), lax.axis_size("seq")) == (4, 8):
        total_kv = lax.all_gather(pre_kv, ("row", "seq"), axis=0)
    else:
        total_kv = lax.psum(pre_kv, ("row", "seq"))[None]

    def back(batch, incoming):
        return attend_back_call(batch, mixed, prefix_low, probs, incoming, att, w_nat)

    def to_far(far, other):
        return (far.astype(F32) + jnp.where(x_side == 1, other, 0).astype(F32)).astype(BF)

    def to_near(near, other, passing):
        return (near.astype(F32) + other.astype(F32) + passing.astype(F32)).astype(BF)

    sides0, sides1, near0, far0, own0 = back(0, grad_att)
    other01 = swapped(sides1, *X)
    other00 = swapped(sides0, *X)
    sides2, sides3, near1, far1, own1 = back(1, after(grad_att, own0))
    other11 = swapped(sides3, *X)
    other10 = swapped(sides2, *X)
    to_far0 = to_far(far0, other01)
    passing0 = moved(to_far0, "seq", -2)
    sides4, sides5, near2, far2, own2 = back(2, after(grad_att, own1, to_far0, other00))
    other21 = swapped(sides5, *X)
    other20 = swapped(sides4, *X)
    to_far1 = to_far(after(far1, own2), other11)
    passing1 = moved(to_far1, "seq", -2)
    to_near0 = to_near(near0, other00, passing0)
    landed0 = moved(to_near0, "seq", -2)
    grad_own = own_back_call((after(own0, to_near0, to_far1), own1, own2), w_nat)
    to_far2 = to_far(after(far2, grad_own), other21)
    passing2 = moved(to_far2, "seq", -2)
    to_near1 = to_near(near1, other10, passing1)
    landed1 = moved(to_near1, "seq", -2)
    output = output_call(
        after(hidden, grad_own, to_near1, to_far2), middle, flat(proj_bias), second
    )
    landed2 = moved(after(to_near(near2, other20, passing2), output), "seq", -2)
    prefix_grad, adapt_in_grad, in_bias_grad, adapt_out_grad, out_bias_grad = prefix_back_call(
        after(total_kv, output, passing2), squashed, prefix_embed, adapt_in, adapt_out
    )
    parts = (landed0, other01, landed1, other11, landed2, other21)
    in_grad = first_back_call(
        seq_me.reshape(1), after(x, prefix_grad), grad_own, grad_mid, flat(ln1_gain), parts
    )
    shape = activations.shape
    return (
        output.reshape(shape),
        in_grad.reshape(shape),
        prefix_grad,
        adapt_in_grad,
        in_bias_grad.reshape(-1),
        adapt_out_grad,
        out_bias_grad.reshape(-1),
    )


def solution(mesh):
    rows = P(None, "row", "seq", None)
    split = P("row", "seq")
    placed = (
        rows,
        rows,
        P(None, "row", "seq"),
        P(),
        P(),
        P(),
        P(),
        P(),
        P(),
        P(),
        split,
        P(),
        split,
        P(),
        P(),
        P(),
        split,
        P(),
        split,
        P(),
    )
    return jax.shard_map(
        local,
        mesh=mesh,
        in_specs=placed,
        out_specs=(rows, rows, P(), P(), P(), P(), P()),
        check_vma=False,
    )
```
